32 devices in a mesh: section: 2 (over y), dp: 4 (over x, core), tensor: 4 (over z).
Axes of the slice: x: 2, y: 2, z: 4, core: 2. Of those that a mesh axis runs over, the one named last changes fastest.
Arguments:
- tokens: bfloat16 [8, 1024, 1024], P('dp', 'tensor'), may hold values from -6 to 6
- lengths: int32 [8], P('dp'), may hold values from 128 to 1024, as said below
- qkv_weight: bfloat16 [2, 3, 1024, 1024], P('section', None, None, 'tensor'), may hold values from -0.1875 to 0.1875
- out_weight: bfloat16 [2, 1024, 1024], P('section', 'tensor'), may hold values from -0.75 to 0.75
- gate_up_weight: bfloat16 [2, 2, 1024, 2816], P('section', None, None, 'tensor'), may hold values from -0.1875 to 0.1875
- down_weight: bfloat16 [2, 2816, 1024], P('section', 'tensor'), may hold values from -0.109375 to 0.109375
- norm_gains: float32 [2, 2, 1024], P('section'), may hold values from 0.5 to 1.5
- cotangent: bfloat16 [8, 1024, 1024], P('dp', 'tensor'), may hold values from -6 to 6
Outputs:
- layer_outs: bfloat16 [2, 8, 1024, 1024], P('section', 'dp', 'tensor')
- input_grads: float32 [2, 8, 1024, 1024], P('section', 'dp', 'tensor')
- qkv_grad: float32 [2, 3, 1024, 1024], P('section', None, 'dp', 'tensor')
- out_grad: float32 [2, 1024, 1024], P('section', 'tensor', 'dp')
- gate_up_grad: float32 [2, 2, 1024, 2816], P('section', None, 'dp', 'tensor')
- down_grad: float32 [2, 2816, 1024], P('section', 'tensor', 'dp')
- gain_grad: float32 [2, 2, 1024], P('section', None, ('dp', 'tensor'))
The draws below stay inside these ranges and needn't reach their ends.
Inputs may be any that keep to these rules, and one draw needn't show every extreme that they name: Positions from lengths[s] on are padding. Some sequence has all 1024 tokens.
All inputs are finite; a program needn't handle non-finite values.
Results may differ from the reference program's by a relative error of at most 0.03.
Values may be sent and summed in bfloat16 or wider, within the bound.
A program may use at most 256 MiB of HBM per device.

```python
import jax
import jax.numpy as jnp
from jax import lax

D = 1024
H = 16
HD = 64
FF = 2816
SEQ = 1024
NSEQ = 8


def draw_lengths(key, part):
    key = jax.random.fold_in(key, 11)
    key_one, key_two, key_three = jax.random.split(key, 3)
    first_pick = jax.random.randint(key_one, (NSEQ,), SEQ // 8, SEQ + 1)
    second_pick = jax.random.randint(key_two, (NSEQ,), SEQ // 8, SEQ + 1)
    shorter = jnp.minimum(first_pick, second_pick)
    longest_at = jax.random.randint(key_three, (), 0, NSEQ)
    return jnp.where(jnp.arange(NSEQ) == longest_at, SEQ, shorter).astype(jnp.int32)


def block_scale(stream_key, dims, cuts, smallest, largest):
    level, own = 1.0, jax.random.fold_in(stream_key, 6)
    for position, parts in cuts:
        steps = jnp.exp(jax.random.uniform(jax.random.fold_in(own, position), (parts,), jnp.float32, smallest / len(cuts), largest / len(cuts)))
        level = level * jnp.repeat(steps, dims[position] // parts).reshape([-1 if axis == position else 1 for axis in range(len(dims))])
    return level


def normal_values(key, shape, spread, bound, pieces=(), kind=jnp.bfloat16):
    loudness = block_scale(key, shape, pieces, -0.22, 0.18) if pieces else 1.0
    entries = jax.random.normal(key, shape, jnp.float32) * spread * loudness
    return jnp.minimum(jnp.maximum(entries, -bound), bound).astype(kind)


def setup_inputs(seed: int = 0) -> dict:
    keys = jax.random.split(jax.random.key(seed), 9)
    return {
        "tokens": normal_values(keys[0], (NSEQ, SEQ, D), 1.0, 6.0, ((0, 4), (1, 4))),
        "lengths": draw_lengths(jax.random.fold_in(keys[8], 71), 0),
        "qkv_weight": normal_values(keys[2], (2, 3, D, D), D ** -0.5, 0.1875, ((0, 2), (3, 4))),
        "out_weight": normal_values(keys[3], (2, D, D), (D // 16) ** -0.5, 0.75, ((0, 2), (1, 4))),
        "gate_up_weight": normal_values(keys[4], (2, 2, D, FF), D ** -0.5, 0.1875, ((0, 2), (3, 4))),
        "down_weight": normal_values(keys[5], (2, FF, D), FF ** -0.5, 0.109375, ((0, 2), (1, 4))),
        "norm_gains": jnp.clip(1.0 + 0.1 * jax.random.normal(keys[6], (2, 2, D), jnp.float32), 0.5, 1.5),
        "cotangent": normal_values(keys[7], (NSEQ, SEQ, D), 1.0, 6.0, ((0, 4), (1, 4))),
    }


NORM_EPS = 1e-06
ROPE_BASE = 10000.0
SCORE_SCALE = 0.125
MASK_VALUE = -1e+30

@jax.custom_vjp
def low(v):
    return lax.optimization_barrier(v.astype(jnp.bfloat16)).astype(jnp.float32)

@jax.custom_vjp
def low_back(v):
    return v

def low_keep(v):
    return (low(v), None)

def low_pass(kept, grad):
    return (grad,)

def back_keep(v):
    return (v, None)

def back_low(kept, grad):
    return (low(grad),)
low.defvjp(low_keep, low_pass)
low_back.defvjp(back_keep, back_low)

def rms_norm(values, gain):
    return values * lax.rsqrt(lax.optimization_barrier(jnp.mean(values * values, axis=-1, keepdims=True)) + NORM_EPS) * gain

def rope_tables(positions_count):
    positions = jnp.arange(positions_count, dtype=jnp.float32)
    frequency = ROPE_BASE ** (-jnp.arange(HD // 2, dtype=jnp.float32) * 2.0 / HD)
    angles = positions[:, None] * frequency[None, :]
    return (jnp.cos(angles), jnp.sin(angles))

def rotate(values, cos_table, sine_table):
    first_half = values[..., :HD // 2]
    second_half = values[..., HD // 2:]
    cos_part = cos_table[:, None, :]
    sin_part = sine_table[:, None, :]
    return jnp.concatenate([first_half * cos_part - second_half * sin_part, first_half * sin_part + second_half * cos_part], axis=-1)

def matmul(left, right):
    return jnp.dot(left, right, precision=lax.Precision.HIGHEST, preferred_element_type=jnp.float32)

def ref_layer(w_qkv, w_out, w_gate_up, w_down, gain_pair, layer_in, first_values, length):
    cos_table, sine_table = rope_tables(SEQ)
    normed = low(rms_norm(layer_in, gain_pair[0]))
    query_raw = low_back(matmul(normed, w_qkv[0]))
    key_raw = low_back(matmul(normed, w_qkv[1]))
    query_rot = low(rotate(query_raw.reshape(SEQ, H, HD), cos_table, sine_table))
    key_rot = low(rotate(key_raw.reshape(SEQ, H, HD), cos_table, sine_table))
    own_values = low_back(low(matmul(normed, w_qkv[2])))
    if first_values is None:
        used_values = own_values
    else:
        used_values = low(0.5 * own_values + 0.5 * first_values)
    raw_scores = jnp.einsum('qhd,khd->hqk', query_rot, key_rot, precision=lax.Precision.HIGHEST)
    raw_scores = low_back(raw_scores * SCORE_SCALE)
    row_index = jnp.arange(SEQ)[:, None]
    col_index = jnp.arange(SEQ)[None, :]
    is_valid = (col_index <= row_index) & (col_index < length)
    scores = jnp.where(is_valid[None], raw_scores, MASK_VALUE)
    row_top = lax.optimization_barrier(jnp.max(scores, axis=-1, keepdims=True))
    expd = jnp.exp(scores - row_top)
    row_total = lax.optimization_barrier(jnp.sum(expd, axis=-1, keepdims=True))
    attn_probs = low(expd / row_total)
    attended = jnp.einsum('hqk,khd->qhd', attn_probs, used_values.reshape(SEQ, H, HD), precision=lax.Precision.HIGHEST)
    attended = low(low_back(attended.reshape(SEQ, D)))
    hidden_res = layer_in + low_back(matmul(attended, w_out))
    mixed = low(rms_norm(hidden_res, gain_pair[1]))
    gate_val = low_back(matmul(mixed, w_gate_up[0]))
    up_val = low_back(matmul(mixed, w_gate_up[1]))
    activ = low(jax.nn.silu(gate_val) * up_val)
    result = hidden_res + low_back(matmul(activ, w_down))
    return (low(result), own_values)

def one_sequence(weights, row_in, row_probe, length):
    w_qkv, w_out, w_gate_up, w_down, gain_pair = weights
    first_out, first_values = ref_layer(w_qkv[0], w_out[0], w_gate_up[0], w_down[0], gain_pair[0], row_in, None, length)
    second_in = low_back(first_out) + row_probe
    second_out, unused_values = ref_layer(w_qkv[1], w_out[1], w_gate_up[1], w_down[1], gain_pair[1], second_in, low_back(first_values), length)
    return (first_out, second_out)

def reference(tokens, lengths, qkv_weight, out_weight, gate_up_weight, down_weight, norm_gains, cotangent):
    params = (qkv_weight.astype(jnp.float32), out_weight.astype(jnp.float32), gate_up_weight.astype(jnp.float32), down_weight.astype(jnp.float32), norm_gains.astype(jnp.float32))
    inputs = tokens.astype(jnp.float32)
    probe = jnp.zeros_like(inputs)
    checked = jax.checkpoint(one_sequence)

    def whole(weights, seq_inputs, seq_probe):
        return lax.map(lambda item: checked(weights, item[0], item[1], item[2]), (seq_inputs, seq_probe, lengths))
    (first_out, second_out), pull = jax.vjp(whole, params, inputs, probe)
    mask = (jnp.arange(SEQ)[None, :] < lengths[:, None]).astype(jnp.float32)
    grad_params, grad_inputs, grad_probe = pull((jnp.zeros_like(first_out), cotangent.astype(jnp.float32) * mask[..., None]))
    layer_outs = jnp.stack([first_out, second_out]).astype(jnp.bfloat16)
    input_grads = jnp.stack([grad_inputs, grad_probe])
    return (layer_outs, input_grads, grad_params[0], grad_params[1], grad_params[2], grad_params[3], grad_params[4])
```

```python
import jax
import jax.numpy as jnp
import numpy as np
from jax import lax
from jax.experimental import pallas as pl
from jax.experimental.pallas import tpu as pltpu
from jax.sharding import PartitionSpec as P

MESH = pl.DeviceIdType.MESH
ANY = pl.BlockSpec(memory_space=pl.ANY)


DEPTH = 2
CUTS = (2, 1, 4, 2)


def weight_pieces(part, _, out_rows, down_rows):
    pieces = []
    for w, total in enumerate((part, out_rows, part, down_rows)):
        cuts = CUTS[w]
        while total % (16 * cuts):
            cuts -= 1
        size = total // cuts
        pieces += [(w, i * size, size) for i in range(cuts)]
    return pieces


def gather_kernel(
    tok, cot, qkv, out, gu, down,
    seq, w_qkv, w_out, w_gu, w_down,
    loc, a2a_s, a2a_r, sib_s, sib_r, own_r, own_l, z_recv, z_fwd, x_s, x_r,
):
    mb, rows, _ = tok.shape
    n_t = lax.axis_size("tensor")
    nx = lax.axis_size("dp") // 2
    sec = lax.axis_index("section")
    dp = lax.axis_index("dp")
    z = lax.axis_index("tensor")
    x, c = dp // 2, lax.rem(dp, 2)
    dim = tok.shape[2]
    part = dim // nx
    head_cols = qkv.shape[3]
    out_rows = out.shape[1]
    here = z // mb == c
    jz = z - c * mb
    sibling = {"dp": 2 * x + 1 - c}

    barrier = pltpu.get_barrier_semaphore()
    for k in range(1, n_t):
        pl.semaphore_signal(
            barrier, inc=1, device_id={"tensor": lax.rem(z + k, n_t)}, device_id_type=MESH
        )
    for k in range(1, nx):
        pl.semaphore_signal(
            barrier, inc=1, device_id={"dp": 2 * lax.rem(x + k, nx) + c}, device_id_type=MESH
        )
    pl.semaphore_signal(barrier, inc=1, device_id=sibling, device_id_type=MESH)
    pl.semaphore_wait(barrier, n_t + nx - 1)

    pieces = weight_pieces(part, gu.shape[1], out_rows, down.shape[1])

    def shard_part(k, p):
        w, lo, size = pieces[k]
        col = pl.multiple_of(p * part, 128)
        row = pl.multiple_of(col + lo, 16)
        return (
            lambda: qkv.at[0, :, pl.ds(row, size), :],
            lambda: out.at[0, pl.ds(lo, size), pl.ds(col, part)],
            lambda: gu.at[0, :, pl.ds(row, size), :],
            lambda: down.at[0, pl.ds(lo, size), pl.ds(col, part)],
        )[w]()

    def slot_part(k, j, p):
        w, lo, size = pieces[k]
        col = pl.multiple_of(p * part, 128)
        row = pl.multiple_of(col + lo, 16)
        return (
            lambda: w_qkv.at[:, pl.ds(row, size), pl.ds(pl.multiple_of(j * head_cols, 128), head_cols)],
            lambda: w_out.at[pl.ds(pl.multiple_of(j * out_rows + lo, 16), size), pl.ds(col, part)],
            lambda: w_gu.at[j, :, pl.ds(row, size), :],
            lambda: w_down.at[j, pl.ds(lo, size), pl.ds(col, part)],
        )[w]()

    def remote(src, dst, send, recv, to):
        return pltpu.make_async_remote_copy(
            src_ref=src, dst_ref=dst, send_sem=send, recv_sem=recv,
            device_id=to, device_id_type=MESH,
        )

    right, left = {"tensor": z + 1}, {"tensor": z - 1}
    block = seq.at[pl.ds(pl.multiple_of(z * rows, 128), rows), :]

    for i in range(mb):
        zt = c * mb + i
        for which, source in ((0, tok), (1, cot)):
            @pl.when((zt != z) & (sec == which))
            def _(source=source, i=i, zt=zt):
                remote(source.at[i], block, a2a_s.at[i], a2a_r.at[z], {"tensor": zt}).start()

            @pl.when((zt == z) & (sec == which))
            def _(source=source, i=i):
                pltpu.make_async_copy(source.at[i], block, loc.at[1]).start()

    n_k = len(pieces)

    @pl.when(here)
    def _():
        for k in range(n_k):
            for p in range(nx):
                pltpu.make_async_copy(shard_part(k, p), slot_part(k, jz, p), loc.at[0]).start()

    def order(i):
        return jnp.where(c == 0, mb - 1 - i, i)

    for k in range(n_k):
        @pl.when(here)
        def _(k=k):
            @pl.when(z < n_t - 1)
            def _():
                if k >= DEPTH:
                    remote(shard_part(k - DEPTH, x), slot_part(k - DEPTH, jz, x), own_r.at[k - DEPTH], z_recv.at[k, jz], right).wait_send()
                remote(shard_part(k, x), slot_part(k, jz, x), own_r.at[k], z_recv.at[k, jz], right).start()

            @pl.when(z > 0)
            def _():
                if k >= DEPTH:
                    remote(shard_part(k - DEPTH, x), slot_part(k - DEPTH, jz, x), own_l.at[k - DEPTH], z_recv.at[k, jz], left).wait_send()
                remote(shard_part(k, x), slot_part(k, jz, x), own_l.at[k], z_recv.at[k, jz], left).start()

        for i in range(mb):
            j = order(i)
            s = c * mb + j
            piece = slot_part(k, j, x)

            @pl.when(s != z)
            def _(k=k, j=j, s=s, piece=piece):
                remote(piece, piece, z_fwd.at[k, j], z_recv.at[k, j], right).wait_recv()

                @pl.when((s < z) & (z < n_t - 1))
                def _():
                    remote(piece, piece, z_fwd.at[k, j], z_recv.at[k, j], right).start()

                @pl.when((s > z) & (z > 0))
                def _():
                    remote(piece, piece, z_fwd.at[k, j], z_recv.at[k, j], left).start()

                for d in range(1, nx):
                    remote(
                        piece, piece, x_s.at[k, j, d], x_r.at[k, j, x],
                        {"dp": 2 * lax.rem(x + d, nx) + c},
                    ).start()

        if k == min(2, n_k - 1):
            @pl.when(here)
            def _():
                for zs in range(n_t):
                    src = seq.at[pl.ds(zs * rows, rows), :]

                    @pl.when(zs != z)
                    def _(src=src, zs=zs):
                        remote(src, src, a2a_s.at[0], a2a_r.at[zs], right).wait_recv()

                pltpu.make_async_copy(block, block, loc.at[1]).wait()
                remote(seq, seq, sib_s, sib_r, sibling).start()

    for k in range(n_k):
        for j in range(mb):
            s = c * mb + j

            @pl.when(s != z)
            def _(k=k, j=j, s=s):
                for d in range(1, nx):
                    p = lax.rem(x + d, nx)
                    piece = slot_part(k, j, p)
                    remote(piece, piece, x_s.at[k, j, d], x_r.at[k, j, p], right).wait_recv()
                    own = slot_part(k, j, x)
                    remote(own, own, x_s.at[k, j, d], x_r.at[k, j, p], right).wait_send()

                @pl.when(((s < z) & (z < n_t - 1)) | ((s > z) & (z > 0)))
                def _():
                    own = slot_part(k, j, x)
                    remote(own, own, z_fwd.at[k, j], z_recv.at[k, j], right).wait_send()

    @pl.when(here)
    def _():
        for k in range(n_k):
            for p in range(nx):
                pltpu.make_async_copy(shard_part(k, p), slot_part(k, jz, p), loc.at[0]).wait()

        for k in range(max(0, n_k - DEPTH), n_k):
            @pl.when(z < n_t - 1)
            def _(k=k):
                remote(shard_part(k, x), slot_part(k, jz, x), own_r.at[k], z_recv.at[k, jz], right).wait_send()

            @pl.when(z > 0)
            def _(k=k):
                remote(shard_part(k, x), slot_part(k, jz, x), own_l.at[k], z_recv.at[k, jz], left).wait_send()

        remote(seq, seq, sib_s, sib_r, sibling).wait_send()

    @pl.when(jnp.logical_not(here))
    def _():
        remote(seq, seq, sib_s, sib_r, sibling).wait_recv()

    for i in range(mb):
        zt = c * mb + i

        @pl.when(zt != z)
        def _(i=i):
            remote(tok.at[i], block, a2a_s.at[i], a2a_r.at[z], right).wait_send()


def gather(tokens, cotangent, qkv, out, gu, down):
    mb, rows, dim = tokens.shape
    n_t = lax.axis_size("tensor")
    nx = lax.axis_size("dp") // 2
    dma = pltpu.SemaphoreType.DMA
    n_k = len(weight_pieces(dim // nx, gu.shape[1], out.shape[1], down.shape[1]))
    return pl.pallas_call(
        gather_kernel,
        out_shape=(
            jax.ShapeDtypeStruct((rows * n_t, dim), jnp.bfloat16),
            jax.ShapeDtypeStruct((3, dim, mb * qkv.shape[3]), jnp.bfloat16),
            jax.ShapeDtypeStruct((mb * out.shape[1], dim), jnp.bfloat16),
            jax.ShapeDtypeStruct((mb, 2, dim, gu.shape[3]), jnp.bfloat16),
            jax.ShapeDtypeStruct((mb, down.shape[1], dim), jnp.bfloat16),
        ),
        in_specs=[ANY] * 2 + [pl.BlockSpec(memory_space=pltpu.VMEM)] * 4,
        out_specs=(ANY,) * 5,
        scratch_shapes=[
            dma((2,)), dma((mb,)), dma((n_t,)), dma, dma,
            dma((n_k,)), dma((n_k,)), dma((n_k, mb)), dma((n_k, mb)),
            dma((n_k, mb, nx)), dma((n_k, mb, nx)),
        ],
        compiler_params=pltpu.CompilerParams(
            collective_id=0, has_side_effects=True, vmem_limit_bytes=16 << 20
        ),
        name="gather_weights",
    )(tokens, cotangent, qkv, out, gu, down)


RING_DEPTH = 3
OWN_LAG = 3


def scatter_kernel(
    g_qkv, g_out, g_gu, g_down, y, dx,
    o_qkv, o_out, o_gu, o_down, o_y, o_dx,
    xb_qkv, xb_out, xb_gu, xb_down,
    zb_qkv, zb_out, zb_gu, zb_down,
    fb_qkv, fb_out, fb_gu, fb_down,
    a2a_s, a2a_r, x_s, x_r, z_s, z_r, zo_r, f_s, f_r,
):
    mb = g_qkv.shape[0]
    n_t = lax.axis_size("tensor")
    nx = lax.axis_size("dp") // 2
    dp = lax.axis_index("dp")
    z = lax.axis_index("tensor")
    x, c = dp // 2, lax.rem(dp, 2)
    dim = g_qkv.shape[2]
    part = dim // nx
    quarter = part // 2
    rows = y.shape[0] // n_t
    here = z // mb == c
    jz = z - c * mb
    sibling = {"dp": 2 * x + 1 - c}
    right, left = {"tensor": z + 1}, {"tensor": z - 1}
    pieces = weight_pieces(part, g_gu.shape[1], g_out.shape[1], g_down.shape[1])
    n_k = len(pieces)

    barrier = pltpu.get_barrier_semaphore()
    for k in range(1, n_t):
        pl.semaphore_signal(
            barrier, inc=1, device_id={"tensor": lax.rem(z + k, n_t)}, device_id_type=MESH
        )
    for k in range(1, nx):
        pl.semaphore_signal(
            barrier, inc=1, device_id={"dp": 2 * lax.rem(x + k, nx) + c}, device_id_type=MESH
        )
    pl.semaphore_signal(barrier, inc=1, device_id=sibling, device_id_type=MESH)
    pl.semaphore_wait(barrier, n_t + nx - 1)

    def remote(src, dst, send, recv, to):
        return pltpu.make_async_remote_copy(
            src_ref=src, dst_ref=dst, send_sem=send, recv_sem=recv,
            device_id=to, device_id_type=MESH,
        )

    def grad_part(k, j, p):
        w, lo, size = pieces[k]
        col = pl.multiple_of(p * part, 128)
        row = pl.multiple_of(col + lo, 16)
        return (
            lambda: g_qkv.at[j, :, pl.ds(row, size), :],
            lambda: g_out.at[j, pl.ds(lo, size), pl.ds(col, part)],
            lambda: g_gu.at[j, :, pl.ds(row, size), :],
            lambda: g_down.at[j, pl.ds(lo, size), pl.ds(col, part)],
        )[w]()

    def buffer_part(bufs, k, j):
        w, lo, size = pieces[k]
        if w in (0, 2):
            return bufs[w].at[j, :, pl.ds(lo, size), :]
        return bufs[w].at[j, pl.ds(lo, size), :]

    def x_buf(k, j, d):
        return buffer_part([b.at[d - 1] for b in (xb_qkv, xb_out, xb_gu, xb_down)], k, j)

    def z_buf(k, j):
        return buffer_part((zb_qkv, zb_out, zb_gu, zb_down), k, j)

    @pl.when(here)
    def _():
        for t, (src, dst) in enumerate(((y, o_y), (dx, o_dx))):
            for d in range(1, n_t):
                zt = lax.rem(z + d, n_t)
                block = src.at[pl.ds(pl.multiple_of(zt * rows, 128), rows), :]
                remote(block, dst.at[jz], a2a_s.at[t, d], a2a_r.at[t, jz], {"tensor": zt}).start()

    def x_send(n):
        k, i = n // mb, n % mb
        j = jnp.where(c == 0, i, mb - 1 - i)
        for d in range(1, nx):
            to = lax.rem(x + d, nx)
            yield remote(
                grad_part(k, j, to), x_buf(k, j, d), x_s.at[k, j, d], x_r.at[k, j, d],
                {"dp": 2 * to + c},
            )

    total = n_k * mb
    for n in range(RING_DEPTH):
        for copy in x_send(n):
            copy.start()

    def final_part(k):
        w, lo, size = pieces[k]
        if w == 0:
            return o_qkv.at[:, pl.ds(lo % quarter, size), :], fb_qkv.at[:, pl.ds(lo % quarter, size), :]
        if w == 1:
            return o_out.at[pl.ds(lo, size), :], fb_out.at[pl.ds(lo, size), :]
        if w == 2:
            return o_gu.at[:, pl.ds(lo % quarter, size), :], fb_gu.at[:, pl.ds(lo % quarter, size), :]
        return o_down.at[pl.ds(lo, size), :], fb_down.at[pl.ds(lo, size), :]

    def own_piece(k):
        w, lo, size = pieces[k]
        total_sum = grad_part(k, jz, x)[...].astype(jnp.float32)
        for d in range(1, nx):
            total_sum = total_sum + x_buf(k, jz, d)[...].astype(jnp.float32)
        x_buf(k, jz, 1)[...] = total_sum.astype(jnp.bfloat16)

        @pl.when(z > 0)
        def _():
            piece = z_buf(k, jz)
            remote(piece, piece, z_s.at[k, jz], z_r.at[k, jz], right).wait_recv()
            x_buf(k, jz, 1)[...] = (
                x_buf(k, jz, 1)[...].astype(jnp.float32) + piece[...].astype(jnp.float32)
            ).astype(jnp.bfloat16)

        @pl.when(z < n_t - 1)
        def _():
            piece = z_buf(k, mb)
            remote(piece, piece, z_s.at[k, jz], zo_r.at[k], right).wait_recv()
            x_buf(k, jz, 1)[...] = (
                x_buf(k, jz, 1)[...].astype(jnp.float32) + piece[...].astype(jnp.float32)
            ).astype(jnp.bfloat16)

        summed = x_buf(k, jz, 1)
        out_ref, fin = final_part(k)
        if w in (0, 2):
            @pl.when(c == lo // quarter)
            def _():
                out_ref[...] = summed[...].astype(jnp.float32)

            @pl.when(c != lo // quarter)
            def _():
                remote(summed, fin, f_s.at[k], f_r.at[k], sibling).start()
        else:
            mine = pl.ds(pl.multiple_of(c * quarter, 128), quarter)
            theirs = pl.ds(pl.multiple_of((1 - c) * quarter, 128), quarter)
            out_ref[...] = summed[:, mine].astype(jnp.float32)
            remote(summed.at[:, theirs], fin, f_s.at[k], f_r.at[k], sibling).start()

    for k in range(n_k):
        for i in range(mb):
            n = k * mb + i
            j = jnp.where(c == 0, i, mb - 1 - i)
            s = c * mb + j
            if n + RING_DEPTH < total:
                for copy in x_send(n):
                    copy.wait_send()
                for copy in x_send(n + RING_DEPTH):
                    copy.start()
            for copy in x_send(n):
                copy.wait_recv()

            @pl.when(s != z)
            def _(k=k, j=j, s=s):
                total_sum = grad_part(k, j, x)[...].astype(jnp.float32)
                for d in range(1, nx):
                    total_sum = total_sum + x_buf(k, j, d)[...].astype(jnp.float32)
                x_buf(k, j, 1)[...] = total_sum.astype(jnp.bfloat16)

                @pl.when(((s > z) & (z > 0)) | ((s < z) & (z < n_t - 1)))
                def _():
                    piece = z_buf(k, j)
                    remote(piece, piece, z_s.at[k, j], z_r.at[k, j], right).wait_recv()
                    x_buf(k, j, 1)[...] = (
                        x_buf(k, j, 1)[...].astype(jnp.float32) + piece[...].astype(jnp.float32)
                    ).astype(jnp.bfloat16)

                @pl.when(s > z)
                def _():
                    remote(x_buf(k, j, 1), z_buf(k, j), z_s.at[k, j], z_r.at[k, j], right).start()

                @pl.when(s < z - 1)
                def _():
                    remote(x_buf(k, j, 1), z_buf(k, j), z_s.at[k, j], z_r.at[k, j], left).start()

                @pl.when(s == z - 1)
                def _():
                    remote(x_buf(k, j, 1), z_buf(k, mb), z_s.at[k, j], zo_r.at[k], left).start()

        if k >= OWN_LAG:
            @pl.when(here)
            def _(k=k):
                own_piece(k - OWN_LAG)

    @pl.when(here)
    def _():
        for k in range(max(0, n_k - OWN_LAG), n_k):
            own_piece(k)

    @pl.when(jnp.logical_not(here))
    def _():
        for k in range(n_k):
            w, lo, size = pieces[k]
            out_ref, fin = final_part(k)
            if w in (0, 2):
                @pl.when(c == lo // quarter)
                def _(k=k, out_ref=out_ref, fin=fin):
                    remote(fin, fin, f_s.at[k], f_r.at[k], sibling).wait_recv()
                    out_ref[...] = fin[...].astype(jnp.float32)
            else:
                remote(fin, fin, f_s.at[k], f_r.at[k], sibling).wait_recv()
                out_ref[...] = fin[...].astype(jnp.float32)

    for n in range(max(0, total - RING_DEPTH), total):
        for copy in x_send(n):
            copy.wait_send()

    for k in range(n_k):
        for j in range(mb):
            s = c * mb + j

            @pl.when(s != z)
            def _(k=k, j=j):
                piece = x_buf(k, j, 1)
                remote(piece, piece, z_s.at[k, j], z_r.at[k, j], right).wait_send()

    @pl.when(here)
    def _():
        for k in range(n_k):
            w, lo, size = pieces[k]
            fin = final_part(k)[1]
            if w in (0, 2):
                @pl.when(c != lo // quarter)
                def _(k=k, fin=fin):
                    remote(fin, fin, f_s.at[k], f_r.at[k], sibling).wait_send()
            else:
                remote(fin, fin, f_s.at[k], f_r.at[k], sibling).wait_send()

        for t, (src, dst) in enumerate(((y, o_y), (dx, o_dx))):
            for d in range(1, n_t):
                block = src.at[pl.ds(0, rows), :]
                remote(block, dst.at[0], a2a_s.at[t, d], a2a_r.at[t, jz], right).wait_send()
            dst[jz] = src[pl.ds(pl.multiple_of(z * rows, 128), rows), :]

    for t, dst in enumerate((o_y, o_dx)):
        for i in range(mb):
            @pl.when(c * mb + i != z)
            def _(t=t, i=i, dst=dst):
                remote(dst.at[i], dst.at[i], a2a_s.at[t, 0], a2a_r.at[t, i], right).wait_recv()


def scatter(g_qkv, g_out, g_gu, g_down, y, dx):
    mb, _, dim, cols = g_qkv.shape
    n_t = lax.axis_size("tensor")
    n_dp = lax.axis_size("dp")
    nx = n_dp // 2
    part, quarter = dim // nx, dim // n_dp
    out_rows, ff, down_rows = g_out.shape[1], g_gu.shape[3], g_down.shape[1]
    rows = y.shape[0] // n_t
    dma = pltpu.SemaphoreType.DMA
    n_k = len(weight_pieces(part, dim, out_rows, down_rows))
    bf, f32 = jnp.bfloat16, jnp.float32

    def shapes(lead, split):
        return (
            (*lead, 3, split, cols), (*lead, out_rows, split),
            (*lead, 2, split, ff), (*lead, down_rows, split),
        )

    vmem = pl.BlockSpec(memory_space=pltpu.VMEM)
    finals = shapes((), quarter)
    return pl.pallas_call(
        scatter_kernel,
        out_shape=(
            *(jax.ShapeDtypeStruct(shape, f32) for shape in finals),
            jax.ShapeDtypeStruct((mb, rows, dim), bf),
            jax.ShapeDtypeStruct((mb, rows, dim), bf),
        ),
        in_specs=[vmem] * 6,
        out_specs=(vmem,) * 6,
        scratch_shapes=[
            *(pltpu.VMEM(shape, bf) for shape in shapes((nx - 1, mb), part)),
            *(pltpu.VMEM(shape, bf) for shape in shapes((mb + 1,), part)),
            *(pltpu.VMEM(shape, bf) for shape in finals),
            dma((2, n_t)), dma((2, mb)), dma((n_k, mb, nx)), dma((n_k, mb, nx)),
            dma((n_k, mb)), dma((n_k, mb)), dma((n_k,)), dma((n_k,)), dma((n_k,)),
        ],
        compiler_params=pltpu.CompilerParams(
            collective_id=1, has_side_effects=True, vmem_limit_bytes=62 << 20
        ),
        name="scatter_grads",
    )(g_qkv, g_out, g_gu, g_down, y, dx)


NORM_EPS = 1e-6
ROPE_BASE = 10000.0
SCORE_SCALE = 0.125
MASK_VALUE = -1e30
HD = 64
PAIR = 2 * HD
BLOCK = 256
NT = (((1,), (1,)), ((), ()))


def rope_tables(positions):
    lane = np.arange(PAIR)
    frequency = ROPE_BASE ** (-(lane % (HD // 2)) * 2.0 / HD)
    angles = np.arange(positions)[:, None] * frequency[None, :]
    sign = np.where(lane % HD < HD // 2, -1.0, 1.0)
    return np.cos(angles).astype(np.float32), (np.sin(angles) * sign).astype(np.float32)


def rotate_pair(values, cos, sin):
    lane = lax.broadcasted_iota(jnp.int32, values.shape, 1)
    partner = jnp.where(
        lax.rem(lane, HD) < HD // 2,
        pltpu.roll(values, PAIR - HD // 2, 1),
        pltpu.roll(values, HD // 2, 1),
    )
    return values * cos + partner * sin


def qkv_kernel(share, x, first, gain, w, cos, sin, a_o, q_o, k_o, v_o, vu_o):
    xf = x[...].astype(jnp.float32)
    scale = lax.rsqrt(jnp.mean(xf * xf, axis=-1, keepdims=True) + NORM_EPS)
    a = (xf * scale * gain[...]).astype(jnp.bfloat16)
    a_o[...] = a
    q = jnp.dot(a, w[0], preferred_element_type=jnp.float32)
    k = jnp.dot(a, w[1], preferred_element_type=jnp.float32)
    for p in range(q.shape[1] // PAIR):
        cols = slice(p * PAIR, (p + 1) * PAIR)
        q_o[:, cols] = (rotate_pair(q[:, cols], cos[...], sin[...]) * SCORE_SCALE).astype(jnp.bfloat16)
        k_o[:, cols] = rotate_pair(k[:, cols], cos[...], sin[...]).astype(jnp.bfloat16)
    v = jnp.dot(a, w[2], preferred_element_type=jnp.float32).astype(jnp.bfloat16)
    v_o[...] = v
    vu_o[...] = (
        share[0] * v.astype(jnp.float32) + (1.0 - share[0]) * first[...].astype(jnp.float32)
    ).astype(jnp.bfloat16)


def project_qkv(x, first, gain, w, share, tables):
    seq, dim = x.shape
    width = w.shape[2]
    blk = min(BLOCK, seq)
    smem = pl.BlockSpec(memory_space=pltpu.SMEM)
    rows = lambda cols: pl.BlockSpec((blk, cols), lambda i: (i, 0))
    out = lambda cols: jax.ShapeDtypeStruct((seq, cols), jnp.bfloat16)
    return pl.pallas_call(
        qkv_kernel,
        grid=(seq // blk,),
        in_specs=[
            smem, rows(dim), rows(width),
            pl.BlockSpec((1, dim), lambda i: (0, 0)),
            pl.BlockSpec(w.shape, lambda i: (0, 0, 0)),
            rows(PAIR), rows(PAIR),
        ],
        out_specs=(rows(dim), rows(width), rows(width), rows(width), rows(width)),
        out_shape=(out(dim), out(width), out(width), out(width), out(width)),
        compiler_params=pltpu.CompilerParams(vmem_limit_bytes=32 << 20),
        cost_estimate=pl.CostEstimate(flops=6 * seq * dim * width, bytes_accessed=w.size * 2 + seq * dim * 8, transcendentals=0),
        name="project_qkv",
    )(share, x, first, gain[None], w, *tables)


def head_views(h, shape):
    lane = lax.broadcasted_iota(jnp.int32, shape, 1)
    return lane // HD == h, lane == (1 - h) * HD


def key_bias(length, shape):
    key = lax.broadcasted_iota(jnp.int32, shape, 0)
    return jnp.where(key < length, 0.0, MASK_VALUE)


def causal_block(blk):
    key = lax.broadcasted_iota(jnp.int32, (blk, blk), 0)
    query = lax.broadcasted_iota(jnp.int32, (blk, blk), 1)
    return key <= query


def attention_kernel(length, q, k, v, o, lse):
    seq = q.shape[0]
    blk = min(BLOCK, seq)
    f32, bf = jnp.float32, jnp.bfloat16
    v_t = v[...].astype(f32).T.astype(bf)
    keys = k[...].astype(f32)
    bias = key_bias(length[0], keys.shape)
    visible = causal_block(blk)
    queries = q[...].astype(f32)
    heads = []
    for h in range(2):
        inside, extra = head_views(h, keys.shape)
        heads.append((
            jnp.where(inside, keys, jnp.where(extra, bias, 0.0)).astype(bf),
            jnp.where(inside, queries, jnp.where(extra, 1.0, 0.0)).astype(bf),
            v_t[h * HD:(h + 1) * HD],
        ))
    for i in range(seq // blk):
        lo, hi = i * blk, (i + 1) * blk
        parts = []
        for h in range(2):
            kh, qh, vh = heads[h]
            qi = qh[lo:hi]
            s_diag = lax.dot_general(kh[lo:hi], qi, NT, preferred_element_type=f32)
            s_diag = jnp.where(visible, s_diag, MASK_VALUE)
            top = jnp.max(s_diag, axis=0, keepdims=True)
            if i:
                s_full = lax.dot_general(kh[:lo], qi, NT, preferred_element_type=f32)
                top = jnp.maximum(top, jnp.max(s_full, axis=0, keepdims=True))
            p_diag = jnp.exp(s_diag - top)
            total = jnp.sum(p_diag, axis=0, keepdims=True)
            acc = jnp.dot(vh[:, lo:hi], p_diag.astype(bf), preferred_element_type=f32)
            if i:
                p_full = jnp.exp(s_full - top)
                total = total + jnp.sum(p_full, axis=0, keepdims=True)
                acc = acc + jnp.dot(vh[:, :lo], p_full.astype(bf), preferred_element_type=f32)
            parts.append(acc / total)
            lse[0, h:h + 1, lo:hi] = top + jnp.log(total)
        o[lo:hi, :] = jnp.concatenate(parts, axis=0).T.astype(bf)


def attention(length, q, k, vu):
    seq, width = q.shape
    pairs = width // PAIR
    col = pl.BlockSpec((seq, PAIR), lambda p: (0, p))
    return pl.pallas_call(
        attention_kernel,
        grid=(pairs,),
        in_specs=[pl.BlockSpec(memory_space=pltpu.SMEM), col, col, col],
        out_specs=(col, pl.BlockSpec((1, 2, seq), lambda p: (p, 0, 0))),
        out_shape=(
            jax.ShapeDtypeStruct((seq, width), jnp.bfloat16),
            jax.ShapeDtypeStruct((pairs, 2, seq), jnp.float32),
        ),
        compiler_params=pltpu.CompilerParams(vmem_limit_bytes=48 << 20),
        cost_estimate=pl.CostEstimate(flops=8 * seq * seq * width, bytes_accessed=8 * seq * width, transcendentals=pairs * seq * seq),
        name="attention",
    )(length, q, k, vu)


def attention_back_kernel(length, share, q, k, v, o, do, lse, first, cos, sin, dq_o, dk_o, dv_o, dv1_o, dk_a, dv_a):
    seq = q.shape[0]
    blk = min(BLOCK, seq)
    f32, bf = jnp.float32, jnp.bfloat16
    keys = k[...].astype(f32)
    k_t = keys.T.astype(bf)
    bias = key_bias(length[0], keys.shape)
    visible = causal_block(blk)
    queries = q[...].astype(f32)
    grads = do[...].astype(f32)
    heads = []
    for h in range(2):
        inside, extra = head_views(h, keys.shape)
        heads.append((
            jnp.where(inside, keys, jnp.where(extra, bias, 0.0)).astype(bf),
            jnp.where(inside, queries, jnp.where(extra, 1.0, 0.0)).astype(bf),
            jnp.where(inside, queries, 0.0).astype(bf),
            jnp.where(inside, grads, 0.0).astype(bf),
            k_t[h * HD:(h + 1) * HD],
        ))
    vals = v[...]
    for i in range(seq // blk):
        lo, hi = i * blk, (i + 1) * blk
        product = (grads[lo:hi] * o[lo:hi, :].astype(f32)).T
        parts = []
        for h in range(2):
            kh, qh, qz, gh, kt = heads[h]
            delta = jnp.sum(product[h * HD:(h + 1) * HD], axis=0, keepdims=True)
            stat = lse[0, h:h + 1, lo:hi]

            def side(a, b, mask):
                s = lax.dot_general(kh[a:b], qh[lo:hi], NT, preferred_element_type=f32)
                p = jnp.exp(s - stat)
                if mask:
                    p = jnp.where(visible, p, 0.0)
                dp = lax.dot_general(vals[a:b], gh[lo:hi], NT, preferred_element_type=f32)
                ds = (p * (dp - delta)).astype(bf)
                dv = jnp.dot(p.astype(bf), gh[lo:hi], preferred_element_type=f32)
                dk = jnp.dot(ds, qz[lo:hi], preferred_element_type=f32)
                if mask and h == 0:
                    dv_a[a:b, :] = dv
                    dk_a[a:b, :] = dk
                else:
                    dv_a[a:b, :] += dv
                    dk_a[a:b, :] += dk
                return jnp.dot(kt[:, a:b], ds, preferred_element_type=f32)

            dq_t = side(lo, hi, True)
            if i:
                dq_t = dq_t + side(0, lo, False)
            parts.append(dq_t)
        dq = jnp.concatenate(parts, axis=0).T * SCORE_SCALE
        dq_o[lo:hi, :] = rotate_pair(dq, cos[lo:hi, :], -sin[lo:hi, :]).astype(bf)
    dk_o[...] = rotate_pair(dk_a[...], cos[...], -sin[...]).astype(bf)
    dv_o[...] = (share[0] * dv_a[...] + first[...].astype(f32)).astype(bf)
    dv1_o[...] = ((1.0 - share[0]) * dv_a[...]).astype(bf)


def attention_back(length, share, q, k, vu, o, do, lse, first, tables):
    seq, width = q.shape
    pairs = width // PAIR
    col = pl.BlockSpec((seq, PAIR), lambda p: (0, p))
    whole = pl.BlockSpec((seq, PAIR), lambda p: (0, 0))
    smem = pl.BlockSpec(memory_space=pltpu.SMEM)
    return pl.pallas_call(
        attention_back_kernel,
        grid=(pairs,),
        in_specs=[smem, smem, col, col, col, col, col, pl.BlockSpec((1, 2, seq), lambda p: (p, 0, 0)), col, whole, whole],
        out_specs=(col,) * 4,
        out_shape=(jax.ShapeDtypeStruct((seq, width), jnp.bfloat16),) * 4,
        scratch_shapes=[pltpu.VMEM((seq, PAIR), jnp.float32)] * 2,
        compiler_params=pltpu.CompilerParams(vmem_limit_bytes=48 << 20),
        cost_estimate=pl.CostEstimate(flops=20 * seq * seq * width, bytes_accessed=20 * seq * width, transcendentals=pairs * seq * seq),
        name="attention_back",
    )(length, share, q, k, vu, o, do, lse, first, *tables)


def rms_norm(values, gain):
    return values * lax.rsqrt(jnp.mean(values * values, axis=-1, keepdims=True) + NORM_EPS) * gain


def pair_sum(part):
    mine = part.astype(jnp.bfloat16)
    swap = [(d, d ^ 1) for d in range(lax.axis_size("dp"))]
    theirs = lax.ppermute(mine, "dp", swap)
    return mine.astype(jnp.float32) + theirs.astype(jnp.float32)


def to_section(values, step):
    return lax.ppermute(values, "section", [(0, 1)] if step > 0 else [(1, 0)])


def dot(a, b):
    return jnp.dot(a, b, preferred_element_type=jnp.float32)


def dot_nt(a, b):
    return lax.dot_general(a, b, NT, preferred_element_type=jnp.float32)


def dot_tn(a, b):
    return lax.dot_general(a, b, (((0,), (0,)), ((), ())), preferred_element_type=jnp.float32)


def forward_layer(weights, x, first, length, share, tables):
    w_qkv, w_out, w_gu, w_down, gains = weights
    a, q, k, v, vu = project_qkv(x, first, gains[0], w_qkv, share, tables)
    o, lse = attention(length, q, k, vu)
    h = x.astype(jnp.float32) + pair_sum(dot(o, w_out))
    b = rms_norm(h, gains[1]).astype(jnp.bfloat16)
    part = 0.0
    hidden = []
    for j in range(w_gu.shape[0]):
        gate, up = dot(b, w_gu[j, 0]), dot(b, w_gu[j, 1])
        m = (jax.nn.silu(gate) * up).astype(jnp.bfloat16)
        part = part + dot(m, w_down[j])
        hidden.append((gate, up, m))
    y = (h + pair_sum(part)).astype(jnp.bfloat16)
    return y, v, (a, q, k, vu, o, lse, h, b, hidden)


def backward_layer(weights, x, kept, length, share, tables, dy, first_grad):
    w_qkv, w_out, w_gu, w_down, gains = weights
    a, q, k, vu, o, lse, h, b, hidden = kept
    dmo = dy.astype(jnp.bfloat16)
    part = 0.0
    g_gu, g_down = [], []
    for j, (gate, up, m) in enumerate(hidden):
        dm = dot_nt(dmo, w_down[j])
        g_down.append(dot_tn(m, dmo).astype(jnp.bfloat16))
        sig = jax.nn.sigmoid(gate)
        d_gate = (dm * up * (sig * (1.0 + gate * (1.0 - sig)))).astype(jnp.bfloat16)
        d_up = (dm * gate * sig).astype(jnp.bfloat16)
        part = part + dot_nt(d_gate, w_gu[j, 0]) + dot_nt(d_up, w_gu[j, 1])
        g_gu.append(jnp.stack([dot_tn(b, d_gate), dot_tn(b, d_up)]).astype(jnp.bfloat16))
    db = pair_sum(part)
    _, norm_back = jax.vjp(rms_norm, h, gains[1])
    dh, dg2 = norm_back(db)
    dh = dy + dh
    dao = dh.astype(jnp.bfloat16)
    do = dot_nt(dao, w_out).astype(jnp.bfloat16)
    mb = w_gu.shape[0]
    cols = w_qkv.shape[2] // mb
    g_out = dot_tn(o, dao).astype(jnp.bfloat16).reshape(mb, -1, dao.shape[1])
    dq, dk, dv, dv1 = attention_back(length, share, q, k, vu, o, do, lse, first_grad, tables)
    grads = (dq, dk, dv)
    g_qkv = jnp.stack([
        jnp.stack([dot_tn(a, g[:, j * cols:(j + 1) * cols]) for g in grads]) for j in range(mb)
    ]).astype(jnp.bfloat16)
    da = pair_sum(sum(dot_nt(g, w_qkv[i]) for i, g in enumerate(grads)))
    _, norm_back = jax.vjp(rms_norm, x.astype(jnp.float32), gains[0])
    dx, dg1 = norm_back(da)
    return dh + dx, dv1, (g_qkv, g_out, jnp.stack(g_gu), jnp.stack(g_down), jnp.stack([dg1, dg2]))


def shards(tokens, lengths, qkv_weight, out_weight, gate_up_weight, down_weight, norm_gains, cotangent):
    is_first = lax.axis_index("section") == 0
    dp, z = lax.axis_index("dp"), lax.axis_index("tensor")
    mb, rows, dim = tokens.shape
    seq_len = rows * lax.axis_size("tensor")
    share = jnp.where(is_first, 1.0, 0.5).astype(jnp.float32)[None]
    all_lengths = lax.all_gather(lengths, "dp", axis=0, tiled=True)
    length = lax.dynamic_slice_in_dim(all_lengths, dp // 2 * 2 * mb + z, 1)
    tables = tuple(jnp.asarray(t) for t in rope_tables(seq_len))

    start, w_qkv, w_out, w_gu, w_down = gather(
        tokens, cotangent, qkv_weight, out_weight, gate_up_weight, down_weight
    )
    weights = (w_qkv, w_out, w_gu, w_down, norm_gains[0])
    first = jnp.zeros((seq_len, w_qkv.shape[2]), jnp.bfloat16)
    y, v, _ = forward_layer(weights, start, first, length, share, tables)
    x = jnp.where(is_first, start, to_section(y, 1))
    first = to_section(v, 1)
    y, _, kept = forward_layer(weights, x, first, length, share, tables)

    mask = jnp.arange(seq_len)[:, None] < length
    cot = jnp.where(mask, start.astype(jnp.float32), 0.0)
    dx, dv1, _ = backward_layer(
        weights, x, kept, length, share, tables, cot, jnp.zeros_like(first)
    )
    dy = jnp.where(is_first, to_section(dx.astype(jnp.bfloat16), -1).astype(jnp.float32), cot)
    first_grad = to_section(dv1, -1)
    dx, _, grads = backward_layer(weights, x, kept, length, share, tables, dy, first_grad)
    g_qkv, g_out, g_gu, g_down, g_gain = grads
    gain = lax.psum_scatter(
        jnp.where(lax.rem(dp, 2) == 0, g_gain, 0.0), ("dp", "tensor"), scatter_dimension=1, tiled=True
    )
    o_qkv, o_out, o_gu, o_down, o_y, o_dx = scatter(
        g_qkv, g_out, g_gu, g_down, y, dx.astype(jnp.bfloat16)
    )
    return (
        o_y[None], o_dx.astype(jnp.float32)[None], o_qkv[None], o_out[None], o_gu[None], o_down[None], gain[None],
    )


def solution(mesh):
    in_specs = (
        P("dp", "tensor", None),
        P("dp"),
        P("section", None, None, "tensor"),
        P("section", "tensor", None),
        P("section", None, None, "tensor"),
        P("section", "tensor", None),
        P("section", None, None),
        P("dp", "tensor", None),
    )
    out_specs = (
        P("section", "dp", "tensor", None),
        P("section", "dp", "tensor", None),
        P("section", None, "dp", "tensor"),
        P("section", "tensor", "dp"),
        P("section", None, "dp", "tensor"),
        P("section", "tensor", "dp"),
        P("section", None, ("dp", "tensor")),
    )
    return jax.shard_map(shards, mesh=mesh, in_specs=in_specs, out_specs=out_specs, check_vma=False)
```

```python
import jax
import jax.numpy as jnp
import numpy as np
from jax import lax
from jax.experimental import pallas as pl
from jax.experimental.pallas import tpu as pltpu
from jax.sharding import PartitionSpec as P

MESH = pl.DeviceIdType.MESH
ANY = pl.BlockSpec(memory_space=pl.ANY)
VMEM = pl.BlockSpec(memory_space=pltpu.VMEM)
NORM_EPS = 1e-6
ROPE_BASE = 10000.0
SCORE_SCALE = 0.125
MASK_VALUE = -1e30
HD = 64
PAIR = 2 * HD
CHUNKS = 4
NT = (((1,), (1,)), ((), ()))
BF, F32 = jnp.bfloat16, jnp.float32

QKV, OUT, GU, DOWN = range(4)
COUNT = (2, 1, 4, 2)
BASE = (0, 2, 3, 7)
N_PIECES = 9


def dot(a, b):
    return jnp.dot(a, b, preferred_element_type=F32)


def dot_nt(a, b):
    return lax.dot_general(a, b, NT, preferred_element_type=F32)


def dot_tn(a, b):
    return lax.dot_general(a, b, (((0,), (0,)), ((), ())), preferred_element_type=F32)


def remote(src, dst, send, recv, to):
    return pltpu.make_async_remote_copy(
        src_ref=src, dst_ref=dst, send_sem=send, recv_sem=recv, device_id=to, device_id_type=MESH
    )


class Place:
    def __init__(self, mb):
        self.n_t = lax.axis_size("tensor")
        self.nx = lax.axis_size("dp") // 2
        self.section = lax.axis_index("section")
        dp = lax.axis_index("dp")
        self.z = lax.axis_index("tensor")
        self.x, self.c = dp // 2, lax.rem(dp, 2)
        self.here = self.z // mb == self.c
        self.jz = self.z - self.c * mb
        self.sibling = {"dp": 2 * self.x + 1 - self.c}
        self.right, self.left = {"tensor": self.z + 1}, {"tensor": self.z - 1}

    def at_x(self, d):
        return {"dp": 2 * lax.rem(self.x + d, self.nx) + self.c}

    def meet(self):
        barrier = pltpu.get_barrier_semaphore()
        partners = [{"tensor": lax.rem(self.z + k, self.n_t)} for k in range(1, self.n_t)]
        partners += [self.at_x(k) for k in range(1, self.nx)]
        partners += [self.sibling, {"section": 1 - self.section}]
        for partner in partners:
            pl.semaphore_signal(barrier, inc=1, device_id=partner, device_id_type=MESH)
        pl.semaphore_wait(barrier, len(partners))


def rope_tables(positions):
    lane = np.arange(PAIR)
    frequency = ROPE_BASE ** (-(lane % (HD // 2)) * 2.0 / HD)
    angles = np.arange(positions)[:, None] * frequency[None, :]
    sign = np.where(lane % HD < HD // 2, -1.0, 1.0)
    return np.cos(angles).astype(np.float32), (np.sin(angles) * sign).astype(np.float32)


def rotate_pair(values, cos, sin):
    lane = lax.broadcasted_iota(jnp.int32, values.shape, 1)
    partner = jnp.where(
        lax.rem(lane, HD) < HD // 2,
        pltpu.roll(values, PAIR - HD // 2, 1),
        pltpu.roll(values, HD // 2, 1),
    )
    return values * cos + partner * sin


def normalise(values):
    return values * lax.rsqrt(jnp.mean(values * values, axis=-1, keepdims=True) + NORM_EPS)


def head_views(h, shape):
    lane = lax.broadcasted_iota(jnp.int32, shape, 1)
    return lane // HD == h, lane == (1 - h) * HD


def key_bias(length, shape):
    key = lax.broadcasted_iota(jnp.int32, shape, 0).astype(F32)
    return jnp.where(key < length, 0.0, MASK_VALUE)


def causal_block(blk):
    key = lax.broadcasted_iota(jnp.int32, (blk, blk), 0)
    query = lax.broadcasted_iota(jnp.int32, (blk, blk), 1)
    return key <= query


def attend(queries, keys, vals, length, put_out, put_lse):
    seq = queries.shape[0]
    blk = seq // CHUNKS
    v_t = vals.astype(F32).T.astype(BF)
    keys, queries = keys.astype(F32), queries.astype(F32)
    bias = key_bias(length, keys.shape)
    visible = causal_block(blk)
    heads = []
    for h in range(2):
        inside, extra = head_views(h, keys.shape)
        heads.append((
            jnp.where(inside, keys, jnp.where(extra, bias, 0.0)).astype(BF),
            jnp.where(inside, queries, jnp.where(extra, 1.0, 0.0)).astype(BF),
            v_t[h * HD:(h + 1) * HD],
        ))
    for i in range(CHUNKS):
        lo, hi = i * blk, (i + 1) * blk
        parts = []
        for h in range(2):
            kh, qh, vh = heads[h]
            qi = qh[lo:hi]
            s_diag = jnp.where(visible, dot_nt(kh[lo:hi], qi), MASK_VALUE)
            top = jnp.max(s_diag, axis=0, keepdims=True)
            if i:
                s_full = dot_nt(kh[:lo], qi)
                top = jnp.maximum(top, jnp.max(s_full, axis=0, keepdims=True))
            p_diag = jnp.exp(s_diag - top)
            total = jnp.sum(p_diag, axis=0, keepdims=True)
            acc = dot(vh[:, lo:hi], p_diag.astype(BF))
            if i:
                p_full = jnp.exp(s_full - top)
                total = total + jnp.sum(p_full, axis=0, keepdims=True)
                acc = acc + dot(vh[:, :lo], p_full.astype(BF))
            parts.append(acc / total)
            put_lse(h, lo, hi, top + jnp.log(total))
        put_out(lo, hi, jnp.concatenate(parts, axis=0).T.astype(BF))


def forward_kernel(
    tok, cot, lens, qkv, out, gu, down, gains, cos, sin,
    x_o, cot_o, y_o, wq_o, wo_o, wg_o, wd_o, a_o, q_o, k_o, vu_o, o_o, lse_o, h_o, b_o, g_o, u_o, m_o, len_o,
    w_qkv, w_out, w_gu, w_down, x_v, first, a_v, q_v, k_v, v_v, vu_v, o_v, lse_v, h_v, b_v, g_v, u_v, m_v,
    acc, s1, r1, r2, len_v,
    loc, a2a_s, a2a_r, sib, own_r, own_l, z_r, z_f, x_s, x_r, hop, hsib, e1, e2, vsem, lsem, outs,
):
    mb, block_rows, dim = tok.shape
    me = Place(mb)
    x, c, z, n_t, nx, jz = me.x, me.c, me.z, me.n_t, me.nx, me.jz
    part = dim // nx
    cols, ow, half = qkv.shape[3], out.shape[1], down.shape[1] // 2
    seq = x_v.shape[0]
    rows = seq // CHUNKS
    pairs = q_v.shape[0]
    first_plane, second_plane = me.section == 0, me.section == 1
    me.meet()

    def column(p):
        return pl.ds(pl.multiple_of(p * part, 128), part)

    def shard_part(w, n, p):
        if w == QKV:
            return qkv.at[0, :, pl.ds(pl.multiple_of(p * part + n * (part // 2), 16), part // 2), :]
        if w == OUT:
            return out.at[0, :, column(p)]
        if w == GU:
            return gu.at[0, n // 2, pl.ds(pl.multiple_of(lax.rem(n, 2) * half, 16), half), column(p)]
        return down.at[0, pl.ds(n * half, half), column(p)]

    def slot_part(w, n, j, p):
        if w == QKV:
            return w_qkv.at[j, :, pl.ds(pl.multiple_of(p * part + n * (part // 2), 16), part // 2), :]
        if w == OUT:
            return w_out.at[pl.ds(pl.multiple_of(j * ow, 16), ow), column(p)]
        if w == GU:
            return w_gu.at[j, n // 2, pl.ds(pl.multiple_of(lax.rem(n, 2) * half, 16), half), column(p)]
        return w_down.at[j, pl.ds(n * half, half), column(p)]

    own_slots = (
        (qkv.at[0], w_qkv.at[jz]),
        (out.at[0], w_out.at[pl.ds(pl.multiple_of(jz * ow, 16), ow), :]),
        (gu.at[0], w_gu.at[jz]),
        (down.at[0], w_down.at[jz]),
    )

    def own_copies(w, n):
        k = BASE[w] + n
        src, dst = shard_part(w, n, x), slot_part(w, n, jz, x)
        return (
            (z < n_t - 1, remote(src, dst, own_r.at[k], z_r.at[k, jz], me.right)),
            (z > 0, remote(src, dst, own_l.at[k], z_r.at[k, jz], me.left)),
        )

    def own_start(w, n):
        @pl.when(me.here)
        def _():
            for there, copy in own_copies(w, n):
                pl.when(there)(copy.start)

    def own_wait(w, n):
        @pl.when(me.here)
        def _():
            for there, copy in own_copies(w, n):
                pl.when(there)(copy.wait_send)

    def order(i):
        return jnp.where(c == 0, mb - 1 - i, i)

    def foreign(w, n, i):
        j = order(i)
        s = c * mb + j
        k = BASE[w] + n

        @pl.when(s != z)
        def _():
            piece = slot_part(w, n, j, x)
            to_right = remote(piece, piece, z_f.at[k, j], z_r.at[k, j], me.right)
            to_left = remote(piece, piece, z_f.at[k, j], z_r.at[k, j], me.left)
            to_right.wait_recv()
            pl.when((s < z) & (z < n_t - 1))(to_right.start)
            pl.when((s > z) & (z > 0))(to_left.start)
            for d in range(1, nx):
                remote(piece, piece, x_s.at[k, j, d], x_r.at[k, j, x], me.at_x(d)).start()

    def wait_slot(w, j):
        s = c * mb + j

        @pl.when(s != z)
        def _():
            for n in range(COUNT[w]):
                k = BASE[w] + n
                for d in range(1, nx):
                    p = lax.rem(x + d, nx)
                    piece = slot_part(w, n, j, p)
                    remote(piece, piece, x_s.at[k, j, d], x_r.at[k, j, p], me.right).wait_recv()

    def gu_step(n, i):
        if i == 0:
            @pl.when(n >= 2)
            def _():
                own_wait(GU, n - 2)
            own_start(GU, n)
        foreign(GU, n, i)

    def down_steps(i):
        for n in range(COUNT[DOWN]):
            if i == 0:
                own_wait(GU, n + 2)
                own_start(DOWN, n)
            foreign(DOWN, n, i)

    block = pl.ds(pl.multiple_of(z * block_rows, 128), block_rows)
    for plane, source, target in ((first_plane, tok, x_v), (second_plane, cot, cot_o)):
        for i in range(mb):
            zt = c * mb + i

            @pl.when(plane & (zt != z))
            def _(source=source, target=target, i=i, zt=zt):
                remote(source.at[i], target.at[block, :], a2a_s.at[i], a2a_r.at[z], {"tensor": zt}).start()

            @pl.when(plane & (zt == z))
            def _(source=source, target=target, i=i):
                pltpu.make_async_copy(source.at[i], target.at[block, :], loc.at[4]).start()

    @pl.when(me.here)
    def _():
        remote(lens.at[jz], len_v, lsem.at[0], lsem.at[1], me.sibling).start()
        len_v[...] = lens[jz]
        for w, (src, dst) in enumerate(own_slots):
            pltpu.make_async_copy(src, dst, loc.at[w]).start()

    own_start(QKV, 0)
    own_start(QKV, 1)
    for w, n in ((QKV, 0), (QKV, 1), (OUT, 0)):
        if w == OUT:
            own_wait(QKV, 0)
            own_start(OUT, 0)
        for i in range(mb):
            foreign(w, n, i)
        if (w, n) == (QKV, 0):
            for plane, target in ((first_plane, x_v), (second_plane, cot_o)):
                @pl.when(plane & me.here)
                def _(target=target):
                    for zs in range(n_t):
                        there = target.at[pl.ds(zs * block_rows, block_rows), :]

                        @pl.when(zs != z)
                        def _(zs=zs, there=there):
                            remote(there, there, a2a_s.at[0], a2a_r.at[zs], me.right).wait_recv()

                    pltpu.make_async_copy(tok.at[0], target.at[block, :], loc.at[4]).wait()
                    remote(target, target, sib.at[0], sib.at[1], me.sibling).start()

    @pl.when(second_plane)
    def _():
        for i in range(mb):
            @pl.loop(0, COUNT[GU])
            def _(n):
                gu_step(n, i)
            down_steps(i)

    @pl.when(jnp.logical_not(me.here))
    def _():
        remote(len_v, len_v, lsem.at[0], lsem.at[1], me.sibling).wait_recv()
        pl.when(first_plane)(remote(x_v, x_v, sib.at[0], sib.at[1], me.sibling).wait_recv)

    length = len_v[0:1, :]

    @pl.when(me.here)
    def _():
        for w, (src, dst) in enumerate(own_slots):
            pltpu.make_async_copy(src, dst, loc.at[w]).wait()

    for j in range(mb):
        wait_slot(QKV, j)
        wait_slot(OUT, j)

    pl.when(second_plane)(remote(first, first, vsem.at[0], vsem.at[1], me.sibling).wait_recv)
    gain_one, gain_two = gains[0:1, :], gains[1:2, :]

    def chunk(r):
        return pl.ds(pl.multiple_of(r * rows, 128), rows)

    def halves(r, core):
        return x_v.at[pl.ds(pl.multiple_of(r * rows + core * (rows // 2), 16), rows // 2), :]

    @pl.loop(0, CHUNKS)
    def _(r):
        @pl.when(second_plane)
        def _():
            mine, theirs = halves(r, c), halves(r, 1 - c)
            remote(mine, mine, hop.at[0, r], hop.at[1, r], me.sibling).wait_recv()
            remote(mine, mine, hsib.at[0, r], hsib.at[1, r], me.sibling).start()
            remote(theirs, theirs, hsib.at[0, r], hsib.at[1, r], me.sibling).wait_recv()

        at = chunk(r)
        a = (normalise(x_v[at, :].astype(F32)) * gain_one).astype(BF)
        a_v[at, :] = a
        cos_r, sin_r = cos[at, :], sin[at, :]
        for j in range(mb):
            q = dot(a, w_qkv[j, 0])
            k = dot(a, w_qkv[j, 1])
            v = dot(a, w_qkv[j, 2])
            for n in range(cols // PAIR):
                p = j * (cols // PAIR) + n
                lanes = slice(n * PAIR, (n + 1) * PAIR)
                q_v[p, at, :] = (rotate_pair(q[:, lanes], cos_r, sin_r) * SCORE_SCALE).astype(BF)
                k_v[p, at, :] = rotate_pair(k[:, lanes], cos_r, sin_r).astype(BF)
                v_v[p, at, :] = v[:, lanes].astype(BF)

    @pl.when(first_plane)
    def _():
        remote(v_v, first, vsem.at[0], vsem.at[1], {"section": 1 - me.section}).start()

        @pl.loop(0, pairs)
        def _(p):
            vu_v[p] = v_v[p]

    @pl.when(second_plane)
    def _():
        @pl.loop(0, pairs)
        def _(p):
            vu_v[p] = (0.5 * v_v[p].astype(F32) + 0.5 * first[p].astype(F32)).astype(BF)

    def keep(n, src, dst):
        return pltpu.make_async_copy(src, dst, outs.at[n])

    kept_early = [
        (x_v, x_o), (a_v, a_o), (q_v, q_o), (k_v, k_o), (vu_v, vu_o), (w_qkv, wq_o), (w_out, wo_o), (len_v, len_o),
    ]
    for n, (src, dst) in enumerate(kept_early):
        keep(n, src, dst).start()

    @pl.loop(0, pairs)
    def _(p):
        pl.when(first_plane)(lambda: gu_step(p, 0))
        lanes = pl.ds(pl.multiple_of(p * PAIR, PAIR), PAIR)

        def put_out(lo, hi, value):
            o_v[lo:hi, lanes] = value

        def put_lse(h, lo, hi, value):
            lse_v[p, h:h + 1, lo:hi] = value

        attend(q_v[p], k_v[p], vu_v[p], length, put_out, put_lse)

    kept_mid = [(o_v, o_o), (lse_v, lse_o)]
    for n, (src, dst) in enumerate(kept_mid, len(kept_early)):
        keep(n, src, dst).start()

    def swap(buffer, r, sems):
        return remote(s1.at[chunk(r), :], buffer.at[chunk(r), :], sems.at[0, r], sems.at[1, r], me.sibling)

    @pl.loop(0, CHUNKS)
    def _(r):
        s1[chunk(r), :] = dot(o_v[chunk(r), :], w_out[...]).astype(BF)
        swap(r1, r, e1).start()

    pl.when(first_plane)(lambda: down_steps(0))

    def finish(r):
        at = chunk(r)
        swap(r2, r, e2).wait_recv()
        r2[at, :] = (h_v[at, :] + s1[at, :].astype(F32) + r2[at, :].astype(F32)).astype(BF)

        @pl.when(first_plane)
        def _():
            mine = pl.ds(pl.multiple_of(r * rows + c * (rows // 2), 16), rows // 2)
            remote(
                r2.at[mine, :], x_v.at[mine, :], hop.at[0, r], hop.at[1, r], {"section": 1 - me.section}
            ).start()

    n_out = len(kept_early) + len(kept_mid)

    def kept_slot(i):
        j = order(i)
        base = n_out + 5 * i
        return [
            keep(base + t, src.at[j], dst.at[j])
            for t, (src, dst) in enumerate(((g_v, g_o), (u_v, u_o), (m_v, m_o), (w_gu, wg_o), (w_down, wd_o)))
        ]

    for i in range(mb):
        j = order(i)
        wait_slot(GU, j)
        wait_slot(DOWN, j)

        @pl.loop(0, CHUNKS)
        def _(r, i=i, j=j):
            at = chunk(r)
            if i + 1 < mb:
                pl.when(first_plane)(lambda: gu_step(r, i + 1))
            if i == 0:
                swap(r1, r, e1).wait_recv()
                h = x_v[at, :].astype(F32) + s1[at, :].astype(F32) + r1[at, :].astype(F32)
                h_v[at, :] = h
                b_v[at, :] = (normalise(h) * gain_two).astype(BF)
            b = b_v[at, :]
            gate = dot_nt(b, w_gu[j, 0])
            up = dot_nt(b, w_gu[j, 1])
            m = (gate / (1.0 + jnp.exp(-gate)) * up).astype(BF)
            g_v[j, at, :] = gate.astype(BF)
            u_v[j, at, :] = up.astype(BF)
            m_v[j, at, :] = m
            grown = dot(m, w_down[j])
            if i:
                grown = acc[at, :] + grown
            if i + 1 < mb:
                acc[at, :] = grown
            else:
                swap(r1, r, e1).wait_send()
                s1[at, :] = grown.astype(BF)
                swap(r2, r, e2).start()

                @pl.when(r > 0)
                def _():
                    finish(r - 1)

        for copy in kept_slot(i):
            copy.start()
        if i + 1 < mb:
            pl.when(first_plane)(lambda: down_steps(i + 1))

    finish(CHUNKS - 1)
    n_last = n_out + 5 * mb
    kept_last = [(h_v, h_o), (b_v, b_o), (r2, y_o)]
    for n, (src, dst) in enumerate(kept_last, n_last):
        keep(n, src, dst).start()

    for w, n in ((QKV, 1), (OUT, 0), (DOWN, 0), (DOWN, 1)):
        own_wait(w, n)
    for w in range(4):
        for n in range(COUNT[w]):
            k = BASE[w] + n
            for j in range(mb):
                s = c * mb + j

                @pl.when(s != z)
                def _(w=w, n=n, k=k, j=j, s=s):
                    piece = slot_part(w, n, j, x)
                    for d in range(1, nx):
                        remote(piece, piece, x_s.at[k, j, d], x_r.at[k, j, x], me.right).wait_send()
                    forwarded = ((s < z) & (z < n_t - 1)) | ((s > z) & (z > 0))
                    pl.when(forwarded)(remote(piece, piece, z_f.at[k, j], z_r.at[k, j], me.right).wait_send)

    for i in range(mb):
        @pl.when(c * mb + i != z)
        def _(i=i):
            remote(tok.at[i], tok.at[i], a2a_s.at[i], a2a_r.at[z], me.right).wait_send()

    @pl.when(me.here)
    def _():
        remote(lens.at[jz], len_v, lsem.at[0], lsem.at[1], me.sibling).wait_send()
        pl.when(first_plane)(remote(x_v, x_v, sib.at[0], sib.at[1], me.sibling).wait_send)
        pl.when(second_plane)(remote(cot_o, cot_o, sib.at[0], sib.at[1], me.sibling).wait_send)

    @pl.when(second_plane & jnp.logical_not(me.here))
    def _():
        remote(cot_o, cot_o, sib.at[0], sib.at[1], me.sibling).wait_recv()

    pl.when(first_plane)(remote(v_v, first, vsem.at[0], vsem.at[1], me.sibling).wait_send)
    for r in range(CHUNKS):
        swap(r2, r, e2).wait_send()
        mine = halves(r, c)
        pl.when(first_plane)(remote(mine, mine, hop.at[0, r], hop.at[1, r], me.sibling).wait_send)
        pl.when(second_plane)(remote(mine, mine, hsib.at[0, r], hsib.at[1, r], me.sibling).wait_send)
    for n, (src, dst) in enumerate(kept_early + kept_mid):
        keep(n, src, dst).wait()
    for i in range(mb):
        for copy in kept_slot(i):
            copy.wait()
    for n, (src, dst) in enumerate(kept_last, n_last):
        keep(n, src, dst).wait()


def forward(tokens, cotangent, lens, qkv, out, gu, down, gains, tables):
    mb, block_rows, dim = tokens.shape
    n_t = lax.axis_size("tensor")
    nx = lax.axis_size("dp") // 2
    seq = block_rows * n_t
    cols, ow, ff = qkv.shape[3], out.shape[1], down.shape[1]
    pairs = mb * cols // PAIR
    assert pairs == COUNT[GU] == CHUNKS
    dma = pltpu.SemaphoreType.DMA
    wide, heads = (seq, dim), (pairs, seq, PAIR)
    hidden, stat = (mb, seq, ff), (pairs, 2, seq)
    weights = [(mb, 3, dim, cols), (mb * ow, dim), (mb, 2, ff, dim), (mb, ff, dim)]
    shape = lambda s, t=BF: jax.ShapeDtypeStruct(s, t)
    return pl.pallas_call(
        forward_kernel,
        out_shape=(
            shape(wide), shape(wide), shape(wide), *(shape(w) for w in weights),
            shape(wide), shape(heads), shape(heads), shape(heads), shape((seq, pairs * PAIR)), shape(stat, F32),
            shape(wide, F32), shape(wide), shape(hidden), shape(hidden), shape(hidden), shape((8, 128), F32),
        ),
        in_specs=[ANY, ANY, VMEM, ANY, ANY, ANY, ANY, VMEM, VMEM, VMEM],
        out_specs=(ANY,) * 19,
        scratch_shapes=[
            *(pltpu.VMEM(w, BF) for w in weights),
            pltpu.VMEM(wide, BF), pltpu.VMEM(heads, BF), pltpu.VMEM(wide, BF),
            *[pltpu.VMEM(heads, BF)] * 4,
            pltpu.VMEM((seq, pairs * PAIR), BF), pltpu.VMEM(stat, F32),
            pltpu.VMEM(wide, F32), pltpu.VMEM(wide, BF),
            *[pltpu.VMEM(hidden, BF)] * 3,
            pltpu.VMEM(wide, F32),
            *[pltpu.VMEM(wide, BF)] * 3,
            pltpu.VMEM((8, 128), F32),
            dma((5,)), dma((mb,)), dma((n_t,)), dma((2,)), dma((N_PIECES,)), dma((N_PIECES,)),
            dma((N_PIECES, mb)), dma((N_PIECES, mb)), dma((N_PIECES, mb, nx)), dma((N_PIECES, mb, nx)),
            dma((2, CHUNKS)), dma((2, CHUNKS)), dma((2, CHUNKS)), dma((2, CHUNKS)), dma((2,)), dma((2,)),
            dma((13 + 5 * mb,)),
        ],
        compiler_params=pltpu.CompilerParams(
            collective_id=0, has_side_effects=True, vmem_limit_bytes=63 << 20
        ),
        name="forward_layer",
    )(tokens, cotangent, lens, qkv, out, gu, down, gains, *tables)


RING_DEPTH = 3
OWN_LAG = 3


def scatter_kernel(
    g_qkv, g_out, g_gu, g_down, y, dx,
    o_qkv, o_out, o_gu, o_down, o_y, o_dx,
    xb_qkv, xb_out, xb_gu, xb_down,
    zb_qkv, zb_out, zb_gu, zb_down,
    fb_qkv, fb_out, fb_gu, fb_down,
    a2a_s, a2a_r, x_s, x_r, z_s, z_r, zo_r, f_s, f_r,
):
    mb = g_qkv.shape[0]
    n_t = lax.axis_size("tensor")
    nx = lax.axis_size("dp") // 2
    dp = lax.axis_index("dp")
    z = lax.axis_index("tensor")
    x, c = dp // 2, lax.rem(dp, 2)
    dim = g_qkv.shape[2]
    part = dim // nx
    quarter = part // 2
    rows = y.shape[0] // n_t
    here = z // mb == c
    jz = z - c * mb
    sibling = {"dp": 2 * x + 1 - c}
    right, left = {"tensor": z + 1}, {"tensor": z - 1}
    half = g_down.shape[1] // 2
    pieces = [(w, n) for w in range(4) for n in range(COUNT[w])]
    n_k = N_PIECES

    barrier = pltpu.get_barrier_semaphore()
    for k in range(1, n_t):
        pl.semaphore_signal(
            barrier, inc=1, device_id={"tensor": lax.rem(z + k, n_t)}, device_id_type=MESH
        )
    for k in range(1, nx):
        pl.semaphore_signal(
            barrier, inc=1, device_id={"dp": 2 * lax.rem(x + k, nx) + c}, device_id_type=MESH
        )
    pl.semaphore_signal(barrier, inc=1, device_id=sibling, device_id_type=MESH)
    pl.semaphore_wait(barrier, n_t + nx - 1)

    def remote(src, dst, send, recv, to):
        return pltpu.make_async_remote_copy(
            src_ref=src, dst_ref=dst, send_sem=send, recv_sem=recv,
            device_id=to, device_id_type=MESH,
        )

    def grad_part(k, j, p):
        w, n = pieces[k]
        col = pl.ds(pl.multiple_of(p * part, 128), part)
        if w == QKV:
            return g_qkv.at[j, :, pl.ds(pl.multiple_of(p * part + n * quarter, 16), quarter), :]
        if w == OUT:
            return g_out.at[j, :, col]
        if w == GU:
            return g_gu.at[j, n // 2, pl.ds(n % 2 * half, half), col]
        return g_down.at[j, pl.ds(n * half, half), col]

    def buffer_part(bufs, k, j):
        w, n = pieces[k]
        if w == QKV:
            return bufs[w].at[j, :, pl.ds(n * quarter, quarter), :]
        if w == OUT:
            return bufs[w].at[j]
        if w == GU:
            return bufs[w].at[j, n // 2, pl.ds(n % 2 * half, half), :]
        return bufs[w].at[j, pl.ds(n * half, half), :]

    def x_buf(k, j, d):
        return buffer_part([b.at[d - 1] for b in (xb_qkv, xb_out, xb_gu, xb_down)], k, j)

    def z_buf(k, j):
        return buffer_part((zb_qkv, zb_out, zb_gu, zb_down), k, j)

    @pl.when(here)
    def _():
        for t, (src, dst) in enumerate(((y, o_y), (dx, o_dx))):
            for d in range(1, n_t):
                zt = lax.rem(z + d, n_t)
                block = src.at[pl.ds(pl.multiple_of(zt * rows, 128), rows), :]
                remote(block, dst.at[jz], a2a_s.at[t, d], a2a_r.at[t, jz], {"tensor": zt}).start()

    def x_send(n):
        k, i = n // mb, n % mb
        j = jnp.where(c == 0, i, mb - 1 - i)
        for d in range(1, nx):
            to = lax.rem(x + d, nx)
            yield remote(
                grad_part(k, j, to), x_buf(k, j, d), x_s.at[k, j, d], x_r.at[k, j, d],
                {"dp": 2 * to + c},
            )

    total = n_k * mb
    for t in range(RING_DEPTH):
        for copy in x_send(t):
            copy.start()

    def final_part(k):
        w, n = pieces[k]
        if w == QKV:
            return o_qkv, fb_qkv
        if w == OUT:
            return o_out, fb_out
        here_rows = pl.ds(n % 2 * half, half)
        if w == GU:
            return o_gu.at[n // 2, here_rows, :], fb_gu.at[n // 2, here_rows, :]
        return o_down.at[here_rows, :], fb_down.at[here_rows, :]

    def own_piece(k):
        w, n = pieces[k]
        total_sum = grad_part(k, jz, x)[...].astype(jnp.float32)
        for d in range(1, nx):
            total_sum = total_sum + x_buf(k, jz, d)[...].astype(jnp.float32)
        x_buf(k, jz, 1)[...] = total_sum.astype(jnp.bfloat16)

        @pl.when(z > 0)
        def _():
            piece = z_buf(k, jz)
            remote(piece, piece, z_s.at[k, jz], z_r.at[k, jz], right).wait_recv()
            x_buf(k, jz, 1)[...] = (
                x_buf(k, jz, 1)[...].astype(jnp.float32) + piece[...].astype(jnp.float32)
            ).astype(jnp.bfloat16)

        @pl.when(z < n_t - 1)
        def _():
            piece = z_buf(k, mb)
            remote(piece, piece, z_s.at[k, jz], zo_r.at[k], right).wait_recv()
            x_buf(k, jz, 1)[...] = (
                x_buf(k, jz, 1)[...].astype(jnp.float32) + piece[...].astype(jnp.float32)
            ).astype(jnp.bfloat16)

        summed = x_buf(k, jz, 1)
        out_ref, fin = final_part(k)
        if w == QKV:
            @pl.when(c == n)
            def _():
                out_ref[...] = summed[...].astype(jnp.float32)

            @pl.when(c != n)
            def _():
                remote(summed, fin, f_s.at[k], f_r.at[k], sibling).start()
        else:
            mine = pl.ds(pl.multiple_of(c * quarter, 128), quarter)
            theirs = pl.ds(pl.multiple_of((1 - c) * quarter, 128), quarter)
            out_ref[...] = summed[:, mine].astype(jnp.float32)
            remote(summed.at[:, theirs], fin, f_s.at[k], f_r.at[k], sibling).start()

    for k in range(n_k):
        for i in range(mb):
            n = k * mb + i
            j = jnp.where(c == 0, i, mb - 1 - i)
            s = c * mb + j
            if n + RING_DEPTH < total:
                for copy in x_send(n):
                    copy.wait_send()
                for copy in x_send(n + RING_DEPTH):
                    copy.start()
            for copy in x_send(n):
                copy.wait_recv()

            @pl.when(s != z)
            def _(k=k, j=j, s=s):
                total_sum = grad_part(k, j, x)[...].astype(jnp.float32)
                for d in range(1, nx):
                    total_sum = total_sum + x_buf(k, j, d)[...].astype(jnp.float32)
                x_buf(k, j, 1)[...] = total_sum.astype(jnp.bfloat16)

                @pl.when(((s > z) & (z > 0)) | ((s < z) & (z < n_t - 1)))
                def _():
                    piece = z_buf(k, j)
                    remote(piece, piece, z_s.at[k, j], z_r.at[k, j], right).wait_recv()
                    x_buf(k, j, 1)[...] = (
                        x_buf(k, j, 1)[...].astype(jnp.float32) + piece[...].astype(jnp.float32)
                    ).astype(jnp.bfloat16)

                @pl.when(s > z)
                def _():
                    remote(x_buf(k, j, 1), z_buf(k, j), z_s.at[k, j], z_r.at[k, j], right).start()

                @pl.when(s < z - 1)
                def _():
                    remote(x_buf(k, j, 1), z_buf(k, j), z_s.at[k, j], z_r.at[k, j], left).start()

                @pl.when(s == z - 1)
                def _():
                    remote(x_buf(k, j, 1), z_buf(k, mb), z_s.at[k, j], zo_r.at[k], left).start()

        if k >= OWN_LAG:
            @pl.when(here)
            def _(k=k):
                own_piece(k - OWN_LAG)

    @pl.when(here)
    def _():
        for k in range(max(0, n_k - OWN_LAG), n_k):
            own_piece(k)

    @pl.when(jnp.logical_not(here))
    def _():
        for k in range(n_k):
            w, n = pieces[k]
            out_ref, fin = final_part(k)
            if w == QKV:
                @pl.when(c == n)
                def _(k=k, out_ref=out_ref, fin=fin):
                    remote(fin, fin, f_s.at[k], f_r.at[k], sibling).wait_recv()
                    out_ref[...] = fin[...].astype(jnp.float32)
            else:
                remote(fin, fin, f_s.at[k], f_r.at[k], sibling).wait_recv()
                out_ref[...] = fin[...].astype(jnp.float32)

    for n in range(max(0, total - RING_DEPTH), total):
        for copy in x_send(n):
            copy.wait_send()

    for k in range(n_k):
        for j in range(mb):
            s = c * mb + j

            @pl.when(s != z)
            def _(k=k, j=j):
                piece = x_buf(k, j, 1)
                remote(piece, piece, z_s.at[k, j], z_r.at[k, j], right).wait_send()

    @pl.when(here)
    def _():
        for k in range(n_k):
            w, n = pieces[k]
            fin = final_part(k)[1]
            if w == QKV:
                @pl.when(c != n)
                def _(k=k, fin=fin):
                    remote(fin, fin, f_s.at[k], f_r.at[k], sibling).wait_send()
            else:
                remote(fin, fin, f_s.at[k], f_r.at[k], sibling).wait_send()

        for t, (src, dst) in enumerate(((y, o_y), (dx, o_dx))):
            for d in range(1, n_t):
                block = src.at[pl.ds(0, rows), :]
                remote(block, dst.at[0], a2a_s.at[t, d], a2a_r.at[t, jz], right).wait_send()
            dst[jz] = src[pl.ds(pl.multiple_of(z * rows, 128), rows), :]

    for t, dst in enumerate((o_y, o_dx)):
        for i in range(mb):
            @pl.when(c * mb + i != z)
            def _(t=t, i=i, dst=dst):
                remote(dst.at[i], dst.at[i], a2a_s.at[t, 0], a2a_r.at[t, i], right).wait_recv()


def scatter(g_qkv, g_out, g_gu, g_down, y, dx):
    mb, _, dim, cols = g_qkv.shape
    n_t = lax.axis_size("tensor")
    n_dp = lax.axis_size("dp")
    nx = n_dp // 2
    part, quarter = dim // nx, dim // n_dp
    out_rows, down_rows = g_out.shape[1], g_down.shape[1]
    rows = y.shape[0] // n_t
    dma = pltpu.SemaphoreType.DMA
    n_k = N_PIECES
    bf, f32 = jnp.bfloat16, jnp.float32

    def shapes(lead, split):
        return (
            (*lead, 3, split, cols), (*lead, out_rows, split),
            (*lead, 2, down_rows, split), (*lead, down_rows, split),
        )

    vmem = pl.BlockSpec(memory_space=pltpu.VMEM)
    finals = shapes((), quarter)
    return pl.pallas_call(
        scatter_kernel,
        out_shape=(
            *(jax.ShapeDtypeStruct(shape, f32) for shape in finals),
            jax.ShapeDtypeStruct((mb, rows, dim), bf),
            jax.ShapeDtypeStruct((mb, rows, dim), bf),
        ),
        in_specs=[vmem] * 6,
        out_specs=(vmem,) * 6,
        scratch_shapes=[
            *(pltpu.VMEM(shape, bf) for shape in shapes((nx - 1, mb), part)),
            *(pltpu.VMEM(shape, bf) for shape in shapes((mb + 1,), part)),
            *(pltpu.VMEM(shape, bf) for shape in finals),
            dma((2, n_t)), dma((2, mb)), dma((n_k, mb, nx)), dma((n_k, mb, nx)),
            dma((n_k, mb)), dma((n_k, mb)), dma((n_k,)), dma((n_k,)), dma((n_k,)),
        ],
        compiler_params=pltpu.CompilerParams(
            collective_id=1, has_side_effects=True, vmem_limit_bytes=62 << 20
        ),
        name="scatter_grads",
    )(g_qkv, g_out, g_gu, g_down, y, dx)


def attention_back_kernel(length, share, q, k, v, o, do, lse, first, cos, sin, dq_o, dk_o, dv_o, dv1_o, dk_a, dv_a):
    seq = q.shape[1]
    blk = seq // CHUNKS
    f32, bf = jnp.float32, jnp.bfloat16
    keys = k[0].astype(f32)
    k_t = keys.T.astype(bf)
    bias = key_bias(length[0:1, :], keys.shape)
    visible = causal_block(blk)
    queries = q[0].astype(f32)
    grads = do[...].astype(f32)
    heads = []
    for h in range(2):
        inside, extra = head_views(h, keys.shape)
        heads.append((
            jnp.where(inside, keys, jnp.where(extra, bias, 0.0)).astype(bf),
            jnp.where(inside, queries, jnp.where(extra, 1.0, 0.0)).astype(bf),
            jnp.where(inside, queries, 0.0).astype(bf),
            jnp.where(inside, grads, 0.0).astype(bf),
            k_t[h * HD:(h + 1) * HD],
        ))
    vals = v[0]
    for i in range(seq // blk):
        lo, hi = i * blk, (i + 1) * blk
        product = (grads[lo:hi] * o[lo:hi, :].astype(f32)).T
        parts = []
        for h in range(2):
            kh, qh, qz, gh, kt = heads[h]
            delta = jnp.sum(product[h * HD:(h + 1) * HD], axis=0, keepdims=True)
            stat = lse[0, h:h + 1, lo:hi]

            def side(a, b, mask):
                s = lax.dot_general(kh[a:b], qh[lo:hi], NT, preferred_element_type=f32)
                p = jnp.exp(s - stat)
                if mask:
                    p = jnp.where(visible, p, 0.0)
                dp = lax.dot_general(vals[a:b], gh[lo:hi], NT, preferred_element_type=f32)
                ds = (p * (dp - delta)).astype(bf)
                dv = jnp.dot(p.astype(bf), gh[lo:hi], preferred_element_type=f32)
                dk = jnp.dot(ds, qz[lo:hi], preferred_element_type=f32)
                if mask and h == 0:
                    dv_a[a:b, :] = dv
                    dk_a[a:b, :] = dk
                else:
                    dv_a[a:b, :] += dv
                    dk_a[a:b, :] += dk
                return jnp.dot(kt[:, a:b], ds, preferred_element_type=f32)

            dq_t = side(lo, hi, True)
            if i:
                dq_t = dq_t + side(0, lo, False)
            parts.append(dq_t)
        dq = jnp.concatenate(parts, axis=0).T * SCORE_SCALE
        dq_o[lo:hi, :] = rotate_pair(dq, cos[lo:hi, :], -sin[lo:hi, :]).astype(bf)
    dk_o[...] = rotate_pair(dk_a[...], cos[...], -sin[...]).astype(bf)
    dv_o[...] = (share[0] * dv_a[...] + first[0].astype(f32)).astype(bf)
    dv1_o[0] = ((1.0 - share[0]) * dv_a[...]).astype(bf)


def attention_back(length, share, q, k, vu, o, do, lse, first, tables):
    pairs, seq, _ = q.shape
    width = pairs * PAIR
    head = pl.BlockSpec((1, seq, PAIR), lambda p: (p, 0, 0))
    col = pl.BlockSpec((seq, PAIR), lambda p: (0, p))
    whole = pl.BlockSpec((seq, PAIR), lambda p: (0, 0))
    smem = pl.BlockSpec(memory_space=pltpu.SMEM)
    return pl.pallas_call(
        attention_back_kernel,
        grid=(pairs,),
        in_specs=[VMEM, smem, head, head, head, col, col, pl.BlockSpec((1, 2, seq), lambda p: (p, 0, 0)), head, whole, whole],
        out_specs=(col, col, col, head),
        out_shape=(*(jax.ShapeDtypeStruct((seq, width), BF),) * 3, jax.ShapeDtypeStruct((pairs, seq, PAIR), BF)),
        scratch_shapes=[pltpu.VMEM((seq, PAIR), jnp.float32)] * 2,
        compiler_params=pltpu.CompilerParams(vmem_limit_bytes=48 << 20),
        cost_estimate=pl.CostEstimate(flops=20 * seq * seq * width, bytes_accessed=20 * seq * width, transcendentals=pairs * seq * seq),
        name="attention_back",
    )(length, share, q, k, vu, o, do, lse, first, *tables)


def rms_norm(values, gain):
    return values * lax.rsqrt(jnp.mean(values * values, axis=-1, keepdims=True) + NORM_EPS) * gain


def pair_sum(part):
    mine = part.astype(jnp.bfloat16)
    swap = [(d, d ^ 1) for d in range(lax.axis_size("dp"))]
    theirs = lax.ppermute(mine, "dp", swap)
    return mine.astype(jnp.float32) + theirs.astype(jnp.float32)


def to_section(values, step):
    return lax.ppermute(values, "section", [(0, 1)] if step > 0 else [(1, 0)])


def backward_layer(weights, x, kept, length, share, tables, dy, first_grad):
    w_qkv, w_out, w_gu, w_down, gains = weights
    a, q, k, vu, o, lse, h, b, gates, ups, ms = kept
    mb = w_gu.shape[0]
    dmo = dy.astype(jnp.bfloat16)
    part = 0.0
    g_gu, g_down = [], []
    for j in range(mb):
        gate, up, m = gates[j].astype(F32), ups[j].astype(F32), ms[j]
        dm = dot_nt(dmo, w_down[j])
        g_down.append(dot_tn(m, dmo).astype(jnp.bfloat16))
        sig = jax.nn.sigmoid(gate)
        d_gate = (dm * up * (sig * (1.0 + gate * (1.0 - sig)))).astype(jnp.bfloat16)
        d_up = (dm * gate * sig).astype(jnp.bfloat16)
        part = part + dot(d_gate, w_gu[j, 0]) + dot(d_up, w_gu[j, 1])
        g_gu.append(jnp.stack([dot_tn(d_gate, b), dot_tn(d_up, b)]).astype(jnp.bfloat16))
    db = pair_sum(part)
    _, norm_back = jax.vjp(rms_norm, h, gains[1])
    dh, dg2 = norm_back(db)
    dh = dy + dh
    dao = dh.astype(jnp.bfloat16)
    do = dot_nt(dao, w_out).astype(jnp.bfloat16)
    cols = w_qkv.shape[3]
    g_out = dot_tn(o, dao).astype(jnp.bfloat16).reshape(mb, -1, dao.shape[1])
    dq, dk, dv, dv1 = attention_back(length, share, q, k, vu, o, do, lse, first_grad, tables)
    grads = (dq, dk, dv)
    g_qkv = jnp.stack([
        jnp.stack([dot_tn(a, g[:, j * cols:(j + 1) * cols]) for g in grads]) for j in range(mb)
    ]).astype(jnp.bfloat16)
    da = pair_sum(sum(dot_nt(g[:, j * cols:(j + 1) * cols], w_qkv[j, i]) for i, g in enumerate(grads) for j in range(mb)))
    _, norm_back = jax.vjp(rms_norm, x.astype(jnp.float32), gains[0])
    dx, dg1 = norm_back(da)
    return dh + dx, dv1, (g_qkv, g_out, jnp.stack(g_gu), jnp.stack(g_down), jnp.stack([dg1, dg2]))


def shards(tokens, lengths, qkv_weight, out_weight, gate_up_weight, down_weight, norm_gains, cotangent):
    is_first = lax.axis_index("section") == 0
    dp = lax.axis_index("dp")
    mb, rows, dim = tokens.shape
    seq_len = rows * lax.axis_size("tensor")
    share = jnp.where(is_first, 1.0, 0.5).astype(F32)[None]
    tables = tuple(jnp.asarray(t) for t in rope_tables(seq_len))
    lens = jnp.broadcast_to(lengths.astype(F32)[:, None, None], (mb, 8, 128))
    (
        x, start, y, w_qkv, w_out, w_gu, w_down, a, q, k, vu, o, lse, h, b, gates, ups, ms, length,
    ) = forward(
        tokens, cotangent, lens, qkv_weight, out_weight, jnp.swapaxes(gate_up_weight, 2, 3), down_weight,
        norm_gains[0], tables,
    )
    weights = (w_qkv, w_out, w_gu, w_down, norm_gains[0])
    kept = (a, q, k, vu, o, lse, h, b, gates, ups, ms)
    mask = jnp.arange(seq_len)[:, None].astype(F32) < length[0, 0]
    cot = jnp.where(mask, start.astype(F32), 0.0)
    dx, dv1, _ = backward_layer(weights, x, kept, length, share, tables, cot, jnp.zeros_like(q))
    dy = jnp.where(is_first, to_section(dx.astype(BF), -1).astype(F32), cot)
    first_grad = to_section(dv1, -1)
    dx, _, grads = backward_layer(weights, x, kept, length, share, tables, dy, first_grad)
    g_qkv, g_out, g_gu, g_down, g_gain = grads
    gain = lax.psum_scatter(
        jnp.where(lax.rem(dp, 2) == 0, g_gain, 0.0), ("dp", "tensor"), scatter_dimension=1, tiled=True
    )
    o_qkv, o_out, o_gu, o_down, o_y, o_dx = scatter(g_qkv, g_out, g_gu, g_down, y, dx.astype(BF))
    return (
        o_y[None], o_dx.astype(F32)[None], o_qkv[None], o_out[None], jnp.swapaxes(o_gu, 1, 2)[None], o_down[None],
        gain[None],
    )


def solution(mesh):
    in_specs = (
        P("dp", "tensor", None),
        P("dp"),
        P("section", None, None, "tensor"),
        P("section", "tensor", None),
        P("section", None, None, "tensor"),
        P("section", "tensor", None),
        P("section", None, None),
        P("dp", "tensor", None),
    )
    out_specs = (
        P("section", "dp", "tensor", None),
        P("section", "dp", "tensor", None),
        P("section", None, "dp", "tensor"),
        P("section", "tensor", "dp"),
        P("section", None, "dp", "tensor"),
        P("section", "tensor", "dp"),
        P("section", None, ("dp", "tensor")),
    )
    return jax.shard_map(shards, mesh=mesh, in_specs=in_specs, out_specs=out_specs, check_vma=False)
```

```python
import jax
import jax.numpy as jnp
import numpy as np
from jax import lax
from jax.experimental import pallas as pl
from jax.experimental.pallas import tpu as pltpu
from jax.sharding import PartitionSpec as P

MESH = pl.DeviceIdType.MESH
ANY = pl.BlockSpec(memory_space=pl.ANY)
VMEM = pl.BlockSpec(memory_space=pltpu.VMEM)
NORM_EPS = 1e-6
ROPE_BASE = 10000.0
SCORE_SCALE = 0.125
MASK_VALUE = -1e30
HD = 64
PAIR = 2 * HD
CHUNKS = 4
NT = (((1,), (1,)), ((), ()))
BF, F32 = jnp.bfloat16, jnp.float32

QKV, OUT, GU, DOWN = range(4)
COUNT = (2, 1, 4, 2)
BASE = (0, 2, 3, 7)
N_PIECES = 9


def dot(a, b):
    return jnp.dot(a, b, preferred_element_type=F32)


def dot_nt(a, b):
    return lax.dot_general(a, b, NT, preferred_element_type=F32)


def dot_tn(a, b):
    return lax.dot_general(a, b, (((0,), (0,)), ((), ())), preferred_element_type=F32)


def remote(src, dst, send, recv, to):
    return pltpu.make_async_remote_copy(
        src_ref=src, dst_ref=dst, send_sem=send, recv_sem=recv, device_id=to, device_id_type=MESH
    )


class Place:
    def __init__(self, mb):
        self.n_t = lax.axis_size("tensor")
        self.nx = lax.axis_size("dp") // 2
        self.section = lax.axis_index("section")
        dp = lax.axis_index("dp")
        self.z = lax.axis_index("tensor")
        self.x, self.c = dp // 2, lax.rem(dp, 2)
        self.here = self.z // mb == self.c
        self.jz = self.z - self.c * mb
        self.sibling = {"dp": 2 * self.x + 1 - self.c}
        self.right, self.left = {"tensor": self.z + 1}, {"tensor": self.z - 1}

    def at_x(self, d):
        return {"dp": 2 * lax.rem(self.x + d, self.nx) + self.c}

    def meet(self):
        barrier = pltpu.get_barrier_semaphore()
        partners = [{"tensor": lax.rem(self.z + k, self.n_t)} for k in range(1, self.n_t)]
        partners += [self.at_x(k) for k in range(1, self.nx)]
        partners += [self.sibling, {"section": 1 - self.section}]
        for partner in partners:
            pl.semaphore_signal(barrier, inc=1, device_id=partner, device_id_type=MESH)
        pl.semaphore_wait(barrier, len(partners))


def rope_tables(positions):
    lane = np.arange(PAIR)
    frequency = ROPE_BASE ** (-(lane % (HD // 2)) * 2.0 / HD)
    angles = np.arange(positions)[:, None] * frequency[None, :]
    sign = np.where(lane % HD < HD // 2, -1.0, 1.0)
    return np.cos(angles).astype(np.float32), (np.sin(angles) * sign).astype(np.float32)


def rotate_pair(values, cos, sin):
    lane = lax.broadcasted_iota(jnp.int32, values.shape, 1)
    partner = jnp.where(
        lax.rem(lane, HD) < HD // 2,
        pltpu.roll(values, PAIR - HD // 2, 1),
        pltpu.roll(values, HD // 2, 1),
    )
    return values * cos + partner * sin


def normalise(values):
    return values * lax.rsqrt(jnp.mean(values * values, axis=-1, keepdims=True) + NORM_EPS)


def head_views(h, shape):
    lane = lax.broadcasted_iota(jnp.int32, shape, 1)
    return lane // HD == h, lane == (1 - h) * HD


def key_bias(length, shape):
    key = lax.broadcasted_iota(jnp.int32, shape, 0).astype(F32)
    return jnp.where(key < length, 0.0, MASK_VALUE)


def causal_block(blk):
    key = lax.broadcasted_iota(jnp.int32, (blk, blk), 0)
    query = lax.broadcasted_iota(jnp.int32, (blk, blk), 1)
    return key <= query


def attend(queries, keys, vals, length, put_out, put_lse):
    seq = queries.shape[0]
    blk = seq // CHUNKS
    v_t = vals.astype(F32).T.astype(BF)
    keys, queries = keys.astype(F32), queries.astype(F32)
    bias = key_bias(length, keys.shape)
    visible = causal_block(blk)
    heads = []
    for h in range(2):
        inside, extra = head_views(h, keys.shape)
        heads.append((
            jnp.where(inside, keys, jnp.where(extra, bias, 0.0)).astype(BF),
            jnp.where(inside, queries, jnp.where(extra, 1.0, 0.0)).astype(BF),
            v_t[h * HD:(h + 1) * HD],
        ))
    for i in range(CHUNKS):
        lo, hi = i * blk, (i + 1) * blk
        parts = []
        for h in range(2):
            kh, qh, vh = heads[h]
            qi = qh[lo:hi]
            s_diag = jnp.where(visible, dot_nt(kh[lo:hi], qi), MASK_VALUE)
            top = jnp.max(s_diag, axis=0, keepdims=True)
            if i:
                s_full = dot_nt(kh[:lo], qi)
                top = jnp.maximum(top, jnp.max(s_full, axis=0, keepdims=True))
            p_diag = jnp.exp(s_diag - top)
            total = jnp.sum(p_diag, axis=0, keepdims=True)
            acc = dot(vh[:, lo:hi], p_diag.astype(BF))
            if i:
                p_full = jnp.exp(s_full - top)
                total = total + jnp.sum(p_full, axis=0, keepdims=True)
                acc = acc + dot(vh[:, :lo], p_full.astype(BF))
            parts.append(acc / total)
            put_lse(h, lo, hi, top + jnp.log(total))
        put_out(lo, hi, jnp.concatenate(parts, axis=0).T.astype(BF))


def forward_kernel(
    tok, cot, lens, qkv, out, gu, down, gains, cos, sin,
    x_o, cot_o, y_o, wq_o, wo_o, wg_o, wd_o, a_o, q_o, k_o, vu_o, o_o, lse_o, h_o, b_o, g_o, u_o, m_o, len_o,
    w_qkv, w_out, w_gu, w_down, x_v, first, a_v, q_v, k_v, v_v, vu_v, o_v, lse_v, h_v, b_v, g_v, u_v, m_v,
    acc, s1, r1, r2, len_v,
    loc, a2a_s, a2a_r, sib, own_r, own_l, z_r, z_f, x_s, x_r, hop, hsib, e1, e2, vsem, lsem, outs,
):
    mb, block_rows, dim = tok.shape
    me = Place(mb)
    x, c, z, n_t, nx, jz = me.x, me.c, me.z, me.n_t, me.nx, me.jz
    part = dim // nx
    cols, ow, half = qkv.shape[3], out.shape[1], down.shape[1] // 2
    seq = x_v.shape[0]
    rows = seq // CHUNKS
    pairs = q_v.shape[0]
    first_plane, second_plane = me.section == 0, me.section == 1
    me.meet()

    def column(p):
        return pl.ds(pl.multiple_of(p * part, 128), part)

    def shard_part(w, n, p):
        if w == QKV:
            return qkv.at[0, :, pl.ds(pl.multiple_of(p * part + n * (part // 2), 16), part // 2), :]
        if w == OUT:
            return out.at[0, :, column(p)]
        if w == GU:
            return gu.at[0, n // 2, pl.ds(pl.multiple_of(lax.rem(n, 2) * half, 16), half), column(p)]
        return down.at[0, pl.ds(n * half, half), column(p)]

    def slot_part(w, n, j, p):
        if w == QKV:
            return w_qkv.at[j, :, pl.ds(pl.multiple_of(p * part + n * (part // 2), 16), part // 2), :]
        if w == OUT:
            return w_out.at[pl.ds(pl.multiple_of(j * ow, 16), ow), column(p)]
        if w == GU:
            return w_gu.at[j, n // 2, pl.ds(pl.multiple_of(lax.rem(n, 2) * half, 16), half), column(p)]
        return w_down.at[j, pl.ds(n * half, half), column(p)]

    own_slots = (
        (qkv.at[0], w_qkv.at[jz]),
        (out.at[0], w_out.at[pl.ds(pl.multiple_of(jz * ow, 16), ow), :]),
        (gu.at[0], w_gu.at[jz]),
        (down.at[0], w_down.at[jz]),
    )

    def own_copies(w, n):
        k = BASE[w] + n
        src, dst = shard_part(w, n, x), slot_part(w, n, jz, x)
        return (
            (z < n_t - 1, remote(src, dst, own_r.at[k], z_r.at[k, jz], me.right)),
            (z > 0, remote(src, dst, own_l.at[k], z_r.at[k, jz], me.left)),
        )

    def own_start(w, n):
        @pl.when(me.here)
        def _():
            for there, copy in own_copies(w, n):
                pl.when(there)(copy.start)

    def own_wait(w, n):
        @pl.when(me.here)
        def _():
            for there, copy in own_copies(w, n):
                pl.when(there)(copy.wait_send)

    def order(i):
        return jnp.where(c == 0, mb - 1 - i, i)

    def foreign(w, n, i):
        j = order(i)
        s = c * mb + j
        k = BASE[w] + n

        @pl.when(s != z)
        def _():
            piece = slot_part(w, n, j, x)
            to_right = remote(piece, piece, z_f.at[k, j], z_r.at[k, j], me.right)
            to_left = remote(piece, piece, z_f.at[k, j], z_r.at[k, j], me.left)
            to_right.wait_recv()
            pl.when((s < z) & (z < n_t - 1))(to_right.start)
            pl.when((s > z) & (z > 0))(to_left.start)
            for d in range(1, nx):
                remote(piece, piece, x_s.at[k, j, d], x_r.at[k, j, x], me.at_x(d)).start()

    def wait_slot(w, j):
        s = c * mb + j

        @pl.when(s != z)
        def _():
            for n in range(COUNT[w]):
                k = BASE[w] + n
                for d in range(1, nx):
                    p = lax.rem(x + d, nx)
                    piece = slot_part(w, n, j, p)
                    remote(piece, piece, x_s.at[k, j, d], x_r.at[k, j, p], me.right).wait_recv()

    def gu_step(n, i):
        if i == 0:
            @pl.when(n >= 2)
            def _():
                own_wait(GU, n - 2)
            own_start(GU, n)
        foreign(GU, n, i)

    def down_steps(i):
        for n in range(COUNT[DOWN]):
            if i == 0:
                own_wait(GU, n + 2)
                own_start(DOWN, n)
            foreign(DOWN, n, i)

    block = pl.ds(pl.multiple_of(z * block_rows, 128), block_rows)
    for plane, source, target in ((first_plane, tok, x_v), (second_plane, cot, cot_o)):
        for i in range(mb):
            zt = c * mb + i

            @pl.when(plane & (zt != z))
            def _(source=source, target=target, i=i, zt=zt):
                remote(source.at[i], target.at[block, :], a2a_s.at[i], a2a_r.at[z], {"tensor": zt}).start()

            @pl.when(plane & (zt == z))
            def _(source=source, target=target, i=i):
                pltpu.make_async_copy(source.at[i], target.at[block, :], loc.at[4]).start()

    @pl.when(me.here)
    def _():
        remote(lens.at[jz], len_v, lsem.at[0], lsem.at[1], me.sibling).start()
        len_v[...] = lens[jz]
        for w, (src, dst) in enumerate(own_slots):
            pltpu.make_async_copy(src, dst, loc.at[w]).start()

    own_start(QKV, 0)
    own_start(QKV, 1)
    for w, n in ((QKV, 0), (QKV, 1), (OUT, 0)):
        if w == OUT:
            own_wait(QKV, 0)
            own_start(OUT, 0)
        for i in range(mb):
            foreign(w, n, i)
        if (w, n) == (QKV, 0):
            for plane, target in ((first_plane, x_v), (second_plane, cot_o)):
                @pl.when(plane & me.here)
                def _(target=target):
                    for zs in range(n_t):
                        there = target.at[pl.ds(zs * block_rows, block_rows), :]

                        @pl.when(zs != z)
                        def _(zs=zs, there=there):
                            remote(there, there, a2a_s.at[0], a2a_r.at[zs], me.right).wait_recv()

                    pltpu.make_async_copy(tok.at[0], target.at[block, :], loc.at[4]).wait()
                    remote(target, target, sib.at[0], sib.at[1], me.sibling).start()

    @pl.when(second_plane)
    def _():
        for i in range(mb):
            @pl.loop(0, COUNT[GU])
            def _(n):
                gu_step(n, i)
            down_steps(i)

    @pl.when(jnp.logical_not(me.here))
    def _():
        remote(len_v, len_v, lsem.at[0], lsem.at[1], me.sibling).wait_recv()
        pl.when(first_plane)(remote(x_v, x_v, sib.at[0], sib.at[1], me.sibling).wait_recv)

    length = len_v[0:1, :]

    @pl.when(me.here)
    def _():
        for w, (src, dst) in enumerate(own_slots):
            pltpu.make_async_copy(src, dst, loc.at[w]).wait()

    for j in range(mb):
        wait_slot(QKV, j)
        wait_slot(OUT, j)

    pl.when(second_plane)(remote(first, first, vsem.at[0], vsem.at[1], me.sibling).wait_recv)
    gain_one, gain_two = gains[0:1, :], gains[1:2, :]

    def chunk(r):
        return pl.ds(pl.multiple_of(r * rows, 128), rows)

    def halves(r, core):
        return x_v.at[pl.ds(pl.multiple_of(r * rows + core * (rows // 2), 16), rows // 2), :]

    @pl.loop(0, CHUNKS)
    def _(r):
        @pl.when(second_plane)
        def _():
            mine, theirs = halves(r, c), halves(r, 1 - c)
            remote(mine, mine, hop.at[0, r], hop.at[1, r], me.sibling).wait_recv()
            remote(mine, mine, hsib.at[0, r], hsib.at[1, r], me.sibling).start()
            remote(theirs, theirs, hsib.at[0, r], hsib.at[1, r], me.sibling).wait_recv()

        at = chunk(r)
        a = (normalise(x_v[at, :].astype(F32)) * gain_one).astype(BF)
        a_v[at, :] = a
        cos_r, sin_r = cos[at, :], sin[at, :]
        for j in range(mb):
            q = dot(a, w_qkv[j, 0])
            k = dot(a, w_qkv[j, 1])
            v = dot(a, w_qkv[j, 2])
            for n in range(cols // PAIR):
                p = j * (cols // PAIR) + n
                lanes = slice(n * PAIR, (n + 1) * PAIR)
                q_v[p, at, :] = (rotate_pair(q[:, lanes], cos_r, sin_r) * SCORE_SCALE).astype(BF)
                k_v[p, at, :] = rotate_pair(k[:, lanes], cos_r, sin_r).astype(BF)
                v_v[p, at, :] = v[:, lanes].astype(BF)

    @pl.when(first_plane)
    def _():
        remote(v_v, first, vsem.at[0], vsem.at[1], {"section": 1 - me.section}).start()

        @pl.loop(0, pairs)
        def _(p):
            vu_v[p] = v_v[p]

    @pl.when(second_plane)
    def _():
        @pl.loop(0, pairs)
        def _(p):
            vu_v[p] = (0.5 * v_v[p].astype(F32) + 0.5 * first[p].astype(F32)).astype(BF)

    def keep(n, src, dst):
        return pltpu.make_async_copy(src, dst, outs.at[n])

    kept_early = [
        (x_v, x_o), (a_v, a_o), (q_v, q_o), (k_v, k_o), (vu_v, vu_o), (w_qkv, wq_o), (w_out, wo_o), (len_v, len_o),
    ]
    for n, (src, dst) in enumerate(kept_early):
        keep(n, src, dst).start()

    @pl.loop(0, pairs)
    def _(p):
        pl.when(first_plane)(lambda: gu_step(p, 0))
        lanes = pl.ds(pl.multiple_of(p * PAIR, PAIR), PAIR)

        def put_out(lo, hi, value):
            o_v[lo:hi, lanes] = value

        def put_lse(h, lo, hi, value):
            lse_v[p, h:h + 1, lo:hi] = value

        attend(q_v[p], k_v[p], vu_v[p], length, put_out, put_lse)

    kept_mid = [(o_v, o_o), (lse_v, lse_o)]
    for n, (src, dst) in enumerate(kept_mid, len(kept_early)):
        keep(n, src, dst).start()

    def swap(buffer, r, sems):
        return remote(s1.at[chunk(r), :], buffer.at[chunk(r), :], sems.at[0, r], sems.at[1, r], me.sibling)

    @pl.loop(0, CHUNKS)
    def _(r):
        s1[chunk(r), :] = dot(o_v[chunk(r), :], w_out[...]).astype(BF)
        swap(r1, r, e1).start()

    pl.when(first_plane)(lambda: down_steps(0))

    def finish(r):
        at = chunk(r)
        swap(r2, r, e2).wait_recv()
        r2[at, :] = (h_v[at, :] + s1[at, :].astype(F32) + r2[at, :].astype(F32)).astype(BF)

        @pl.when(first_plane)
        def _():
            mine = pl.ds(pl.multiple_of(r * rows + c * (rows // 2), 16), rows // 2)
            remote(
                r2.at[mine, :], x_v.at[mine, :], hop.at[0, r], hop.at[1, r], {"section": 1 - me.section}
            ).start()

    n_out = len(kept_early) + len(kept_mid)

    def kept_slot(i):
        j = order(i)
        base = n_out + 5 * i
        return [
            keep(base + t, src.at[j], dst.at[j])
            for t, (src, dst) in enumerate(((g_v, g_o), (u_v, u_o), (m_v, m_o), (w_gu, wg_o), (w_down, wd_o)))
        ]

    for i in range(mb):
        j = order(i)
        wait_slot(GU, j)
        wait_slot(DOWN, j)

        @pl.loop(0, CHUNKS)
        def _(r, i=i, j=j):
            at = chunk(r)
            if i + 1 < mb:
                pl.when(first_plane)(lambda: gu_step(r, i + 1))
            if i == 0:
                swap(r1, r, e1).wait_recv()
                h = x_v[at, :].astype(F32) + s1[at, :].astype(F32) + r1[at, :].astype(F32)
                h_v[at, :] = h
                b_v[at, :] = (normalise(h) * gain_two).astype(BF)
            b = b_v[at, :]
            gate = dot_nt(b, w_gu[j, 0])
            up = dot_nt(b, w_gu[j, 1])
            m = (gate / (1.0 + jnp.exp(-gate)) * up).astype(BF)
            g_v[j, at, :] = gate.astype(BF)
            u_v[j, at, :] = up.astype(BF)
            m_v[j, at, :] = m
            grown = dot(m, w_down[j])
            if i:
                grown = acc[at, :] + grown
            if i + 1 < mb:
                acc[at, :] = grown
            else:
                swap(r1, r, e1).wait_send()
                s1[at, :] = grown.astype(BF)
                swap(r2, r, e2).start()

                @pl.when(r > 0)
                def _():
                    finish(r - 1)

        for copy in kept_slot(i):
            copy.start()
        if i + 1 < mb:
            pl.when(first_plane)(lambda: down_steps(i + 1))

    finish(CHUNKS - 1)
    n_last = n_out + 5 * mb
    kept_last = [(h_v, h_o), (b_v, b_o), (r2, y_o)]
    for n, (src, dst) in enumerate(kept_last, n_last):
        keep(n, src, dst).start()

    for w, n in ((QKV, 1), (OUT, 0), (DOWN, 0), (DOWN, 1)):
        own_wait(w, n)
    for w in range(4):
        for n in range(COUNT[w]):
            k = BASE[w] + n
            for j in range(mb):
                s = c * mb + j

                @pl.when(s != z)
                def _(w=w, n=n, k=k, j=j, s=s):
                    piece = slot_part(w, n, j, x)
                    for d in range(1, nx):
                        remote(piece, piece, x_s.at[k, j, d], x_r.at[k, j, x], me.right).wait_send()
                    forwarded = ((s < z) & (z < n_t - 1)) | ((s > z) & (z > 0))
                    pl.when(forwarded)(remote(piece, piece, z_f.at[k, j], z_r.at[k, j], me.right).wait_send)

    for i in range(mb):
        @pl.when(c * mb + i != z)
        def _(i=i):
            remote(tok.at[i], tok.at[i], a2a_s.at[i], a2a_r.at[z], me.right).wait_send()

    @pl.when(me.here)
    def _():
        remote(lens.at[jz], len_v, lsem.at[0], lsem.at[1], me.sibling).wait_send()
        pl.when(first_plane)(remote(x_v, x_v, sib.at[0], sib.at[1], me.sibling).wait_send)
        pl.when(second_plane)(remote(cot_o, cot_o, sib.at[0], sib.at[1], me.sibling).wait_send)

    @pl.when(second_plane & jnp.logical_not(me.here))
    def _():
        remote(cot_o, cot_o, sib.at[0], sib.at[1], me.sibling).wait_recv()

    pl.when(first_plane)(remote(v_v, first, vsem.at[0], vsem.at[1], me.sibling).wait_send)
    for r in range(CHUNKS):
        swap(r2, r, e2).wait_send()
        mine = halves(r, c)
        pl.when(first_plane)(remote(mine, mine, hop.at[0, r], hop.at[1, r], me.sibling).wait_send)
        pl.when(second_plane)(remote(mine, mine, hsib.at[0, r], hsib.at[1, r], me.sibling).wait_send)
    for n, (src, dst) in enumerate(kept_early + kept_mid):
        keep(n, src, dst).wait()
    for i in range(mb):
        for copy in kept_slot(i):
            copy.wait()
    for n, (src, dst) in enumerate(kept_last, n_last):
        keep(n, src, dst).wait()


def forward(tokens, cotangent, lens, qkv, out, gu, down, gains, tables):
    mb, block_rows, dim = tokens.shape
    n_t = lax.axis_size("tensor")
    nx = lax.axis_size("dp") // 2
    seq = block_rows * n_t
    cols, ow, ff = qkv.shape[3], out.shape[1], down.shape[1]
    pairs = mb * cols // PAIR
    assert pairs == COUNT[GU] == CHUNKS
    dma = pltpu.SemaphoreType.DMA
    wide, heads = (seq, dim), (pairs, seq, PAIR)
    hidden, stat = (mb, seq, ff), (pairs, 2, seq)
    weights = [(mb, 3, dim, cols), (mb * ow, dim), (mb, 2, ff, dim), (mb, ff, dim)]
    shape = lambda s, t=BF: jax.ShapeDtypeStruct(s, t)
    return pl.pallas_call(
        forward_kernel,
        out_shape=(
            shape(wide), shape(wide), shape(wide), *(shape(w) for w in weights),
            shape(wide), shape(heads), shape(heads), shape(heads), shape((seq, pairs * PAIR)), shape(stat, F32),
            shape(wide, F32), shape(wide), shape(hidden), shape(hidden), shape(hidden), shape((8, 128), F32),
        ),
        in_specs=[ANY, ANY, VMEM, ANY, ANY, ANY, ANY, VMEM, VMEM, VMEM],
        out_specs=(ANY,) * 19,
        scratch_shapes=[
            *(pltpu.VMEM(w, BF) for w in weights),
            pltpu.VMEM(wide, BF), pltpu.VMEM(heads, BF), pltpu.VMEM(wide, BF),
            *[pltpu.VMEM(heads, BF)] * 4,
            pltpu.VMEM((seq, pairs * PAIR), BF), pltpu.VMEM(stat, F32),
            pltpu.VMEM(wide, F32), pltpu.VMEM(wide, BF),
            *[pltpu.VMEM(hidden, BF)] * 3,
            pltpu.VMEM(wide, F32),
            *[pltpu.VMEM(wide, BF)] * 3,
            pltpu.VMEM((8, 128), F32),
            dma((5,)), dma((mb,)), dma((n_t,)), dma((2,)), dma((N_PIECES,)), dma((N_PIECES,)),
            dma((N_PIECES, mb)), dma((N_PIECES, mb)), dma((N_PIECES, mb, nx)), dma((N_PIECES, mb, nx)),
            dma((2, CHUNKS)), dma((2, CHUNKS)), dma((2, CHUNKS)), dma((2, CHUNKS)), dma((2,)), dma((2,)),
            dma((13 + 5 * mb,)),
        ],
        compiler_params=pltpu.CompilerParams(
            collective_id=0, has_side_effects=True, vmem_limit_bytes=63 << 20
        ),
        name="forward_layer",
    )(tokens, cotangent, lens, qkv, out, gu, down, gains, *tables)


LAG = 2
AHEAD = 3
FF, OUTS, HEADS = range(3)
FF_PIECES = 6
PIECES = [(FF, n) for n in range(FF_PIECES)] + [(OUTS, 0), (HEADS, 0), (HEADS, 1)]
KEY = (0, FF_PIECES, FF_PIECES + 1)


def attend_back(queries, keys, vals, outs, grads, stats, length, add_dv, add_dk, put_dq):
    seq = queries.shape[0]
    blk = seq // CHUNKS
    keys, queries, grads = keys.astype(F32), queries.astype(F32), grads.astype(F32)
    k_t = keys.T.astype(BF)
    bias = key_bias(length, keys.shape)
    visible = causal_block(blk)
    heads = []
    for h in range(2):
        inside, extra = head_views(h, keys.shape)
        heads.append((
            jnp.where(inside, keys, jnp.where(extra, bias, 0.0)).astype(BF),
            jnp.where(inside, queries, jnp.where(extra, 1.0, 0.0)).astype(BF),
            jnp.where(inside, queries, 0.0).astype(BF),
            jnp.where(inside, grads, 0.0).astype(BF),
            k_t[h * HD:(h + 1) * HD],
        ))
    for i in range(CHUNKS):
        lo, hi = i * blk, (i + 1) * blk
        product = (grads[lo:hi] * outs[lo:hi].astype(F32)).T
        parts = []
        for h in range(2):
            kh, qh, qz, gh, kt = heads[h]
            delta = jnp.sum(product[h * HD:(h + 1) * HD], axis=0, keepdims=True)
            stat = stats(h, lo, hi)

            def side(a, b, diagonal):
                p = jnp.exp(dot_nt(kh[a:b], qh[lo:hi]) - stat)
                if diagonal:
                    p = jnp.where(visible, p, 0.0)
                dp = dot_nt(vals[a:b], gh[lo:hi])
                ds = (p * (dp - delta)).astype(BF)
                fresh = diagonal and h == 0
                add_dv(a, b, dot(p.astype(BF), gh[lo:hi]), fresh)
                add_dk(a, b, dot(ds, qz[lo:hi]), fresh)
                return dot(kt[:, a:b], ds)

            dq_t = side(lo, hi, True)
            if i:
                dq_t = dq_t + side(0, lo, False)
            parts.append(dq_t)
        put_dq(lo, hi, jnp.concatenate(parts, axis=0).T * SCORE_SCALE)


def norm_back(values, gain, grad):
    scale = lax.rsqrt(jnp.mean(values * values, axis=-1, keepdims=True) + NORM_EPS)
    unit = values * scale
    inner = grad * gain
    back = scale * (inner - unit * jnp.mean(inner * unit, axis=-1, keepdims=True))
    return back, jnp.sum(grad * unit, axis=0, keepdims=True)


def backward_kernel(
    y_i, cot_i, len_i, wq_i, wo_i, wg_i, wd_i, x_i, a_i, q_i, k_i, vu_i, o_i, lse_i, h_i, b_i, g_i, u_i, m_i,
    gains, cos, sin,
    o_y, o_dx, o_qkv, o_out, o_gu, o_down, o_gain, lx_ff, lx_out, lx_qkv, lz_ff, lz_out, lz_qkv,
    w_qkv, w_out, w_ff, x_v, a_v, q_v, k_v, vu_v, o_v, lse_v, h_v, b_v, g_v, u_v, m_v,
    dmo, dao, do_v, first, s1, r1, r2, dk_a, dv_a, st_ff, st_out, st_qkv, fb_ff, fb_out, fb_qkv, g_z, g_x,
    ld, loc, a2a_s, a2a_r, hop, hsib, e1, e2, vsem, x_s, x_r, z_s, z_r, zo_r, f_s, f_r, stage, gz_s, gz_r, gx_s, gx_r,
):
    mb, block_rows, dim = o_y.shape
    me = Place(mb)
    x, c, z, n_t, nx, jz = me.x, me.c, me.z, me.n_t, me.nx, me.jz
    part = dim // nx
    quarter = part // 2
    cols, ow, half = w_qkv.shape[3], w_out.shape[0] // mb, w_ff.shape[2] // 2
    seq = x_v.shape[0]
    rows = seq // CHUNKS
    pairs = q_v.shape[0]
    slot_pairs = cols // PAIR
    first_plane, second_plane = me.section == 0, me.section == 1
    other_plane = {"section": 1 - me.section}
    me.meet()

    loads = [
        (wd_i, w_ff.at[:, 0]), (wg_i, w_ff.at[:, 1:3]), (g_i, g_v), (u_i, u_v), (h_i, h_v), (wo_i, w_out),
        (m_i, m_v), (b_i, b_v), (q_i, q_v), (k_i, k_v), (vu_i, vu_v), (o_i, o_v), (lse_i, lse_v),
        (wq_i, w_qkv), (x_i, x_v), (a_i, a_v),
    ]
    pl.when(second_plane)(pltpu.make_async_copy(cot_i, dmo, ld.at[len(loads)]).start)
    for n, (src, dst) in enumerate(loads):
        pltpu.make_async_copy(src, dst, ld.at[n]).start()

    def loaded(lo, hi):
        for n in range(lo, hi):
            pltpu.make_async_copy(*loads[n], ld.at[n]).wait()

    def block(n):
        return pl.ds(pl.multiple_of(n * block_rows, 128), block_rows)

    def give_back(t, src, dst):
        @pl.when(me.here)
        def _():
            for d in range(1, n_t):
                to = lax.rem(z + d, n_t)
                remote(src.at[block(to), :], dst.at[jz], a2a_s.at[t, d], a2a_r.at[t, jz], {"tensor": to}).start()
            pltpu.make_async_copy(src.at[block(z), :], dst.at[jz], loc.at[t]).start()

    give_back(0, y_i, o_y)

    def chunk(r):
        return pl.ds(pl.multiple_of(r * rows, 128), rows)

    def half_rows(r, core):
        return dmo.at[pl.ds(pl.multiple_of(r * rows + core * (rows // 2), 16), rows // 2), :]

    def swap(buffer, r, sems):
        return remote(s1.at[chunk(r), :], buffer.at[chunk(r), :], sems.at[0, r], sems.at[1, r], me.sibling)

    gain_one, gain_two = gains[0:1, :], gains[1:2, :]
    length = len_i[0:1, :]
    o_gain[...] = jnp.zeros_like(o_gain)
    loaded(0, 6)
    pl.when(second_plane)(pltpu.make_async_copy(cot_i, dmo, ld.at[len(loads)]).wait)

    def finish_mixed(r):
        at = chunk(r)
        swap(r1, r, e1).wait_recv()
        db = s1[at, :].astype(F32) + r1[at, :].astype(F32)
        back, gain = norm_back(h_v[at, :], gain_two, db)
        o_gain[1:2, :] += gain
        dh = dmo[at, :].astype(F32) + back
        h_v[at, :] = dh
        low = dh.astype(BF)
        dao[at, :] = low
        do_v[at, :] = dot_nt(low, w_out[...]).astype(BF)

    @pl.loop(0, CHUNKS)
    def _(r):
        at = chunk(r)

        @pl.when(first_plane)
        def _():
            mine, theirs = half_rows(r, c), half_rows(r, 1 - c)
            remote(mine, mine, hop.at[0, r], hop.at[1, r], me.sibling).wait_recv()
            remote(mine, mine, hsib.at[0, r], hsib.at[1, r], me.sibling).start()
            remote(theirs, theirs, hsib.at[0, r], hsib.at[1, r], me.sibling).wait_recv()

        @pl.when(second_plane)
        def _():
            position = (r * rows + lax.broadcasted_iota(jnp.int32, (rows, dim), 0)).astype(F32)
            dmo[at, :] = jnp.where(position < len_i[0:1, 0:1], dmo[at, :].astype(F32), 0.0).astype(BF)

        dy = dmo[at, :]
        total = None
        for j in range(mb):
            dm = dot_nt(dy, w_ff[j, 0])
            gate, up = g_v[j, at, :].astype(F32), u_v[j, at, :].astype(F32)
            sig = 1.0 / (1.0 + jnp.exp(-gate))
            d_gate = (dm * up * (sig * (1.0 + gate * (1.0 - sig)))).astype(BF)
            d_up = (dm * (gate * sig)).astype(BF)
            g_v[j, at, :] = d_gate
            u_v[j, at, :] = d_up
            term = dot(d_gate, w_ff[j, 1]) + dot(d_up, w_ff[j, 2])
            total = term if total is None else total + term
        s1[at, :] = total.astype(BF)
        swap(r1, r, e1).start()

        @pl.when(r > 0)
        def _():
            finish_mixed(r - 1)

    def ff_grads(t):
        left = (m_v, g_v, u_v)[t]
        right = (dmo, b_v, b_v)[t]

        @pl.loop(0, mb)
        def _(j):
            @pl.loop(0, 2)
            def _(n):
                lanes = pl.ds(pl.multiple_of(n * (dim // 2), 128), dim // 2)
                w_ff[j, t, :, lanes] = dot_tn(left[j], right[:, lanes]).astype(BF)

    def column(p):
        return pl.ds(pl.multiple_of(p * part, 128), part)

    def order(i):
        return jnp.where(c == 0, i, mb - 1 - i)

    def key(kind, n):
        return KEY[kind] + n

    def half_of(n):
        return pl.ds(pl.multiple_of(lax.rem(n, 2) * half, 16), half)

    def grad_part(kind, n, j, p):
        if kind == FF:
            return w_ff.at[j, n // 2, half_of(n), column(p)]
        if kind == OUTS:
            return w_out.at[pl.ds(pl.multiple_of(j * ow, 16), ow), column(p)]
        return w_qkv.at[j, :, pl.ds(pl.multiple_of(p * part + n * quarter, 16), quarter), :]

    def landing(bufs, kind, n, slot):
        if kind == FF:
            return bufs[FF].at[slot, n // 2, half_of(n), :]
        if kind == OUTS:
            return bufs[OUTS].at[slot]
        return bufs[HEADS].at[slot, :, pl.ds(n * quarter, quarter), :]

    def land_x(kind, n, j, d):
        return landing([b.at[d - 1] for b in (lx_ff, lx_out, lx_qkv)], kind, n, j)

    def land_z(kind, n, slot):
        return landing((lz_ff, lz_out, lz_qkv), kind, n, slot)

    def staged(kind, slot):
        return (st_ff, st_out, st_qkv)[kind].at[slot]

    def x_copies(kind, n, j):
        k = key(kind, n)
        for d in range(1, nx):
            to = lax.rem(x + d, nx)
            yield d, remote(
                grad_part(kind, n, j, to), land_x(kind, n, j, d), x_s.at[k, j, d], x_r.at[k, j, d], me.at_x(d)
            )

    def x_start(kind, n, i):
        for _, copy in x_copies(kind, n, order(i)):
            copy.start()

    def reduce_step(kind, n, i):
        k, j = key(kind, n), order(i)
        s = c * mb + j
        mine = grad_part(kind, n, j, x)
        outer = ((s > z) & (z > 0)) | ((s < z) & (z < n_t - 1))
        fetch = [pltpu.make_async_copy(land_x(kind, n, j, d), staged(kind, d - 1), stage.at[d - 1]) for d in range(1, nx)]
        from_z = land_z(kind, n, j)
        fetch_z = pltpu.make_async_copy(from_z, staged(kind, nx - 1), stage.at[nx - 1])
        for d, copy in x_copies(kind, n, j):
            copy.wait_recv()
            fetch[d - 1].start()

        @pl.when(outer)
        def _():
            remote(from_z, from_z, z_s.at[k, j], z_r.at[k, j], me.right).wait_recv()
            fetch_z.start()

        for copy in fetch:
            copy.wait()
        total = mine[...].astype(F32)
        for d in range(1, nx):
            total = total + staged(kind, d - 1)[...].astype(F32)
        mine[...] = total.astype(BF)

        @pl.when(outer)
        def _():
            fetch_z.wait()
            mine[...] = (mine[...].astype(F32) + staged(kind, nx - 1)[...].astype(F32)).astype(BF)

        pl.when(s > z)(remote(mine, land_z(kind, n, j), z_s.at[k, j], z_r.at[k, j], me.right).start)
        pl.when(s < z - 1)(remote(mine, land_z(kind, n, j), z_s.at[k, j], z_r.at[k, j], me.left).start)
        pl.when(s == z - 1)(remote(mine, land_z(kind, n, mb), z_s.at[k, j], zo_r.at[k], me.left).start)

    def final_part(kind, n):
        if kind == FF:
            return (o_down.at[half_of(n), :], o_gu.at[jnp.maximum(n // 2 - 1, 0), half_of(n), :]), fb_ff.at[n // 2, half_of(n), :]
        if kind == OUTS:
            return (o_out,), fb_out
        return (o_qkv,), fb_qkv

    def put_final(kind, n, value):
        targets = final_part(kind, n)[0]
        if kind == FF:
            @pl.when(n < 2)
            def _():
                targets[0][...] = value

            @pl.when(n >= 2)
            def _():
                targets[1][...] = value
        else:
            targets[0][...] = value

    def own_piece(kind, n):
        k = key(kind, n)
        mine = grad_part(kind, n, jz, x)
        fin = final_part(kind, n)[1]

        @pl.when(me.here)
        def _():
            sides = ((z > 0, land_z(kind, n, jz), z_r.at[k, jz], 0), (z < n_t - 1, land_z(kind, n, mb), zo_r.at[k], nx - 1))
            for there, src, sem, slot in sides:
                @pl.when(there)
                def _(src=src, sem=sem, slot=slot):
                    remote(src, src, f_s.at[k], sem, me.right).wait_recv()
                    pltpu.make_async_copy(src, staged(kind, slot), stage.at[slot]).start()
            for there, src, sem, slot in sides:
                @pl.when(there)
                def _(src=src, slot=slot):
                    pltpu.make_async_copy(src, staged(kind, slot), stage.at[slot]).wait()
                    mine[...] = (mine[...].astype(F32) + staged(kind, slot)[...].astype(F32)).astype(BF)
            if kind == HEADS:
                @pl.when(c == n)
                def _():
                    put_final(kind, n, mine[...].astype(F32))

                pl.when(c != n)(remote(mine, fin, f_s.at[k], f_r.at[k], me.sibling).start)
            else:
                for core in range(2):
                    @pl.when(c == core)
                    def _(core=core):
                        put_final(kind, n, mine[:, core * quarter:(core + 1) * quarter].astype(F32))
                        theirs = mine.at[:, (1 - core) * quarter:(2 - core) * quarter]
                        remote(theirs, fin, f_s.at[k], f_r.at[k], me.sibling).start()

    def ahead(index):
        if index + AHEAD < len(PIECES) * mb:
            piece, i = divmod(index + AHEAD, mb)
            x_start(*PIECES[piece], i)

    def begin_reduce():
        for index in range(AHEAD):
            x_start(FF, index // mb, index % mb)

    def ff_round(n):
        for i in range(mb):
            n_next, i_next = n + (i + AHEAD) // mb, (i + AHEAD) % mb

            @pl.when(n_next < FF_PIECES)
            def _(n_next=n_next, i_next=i_next):
                x_start(FF, n_next, i_next)
            reduce_step(FF, n, i)

        @pl.when(n >= LAG)
        def _():
            own_piece(FF, n - LAG)

    loaded(6, 8)
    pl.when(first_plane)(lambda: ff_grads(0))
    finish_mixed(CHUNKS - 1)

    @pl.when(first_plane)
    def _():
        begin_reduce()
        ff_grads(1)
        ff_grads(2)

    loaded(8, len(loads))

    def send_dv(p):
        return remote(vu_v.at[p], first.at[p], vsem.at[0, p], vsem.at[1, p], other_plane)

    @pl.loop(0, pairs)
    def _(p):
        pl.when(first_plane)(lambda: ff_round(p))
        lanes = pl.ds(pl.multiple_of(p * PAIR, PAIR), PAIR)

        def add_to(acc):
            def add(a, b, value, fresh):
                if fresh:
                    acc[a:b, :] = value
                else:
                    acc[a:b, :] += value
            return add

        def put_dq(lo, hi, dq):
            q_v[p, lo:hi, :] = rotate_pair(dq, cos[lo:hi, :], -sin[lo:hi, :]).astype(BF)

        attend_back(
            q_v[p], k_v[p], vu_v[p], o_v[:, lanes], do_v[:, lanes], lambda h, lo, hi: lse_v[p, h:h + 1, lo:hi],
            length, add_to(dv_a), add_to(dk_a), put_dq,
        )
        k_v[p] = rotate_pair(dk_a[...], cos[...], -sin[...]).astype(BF)

        @pl.when(first_plane)
        def _():
            send_dv(p).wait_recv()
            vu_v[p] = (dv_a[...] + first[p].astype(F32)).astype(BF)

        @pl.when(second_plane)
        def _():
            vu_v[p] = (0.5 * dv_a[...]).astype(BF)
            send_dv(p).start()

    def slot_rows(t, j, at):
        source = (q_v, k_v, vu_v)[t]
        return jnp.concatenate([source[j * slot_pairs + n, at, :] for n in range(slot_pairs)], axis=1)

    def finish_input(r):
        at = chunk(r)
        swap(r2, r, e2).wait_recv()
        da = s1[at, :].astype(F32) + r2[at, :].astype(F32)
        back, gain = norm_back(x_v[at, :].astype(F32), gain_one, da)
        o_gain[0:1, :] += gain
        r2[at, :] = (h_v[at, :] + back).astype(BF)

        @pl.when(second_plane)
        def _():
            mine = pl.ds(pl.multiple_of(r * rows + c * (rows // 2), 16), rows // 2)
            remote(r2.at[mine, :], dmo.at[mine, :], hop.at[0, r], hop.at[1, r], other_plane).start()

    @pl.loop(0, CHUNKS)
    def _(r):
        at = chunk(r)
        total = None
        for j in range(mb):
            for t in range(3):
                term = dot_nt(slot_rows(t, j, at), w_qkv[j, t])
                total = term if total is None else total + term
        swap(r1, r, e1).wait_send()
        s1[at, :] = total.astype(BF)
        swap(r2, r, e2).start()

        @pl.when(r > 0)
        def _():
            finish_input(r - 1)

    finish_input(CHUNKS - 1)
    give_back(1, r2, o_dx)
    for d in range(1, n_t):
        remote(o_gain, g_z.at[d], gz_s.at[d], gz_r.at[d], {"tensor": lax.rem(z + d, n_t)}).start()

    @pl.when(second_plane)
    def _():
        for t in range(3):
            ff_grads(t)
        begin_reduce()

    @pl.loop(0, 2)
    def _(n):
        lanes = pl.ds(pl.multiple_of(n * (dim // 2), 128), dim // 2)
        w_out[:, lanes] = dot_tn(o_v[...], dao[:, lanes]).astype(BF)

    everything = pl.ds(0, seq)

    @pl.loop(0, mb)
    def _(j):
        for t in range(3):
            w_qkv[j, t] = dot_tn(a_v[...], slot_rows(t, j, everything)).astype(BF)

    @pl.when(second_plane)
    def _():
        @pl.loop(0, pairs)
        def _(p):
            ff_round(p)

    for piece in range(pairs, len(PIECES)):
        kind, n = PIECES[piece]
        for i in range(mb):
            ahead(piece * mb + i)
            reduce_step(kind, n, i)
        own_piece(*PIECES[piece - LAG])
    for piece in range(len(PIECES) - LAG, len(PIECES)):
        own_piece(*PIECES[piece])

    for d in range(1, n_t):
        remote(o_gain, g_z.at[d], gz_s.at[d], gz_r.at[d], me.right).wait()
    g_z[0] = o_gain[...]
    for d in range(1, n_t):
        g_z[0] += g_z[d]
    for d in range(1, nx):
        remote(g_z.at[0], g_x.at[d], gx_s.at[d], gx_r.at[d], me.at_x(d)).start()
    for d in range(1, nx):
        remote(g_z.at[0], g_x.at[d], gx_s.at[d], gx_r.at[d], me.at_x(d)).wait()
    o_gain[...] = g_z[0]
    for d in range(1, nx):
        o_gain[...] += g_x[d]

    @pl.when(jnp.logical_not(me.here))
    def _():
        for kind, n in PIECES:
            k, fin = key(kind, n), final_part(kind, n)[1]

            def take(kind=kind, n=n, k=k, fin=fin):
                remote(fin, fin, f_s.at[k], f_r.at[k], me.sibling).wait_recv()
                put_final(kind, n, fin[...].astype(F32))

            if kind == HEADS:
                pl.when(c == n)(take)
            else:
                take()

    for kind, n in PIECES:
        k = key(kind, n)
        for j in range(mb):
            for _, copy in x_copies(kind, n, j):
                copy.wait_send()
            mine = grad_part(kind, n, j, x)
            pl.when(c * mb + j != z)(remote(mine, mine, z_s.at[k, j], z_r.at[k, j], me.right).wait_send)

    @pl.when(me.here)
    def _():
        for kind, n in PIECES:
            k, fin = key(kind, n), final_part(kind, n)[1]
            sent = remote(fin, fin, f_s.at[k], f_r.at[k], me.sibling)
            if kind == HEADS:
                pl.when(c != n)(sent.wait_send)
            else:
                sent.wait_send()
        for t, (src, dst) in enumerate(((y_i, o_y), (r2, o_dx))):
            for d in range(1, n_t):
                there = src.at[block(0), :]
                remote(there, dst.at[0], a2a_s.at[t, d], a2a_r.at[t, jz], me.right).wait_send()
            pltpu.make_async_copy(src.at[block(z), :], dst.at[jz], loc.at[t]).wait()

    for t, dst in enumerate((o_y, o_dx)):
        for i in range(mb):
            @pl.when(c * mb + i != z)
            def _(t=t, i=i, dst=dst):
                remote(dst.at[i], dst.at[i], a2a_s.at[t, 0], a2a_r.at[t, i], me.right).wait_recv()

    for p in range(pairs):
        pl.when(second_plane)(send_dv(p).wait_send)
    for r in range(CHUNKS):
        swap(r2, r, e2).wait_send()
        mine = half_rows(r, c)
        pl.when(second_plane)(remote(mine, mine, hop.at[0, r], hop.at[1, r], me.sibling).wait_send)
        pl.when(first_plane)(remote(mine, mine, hsib.at[0, r], hsib.at[1, r], me.sibling).wait_send)


def backward(y, cot, length, weights, kept, gains, tables, mb):
    w_qkv, w_out, w_gu, w_down = weights
    n_t = lax.axis_size("tensor")
    n_dp = lax.axis_size("dp")
    nx = n_dp // 2
    seq, dim = y.shape
    part, quarter = dim // nx, dim // n_dp
    cols, ow, ff = w_qkv.shape[3], w_out.shape[0] // mb, w_down.shape[1]
    pairs = mb * cols // PAIR
    dma = pltpu.SemaphoreType.DMA
    wide, heads, hidden = (seq, dim), (pairs, seq, PAIR), (mb, seq, ff)
    block = (mb, seq // n_t, dim)
    shape = lambda s, t=BF: jax.ShapeDtypeStruct(s, t)
    n_k = len(PIECES)
    ins = (y, cot, length, *weights, *kept, gains, *tables)
    vmem_in = {2, len(ins) - 3, len(ins) - 2, len(ins) - 1}

    def parts(lead, split):
        return (*lead, 3, ff, split), (*lead, ow, split), (*lead, 3, split, cols)

    return pl.pallas_call(
        backward_kernel,
        out_shape=(
            shape(block), shape(block),
            shape((3, quarter, cols), F32), shape((ow, quarter), F32), shape((2, ff, quarter), F32),
            shape((ff, quarter), F32), shape((2, dim), F32),
            *(shape(s) for s in parts((nx - 1, mb), part)),
            *(shape(s) for s in parts((mb + 1,), part)),
        ),
        in_specs=[VMEM if n in vmem_in else ANY for n in range(len(ins))],
        out_specs=(ANY, ANY, *(VMEM,) * 5, *(ANY,) * 6),
        scratch_shapes=[
            pltpu.VMEM(w_qkv.shape, BF), pltpu.VMEM(w_out.shape, BF), pltpu.VMEM((mb, 3, ff, dim), BF),
            pltpu.VMEM(wide, BF), pltpu.VMEM(wide, BF), *[pltpu.VMEM(heads, BF)] * 3,
            pltpu.VMEM((seq, pairs * PAIR), BF), pltpu.VMEM((pairs, 2, seq), F32),
            pltpu.VMEM(wide, F32), pltpu.VMEM(wide, BF), *[pltpu.VMEM(hidden, BF)] * 3,
            pltpu.VMEM(wide, BF), pltpu.VMEM(wide, BF), pltpu.VMEM((seq, pairs * PAIR), BF), pltpu.VMEM(heads, BF),
            *[pltpu.VMEM(wide, BF)] * 3, *[pltpu.VMEM((seq, PAIR), F32)] * 2,
            pltpu.VMEM((nx, ff // 2, part), BF), pltpu.VMEM((nx, ow, part), BF), pltpu.VMEM((nx, 3, quarter, cols), BF),
            *(pltpu.VMEM(s, BF) for s in parts((), quarter)),
            pltpu.VMEM((n_t, 2, dim), F32), pltpu.VMEM((nx, 2, dim), F32),
            dma((17,)), dma((2,)), dma((2, n_t)), dma((2, mb)),
            dma((2, CHUNKS)), dma((2, CHUNKS)), dma((2, CHUNKS)), dma((2, CHUNKS)), dma((2, pairs)),
            dma((n_k, mb, nx)), dma((n_k, mb, nx)), dma((n_k, mb)), dma((n_k, mb)), dma((n_k,)), dma((n_k,)), dma((n_k,)),
            dma((nx,)), dma((n_t,)), dma((n_t,)), dma((nx,)), dma((nx,)),
        ],
        compiler_params=pltpu.CompilerParams(
            collective_id=1, has_side_effects=True, vmem_limit_bytes=63 << 20
        ),
        name="backward_layer",
    )(*ins)


def shards(tokens, lengths, qkv_weight, out_weight, gate_up_weight, down_weight, norm_gains, cotangent):
    dp, z = lax.axis_index("dp"), lax.axis_index("tensor")
    mb, rows, dim = tokens.shape
    n_t = lax.axis_size("tensor")
    tables = tuple(jnp.asarray(t) for t in rope_tables(rows * n_t))
    lens = jnp.broadcast_to(lengths.astype(F32)[:, None, None], (mb, 8, 128))
    (
        x, cot, y, w_qkv, w_out, w_gu, w_down, a, q, k, vu, o, lse, h, b, gates, ups, ms, length,
    ) = forward(
        tokens, cotangent, lens, qkv_weight, out_weight, jnp.swapaxes(gate_up_weight, 2, 3), down_weight,
        norm_gains[0], tables,
    )
    o_y, o_dx, o_qkv, o_out, o_gu, o_down, gain = backward(
        y, cot, length, (w_qkv, w_out, w_gu, w_down), (x, a, q, k, vu, o, lse, h, b, gates, ups, ms),
        norm_gains[0], tables, mb,
    )[:7]
    share = dim // (lax.axis_size("dp") * n_t)
    gain = lax.dynamic_slice_in_dim(gain, (dp * n_t + z) * share, share, 1)
    return (
        o_y[None], o_dx.astype(F32)[None], o_qkv[None], o_out[None], jnp.swapaxes(o_gu, 1, 2)[None], o_down[None],
        gain[None],
    )


def solution(mesh):
    in_specs = (
        P("dp", "tensor", None),
        P("dp"),
        P("section", None, None, "tensor"),
        P("section", "tensor", None),
        P("section", None, None, "tensor"),
        P("section", "tensor", None),
        P("section", None, None),
        P("dp", "tensor", None),
    )
    out_specs = (
        P("section", "dp", "tensor", None),
        P("section", "dp", "tensor", None),
        P("section", None, "dp", "tensor"),
        P("section", "tensor", "dp"),
        P("section", None, "dp", "tensor"),
        P("section", "tensor", "dp"),
        P("section", None, ("dp", "tensor")),
    )
    return jax.shard_map(shards, mesh=mesh, in_specs=in_specs, out_specs=out_specs, check_vma=False)
```

```python
import jax
import jax.numpy as jnp
import numpy as np
from jax import lax
from jax.experimental import pallas as pl
from jax.experimental.pallas import tpu as pltpu
from jax.sharding import PartitionSpec as P

MESH = pl.DeviceIdType.MESH
ANY = pl.BlockSpec(memory_space=pl.ANY)
VMEM = pl.BlockSpec(memory_space=pltpu.VMEM)
NORM_EPS = 1e-6
ROPE_BASE = 10000.0
SCORE_SCALE = 0.125
MASK_VALUE = -1e30
HD = 64
PAIR = 2 * HD
CHUNKS = 4
NT = (((1,), (1,)), ((), ()))
BF, F32 = jnp.bfloat16, jnp.float32

QKV, OUT, GU, DOWN = range(4)
COUNT = (2, 1, 4, 2)
BASE = (0, 2, 3, 7)
N_PIECES = 9


def dot(a, b):
    return jnp.dot(a, b, preferred_element_type=F32)


def dot_nt(a, b):
    return lax.dot_general(a, b, NT, preferred_element_type=F32)


def dot_tn(a, b):
    return lax.dot_general(a, b, (((0,), (0,)), ((), ())), preferred_element_type=F32)


def remote(src, dst, send, recv, to):
    return pltpu.make_async_remote_copy(
        src_ref=src, dst_ref=dst, send_sem=send, recv_sem=recv, device_id=to, device_id_type=MESH
    )


class Place:
    def __init__(self, mb):
        self.n_t = lax.axis_size("tensor")
        self.nx = lax.axis_size("dp") // 2
        self.section = lax.axis_index("section")
        dp = lax.axis_index("dp")
        self.z = lax.axis_index("tensor")
        self.x, self.c = dp // 2, lax.rem(dp, 2)
        self.here = self.z // mb == self.c
        self.jz = self.z - self.c * mb
        self.sibling = {"dp": 2 * self.x + 1 - self.c}
        self.right, self.left = {"tensor": self.z + 1}, {"tensor": self.z - 1}

    def at_x(self, d):
        return {"dp": 2 * lax.rem(self.x + d, self.nx) + self.c}

    def meet(self):
        barrier = pltpu.get_barrier_semaphore()
        partners = [{"tensor": lax.rem(self.z + k, self.n_t)} for k in range(1, self.n_t)]
        partners += [self.at_x(k) for k in range(1, self.nx)]
        partners += [self.sibling, {"section": 1 - self.section}]
        for partner in partners:
            pl.semaphore_signal(barrier, inc=1, device_id=partner, device_id_type=MESH)
        pl.semaphore_wait(barrier, len(partners))


def rope_tables(positions):
    lane = np.arange(PAIR)
    frequency = ROPE_BASE ** (-(lane % (HD // 2)) * 2.0 / HD)
    angles = np.arange(positions)[:, None] * frequency[None, :]
    sign = np.where(lane % HD < HD // 2, -1.0, 1.0)
    return np.cos(angles).astype(np.float32), (np.sin(angles) * sign).astype(np.float32)


def rotate_pair(values, cos, sin):
    lane = lax.broadcasted_iota(jnp.int32, values.shape, 1)
    partner = jnp.where(
        lax.rem(lane, HD) < HD // 2,
        pltpu.roll(values, PAIR - HD // 2, 1),
        pltpu.roll(values, HD // 2, 1),
    )
    return values * cos + partner * sin


def normalise(values):
    return values * lax.rsqrt(jnp.mean(values * values, axis=-1, keepdims=True) + NORM_EPS)


def head_views(h, shape):
    lane = lax.broadcasted_iota(jnp.int32, shape, 1)
    return lane // HD == h, lane == (1 - h) * HD


def causal_block(blk):
    key = lax.broadcasted_iota(jnp.int32, (blk, blk), 0)
    query = lax.broadcasted_iota(jnp.int32, (blk, blk), 1)
    return key <= query


def head_keys(keys, length, first_row):
    position = (first_row + lax.broadcasted_iota(jnp.int32, keys.shape, 0)).astype(F32)
    bias = jnp.where(position < length, 0.0, MASK_VALUE)
    views = []
    for h in range(2):
        inside, extra = head_views(h, keys.shape)
        views.append(jnp.where(inside, keys, jnp.where(extra, bias, 0.0)).astype(BF))
    return views


def head_queries(h, queries, mark):
    inside, extra = head_views(h, queries.shape)
    return jnp.where(inside, queries, jnp.where(extra, mark, 0.0)).astype(BF)


def attend_block(i, blk, queries, keys, vals_t, put_out, put_lse):
    lo, hi = i * blk, (i + 1) * blk
    visible = causal_block(blk)
    queries = queries.astype(F32)
    parts = []
    for h in range(2):
        qi = head_queries(h, queries, 1.0)
        vh = slice(h * HD, (h + 1) * HD)
        s_diag = jnp.where(visible, dot_nt(keys(h, lo, hi), qi), MASK_VALUE)
        top = jnp.max(s_diag, axis=0, keepdims=True)
        if i:
            s_full = dot_nt(keys(h, 0, lo), qi)
            top = jnp.maximum(top, jnp.max(s_full, axis=0, keepdims=True))
        p_diag = jnp.exp(s_diag - top)
        total = jnp.sum(p_diag, axis=0, keepdims=True)
        acc = dot(vals_t(vh, lo, hi), p_diag.astype(BF))
        if i:
            p_full = jnp.exp(s_full - top)
            total = total + jnp.sum(p_full, axis=0, keepdims=True)
            acc = acc + dot(vals_t(vh, 0, lo), p_full.astype(BF))
        parts.append(acc / total)
        put_lse(h, lo, hi, top + jnp.log(total))
    put_out(lo, hi, jnp.concatenate(parts, axis=0).T.astype(BF))


def forward_part(
    me, tok, cot, lens, qkv, out, gu, down, gains, cos, sin, tok_o,
    w_qkv, w_out, w_ff, x_v, first, q_v, ka_v, kb_v, vt_v, v_v, vu_v, o_v, lse_v, h_v, b_v, g_v, u_v, m_v,
    s1, r1, r2, dmo, len_v,
    loc, a2a_s, a2a_r, c2a_s, c2a_r, y_s, y_r, sib, own_r, own_l, z_r, z_f, x_s, x_r, hop, hsib, e1, e2, vsem, lsem,
):
    mb, block_rows, dim = tok.shape
    x, c, z, n_t, nx, jz = me.x, me.c, me.z, me.n_t, me.nx, me.jz
    part = dim // nx
    cols, ow, half = qkv.shape[3], out.shape[1], down.shape[1] // 2
    seq = x_v.shape[0]
    rows = seq // CHUNKS
    pairs = q_v.shape[0]
    first_plane, second_plane = me.section == 0, me.section == 1

    def column(p):
        return pl.ds(pl.multiple_of(p * part, 128), part)

    def shard_part(w, n, p):
        if w == QKV:
            return qkv.at[0, :, pl.ds(pl.multiple_of(p * part + n * (part // 2), 16), part // 2), :]
        if w == OUT:
            return out.at[0, :, column(p)]
        if w == GU:
            return gu.at[0, n // 2, pl.ds(pl.multiple_of(lax.rem(n, 2) * half, 16), half), column(p)]
        return down.at[0, pl.ds(n * half, half), column(p)]

    def slot_part(w, n, j, p):
        if w == QKV:
            return w_qkv.at[j, :, pl.ds(pl.multiple_of(p * part + n * (part // 2), 16), part // 2), :]
        if w == OUT:
            return w_out.at[pl.ds(pl.multiple_of(j * ow, 16), ow), column(p)]
        if w == GU:
            return w_ff.at[j, 1 + n // 2, pl.ds(pl.multiple_of(lax.rem(n, 2) * half, 16), half), column(p)]
        return w_ff.at[j, 0, pl.ds(n * half, half), column(p)]

    own_slots = (
        (qkv.at[0], w_qkv.at[jz]),
        (out.at[0], w_out.at[pl.ds(pl.multiple_of(jz * ow, 16), ow), :]),
        (gu.at[0], w_ff.at[jz, 1:3]),
        (down.at[0], w_ff.at[jz, 0]),
    )

    def own_copies(w, n):
        k = BASE[w] + n
        src, dst = shard_part(w, n, x), slot_part(w, n, jz, x)
        return (
            (z < n_t - 1, remote(src, dst, own_r.at[k], z_r.at[k, jz], me.right)),
            (z > 0, remote(src, dst, own_l.at[k], z_r.at[k, jz], me.left)),
        )

    def own_start(w, n):
        @pl.when(me.here)
        def _():
            for there, copy in own_copies(w, n):
                pl.when(there)(copy.start)

    def own_wait(w, n):
        @pl.when(me.here)
        def _():
            for there, copy in own_copies(w, n):
                pl.when(there)(copy.wait_send)

    def order(i):
        return jnp.where(c == 0, mb - 1 - i, i)

    def foreign(w, n, i):
        j = order(i)
        s = c * mb + j
        k = BASE[w] + n

        @pl.when(s != z)
        def _():
            piece = slot_part(w, n, j, x)
            to_right = remote(piece, piece, z_f.at[k, j], z_r.at[k, j], me.right)
            to_left = remote(piece, piece, z_f.at[k, j], z_r.at[k, j], me.left)
            to_right.wait_recv()
            pl.when((s < z) & (z < n_t - 1))(to_right.start)
            pl.when((s > z) & (z > 0))(to_left.start)
            for d in range(1, nx):
                remote(piece, piece, x_s.at[k, j, d], x_r.at[k, j, x], me.at_x(d)).start()

    def wait_slot(w, j):
        s = c * mb + j

        @pl.when(s != z)
        def _():
            for n in range(COUNT[w]):
                k = BASE[w] + n
                for d in range(1, nx):
                    p = lax.rem(x + d, nx)
                    piece = slot_part(w, n, j, p)
                    remote(piece, piece, x_s.at[k, j, d], x_r.at[k, j, p], me.right).wait_recv()

    def gu_step(n, i):
        if i == 0:
            @pl.when(n >= 2)
            def _():
                own_wait(GU, n - 2)
            own_start(GU, n)
        foreign(GU, n, i)

    def down_steps(i):
        for n in range(COUNT[DOWN]):
            if i == 0:
                own_wait(GU, n + 2)
                own_start(DOWN, n)
            foreign(DOWN, n, i)

    def block_at(n):
        return pl.ds(pl.multiple_of(n * block_rows, 128), block_rows)

    block = block_at(z)
    other_plane = {"section": 1 - me.section}

    def spread(source, target, send, recv):
        for i in range(mb):
            zt = c * mb + i

            @pl.when(zt != z)
            def _(i=i, zt=zt):
                remote(source.at[i], target.at[block, :], send.at[i], recv.at[z], {"tensor": zt}).start()

    def arrived(target, zs, recv):
        there = target.at[block_at(zs), :]
        return remote(there, there, recv.at[zs], recv.at[zs], me.right)

    def to_first(zs):
        return remote(tok_o.at[block_at(zs), :], x_v.at[block_at(zs), :], y_s.at[zs], y_r.at[zs], other_plane)

    pl.when(second_plane)(lambda: spread(tok, tok_o, a2a_s, a2a_r))
    for i in range(mb):
        @pl.when(first_plane & (c * mb + i == z))
        def _(i=i):
            pltpu.make_async_copy(tok.at[i], x_v.at[block, :], loc.at[4]).start()

    @pl.when(me.here)
    def _():
        remote(lens.at[jz], len_v, lsem.at[0], lsem.at[1], me.sibling).start()
        len_v[...] = lens[jz]
        for w, (src, dst) in enumerate(own_slots):
            pltpu.make_async_copy(src, dst, loc.at[w]).start()

    own_start(QKV, 0)
    own_start(QKV, 1)
    for w, n in ((QKV, 0), (QKV, 1), (OUT, 0)):
        if w == OUT:
            own_wait(QKV, 0)
            own_start(OUT, 0)
        for i in range(mb):
            foreign(w, n, i)
        if (w, n) == (QKV, 1):
            @pl.when(second_plane & me.here)
            def _():
                for zs in range(n_t):
                    @pl.when(zs != z)
                    def _(zs=zs):
                        arrived(tok_o, zs, a2a_r).wait_recv()
                        to_first(zs).start()

    def ff_steps(i):
        @pl.loop(0, COUNT[GU])
        def _(n):
            gu_step(n, i)
        down_steps(i)

    for i in range(mb - 1):
        ff_steps(i)
    @pl.when(second_plane)
    def _():
        ff_steps(mb - 1)
        spread(cot, dmo, c2a_s, c2a_r)
        for i in range(mb):
            @pl.when(c * mb + i == z)
            def _(i=i):
                pltpu.make_async_copy(cot.at[i], dmo.at[block, :], loc.at[4]).start()

    @pl.when(first_plane & me.here)
    def _():
        for zs in range(n_t):
            @pl.when(zs != z)
            def _(zs=zs):
                to_first(zs).wait_recv()
        pltpu.make_async_copy(tok.at[0], x_v.at[block, :], loc.at[4]).wait()
        remote(x_v, x_v, sib.at[0], sib.at[1], me.sibling).start()

    @pl.when(jnp.logical_not(me.here))
    def _():
        remote(len_v, len_v, lsem.at[0], lsem.at[1], me.sibling).wait_recv()
        pl.when(first_plane)(remote(x_v, x_v, sib.at[0], sib.at[1], me.sibling).wait_recv)

    length = len_v[0:1, :]

    @pl.when(me.here)
    def _():
        for w, (src, dst) in enumerate(own_slots):
            pltpu.make_async_copy(src, dst, loc.at[w]).wait()

    for j in range(mb):
        wait_slot(QKV, j)
        wait_slot(OUT, j)

    gain_one, gain_two = gains[0:1, :], gains[1:2, :]

    def chunk(r):
        return pl.ds(pl.multiple_of(r * rows, 128), rows)

    def halves(r, core):
        return x_v.at[pl.ds(pl.multiple_of(r * rows + core * (rows // 2), 16), rows // 2), :]

    def send_v(r):
        return remote(v_v.at[:, chunk(r), :], first.at[:, chunk(r), :], vsem.at[0, r], vsem.at[1, r], other_plane)

    def swap(buffer, r, sems):
        return remote(s1.at[chunk(r), :], buffer.at[chunk(r), :], sems.at[0, r], sems.at[1, r], me.sibling)

    def project(r):
        at = chunk(r)
        a = (normalise(x_v[at, :].astype(F32)) * gain_one).astype(BF)
        cos_r, sin_r = cos[at, :], sin[at, :]
        for j in range(mb):
            q = dot(a, w_qkv[j, 0])
            k = dot(a, w_qkv[j, 1])
            v = dot(a, w_qkv[j, 2])
            for n in range(cols // PAIR):
                p = j * (cols // PAIR) + n
                lanes = slice(n * PAIR, (n + 1) * PAIR)
                q_v[p, at, :] = (rotate_pair(q[:, lanes], cos_r, sin_r) * SCORE_SCALE).astype(BF)
                keys = rotate_pair(k[:, lanes], cos_r, sin_r).astype(BF).astype(F32)
                ka_v[p, at, :], kb_v[p, at, :] = head_keys(keys, length, r * rows)
                v_v[p, at, :] = v[:, lanes].astype(BF)

        @pl.when(first_plane)
        def _():
            send_v(r).start()
            for p in range(pairs):
                vals = v_v[p, at, :]
                vu_v[p, at, :] = vals
                vt_v[p, :, at] = vals.astype(F32).T.astype(BF)

        @pl.when(second_plane)
        def _():
            send_v(r).wait_recv()
            for p in range(pairs):
                vals = (0.5 * v_v[p, at, :].astype(F32) + 0.5 * first[p, at, :].astype(F32)).astype(BF)
                vu_v[p, at, :] = vals
                vt_v[p, :, at] = vals.astype(F32).T.astype(BF)

    def attention(r):
        for i in range(CHUNKS):
            @pl.when(r == i)
            def _(i=i):
                @pl.loop(0, pairs, unroll=2)
                def _(p):
                    lanes = pl.ds(pl.multiple_of(p * PAIR, PAIR), PAIR)

                    def put_out(lo, hi, value):
                        o_v[lo:hi, lanes] = value

                    def put_lse(h, lo, hi, value):
                        lse_v[p, h:h + 1, lo:hi] = value

                    attend_block(
                        i, rows, q_v[p, i * rows:(i + 1) * rows, :],
                        lambda h, lo, hi: (ka_v, kb_v)[h][p, lo:hi, :],
                        lambda vh, lo, hi: vt_v[p, vh, lo:hi],
                        put_out, put_lse,
                    )

    def mix(r):
        at = chunk(r)
        swap(r1, r, e1).wait_recv()
        h = x_v[at, :].astype(F32) + s1[at, :].astype(F32) + r1[at, :].astype(F32)
        h_v[at, :] = h
        b = (normalise(h) * gain_two).astype(BF)
        b_v[at, :] = b
        grown = None
        for j in range(mb):
            gate = dot_nt(b, w_ff[j, 1])
            up = dot_nt(b, w_ff[j, 2])
            m = (gate / (1.0 + jnp.exp(-gate)) * up).astype(BF)
            g_v[j, at, :] = gate.astype(BF)
            u_v[j, at, :] = up.astype(BF)
            m_v[j, at, :] = m
            term = dot(m, w_ff[j, 0])
            grown = term if grown is None else grown + term
        swap(r1, r, e1).wait_send()
        s1[at, :] = grown.astype(BF)
        swap(r2, r, e2).start()

    def finish(r):
        at = chunk(r)
        swap(r2, r, e2).wait_recv()
        r2[at, :] = (h_v[at, :] + s1[at, :].astype(F32) + r2[at, :].astype(F32)).astype(BF)

        @pl.when(first_plane)
        def _():
            mine = pl.ds(pl.multiple_of(r * rows + c * (rows // 2), 16), rows // 2)
            remote(
                r2.at[mine, :], x_v.at[mine, :], hop.at[0, r], hop.at[1, r], other_plane
            ).start()

    def mix_all(r):
        mix(r)

        @pl.when(r > 0)
        def _():
            finish(r - 1)

    @pl.when(second_plane)
    def _():
        for j in range(mb):
            wait_slot(GU, j)
            wait_slot(DOWN, j)

    @pl.loop(0, CHUNKS)
    def _(r):
        @pl.when(first_plane)
        def _():
            gu_step(r, mb - 1)

        @pl.when(second_plane)
        def _():
            mine, theirs = halves(r, c), halves(r, 1 - c)
            remote(mine, mine, hop.at[0, r], hop.at[1, r], me.sibling).wait_recv()
            remote(mine, mine, hsib.at[0, r], hsib.at[1, r], me.sibling).start()
            remote(theirs, theirs, hsib.at[0, r], hsib.at[1, r], me.sibling).wait_recv()

        project(r)
        attention(r)
        s1[chunk(r), :] = dot(o_v[chunk(r), :], w_out[...]).astype(BF)
        swap(r1, r, e1).start()

        @pl.when(second_plane & (r > 0))
        def _():
            mix_all(r - 1)

    pl.when(second_plane)(lambda: mix_all(CHUNKS - 1))
    @pl.when(second_plane & me.here)
    def _():
        for zs in range(n_t):
            @pl.when(zs != z)
            def _(zs=zs):
                arrived(dmo, zs, c2a_r).wait_recv()
        pltpu.make_async_copy(cot.at[0], dmo.at[block, :], loc.at[4]).wait()
        remote(dmo, dmo, sib.at[0], sib.at[1], me.sibling).start()

    @pl.when(first_plane)
    def _():
        down_steps(mb - 1)
        for j in range(mb):
            wait_slot(GU, j)
            wait_slot(DOWN, j)

        pl.loop(0, CHUNKS)(mix_all)

    finish(CHUNKS - 1)
    for w, n in ((QKV, 1), (OUT, 0), (DOWN, 0), (DOWN, 1)):
        own_wait(w, n)
    for w in range(4):
        for n in range(COUNT[w]):
            k = BASE[w] + n
            for j in range(mb):
                s = c * mb + j

                @pl.when(s != z)
                def _(w=w, n=n, k=k, j=j, s=s):
                    piece = slot_part(w, n, j, x)
                    for d in range(1, nx):
                        remote(piece, piece, x_s.at[k, j, d], x_r.at[k, j, x], me.right).wait_send()
                    forwarded = ((s < z) & (z < n_t - 1)) | ((s > z) & (z > 0))
                    pl.when(forwarded)(remote(piece, piece, z_f.at[k, j], z_r.at[k, j], me.right).wait_send)

    @pl.when(second_plane)
    def _():
        for i in range(mb):
            @pl.when(c * mb + i != z)
            def _(i=i):
                remote(tok.at[i], tok.at[i], a2a_s.at[i], a2a_r.at[z], me.right).wait_send()
                remote(tok.at[i], tok.at[i], c2a_s.at[i], c2a_r.at[z], me.right).wait_send()

        @pl.when(me.here)
        def _():
            for zs in range(n_t):
                @pl.when(zs != z)
                def _(zs=zs):
                    to_first(zs).wait_send()

    @pl.when(me.here)
    def _():
        remote(lens.at[jz], len_v, lsem.at[0], lsem.at[1], me.sibling).wait_send()
        pl.when(first_plane)(remote(x_v, x_v, sib.at[0], sib.at[1], me.sibling).wait_send)
        pl.when(second_plane)(remote(dmo, dmo, sib.at[0], sib.at[1], me.sibling).wait_send)

    @pl.when(second_plane & jnp.logical_not(me.here))
    def _():
        remote(dmo, dmo, sib.at[0], sib.at[1], me.sibling).wait_recv()

    for r in range(CHUNKS):
        swap(r2, r, e2).wait_send()
        pl.when(first_plane)(send_v(r).wait_send)
        mine = halves(r, c)
        pl.when(first_plane)(remote(mine, mine, hop.at[0, r], hop.at[1, r], me.sibling).wait_send)
        pl.when(second_plane)(remote(mine, mine, hsib.at[0, r], hsib.at[1, r], me.sibling).wait_send)


LAG = 2
AHEAD = 3
FF, OUTS, HEADS = range(3)
FF_PIECES = 6
PIECES = [(FF, n) for n in range(FF_PIECES)] + [(OUTS, 0), (HEADS, 0), (HEADS, 1)]
KEY = (0, FF_PIECES, FF_PIECES + 1)


def attend_back_block(i, blk, queries, keys, keys_t, vals, outs, grads, stats, add_dv, add_dk):
    lo, hi = i * blk, (i + 1) * blk
    visible = causal_block(blk)
    queries, grads = queries.astype(F32), grads.astype(F32)
    product = (grads * outs.astype(F32)).T
    parts = []
    for h in range(2):
        qh, qz, gh = head_queries(h, queries, 1.0), head_queries(h, queries, 0.0), head_queries(h, grads, 0.0)
        rows_h = slice(h * HD, (h + 1) * HD)
        delta = jnp.sum(product[rows_h], axis=0, keepdims=True)
        stat = stats(h, lo, hi)

        def side(a, b, diagonal):
            p = jnp.exp(dot_nt(keys(h, a, b), qh) - stat)
            if diagonal:
                p = jnp.where(visible, p, 0.0)
            ds = (p * (dot_nt(vals(a, b), gh) - delta)).astype(BF)
            fresh = i == CHUNKS - 1 and h == 0
            add_dv(a, b, dot(p.astype(BF), gh), fresh)
            add_dk(a, b, dot(ds, qz), fresh)
            return dot(keys_t(rows_h, a, b), ds)

        dq_t = side(lo, hi, True)
        if i:
            dq_t = dq_t + side(0, lo, False)
        parts.append(dq_t)
    return jnp.concatenate(parts, axis=0).T * SCORE_SCALE


def norm_back(values, gain, grad):
    scale = lax.rsqrt(jnp.mean(values * values, axis=-1, keepdims=True) + NORM_EPS)
    unit = values * scale
    inner = grad * gain
    back = scale * (inner - unit * jnp.mean(inner * unit, axis=-1, keepdims=True))
    return back, jnp.sum(grad * unit, axis=0, keepdims=True)


def backward_part(
    me, gains, cos, sin, o_y, o_dx, o_qkv, o_out, o_gu, o_down, o_gain, lx_ff, lx_out, lx_qkv, lz_ff, lz_out, lz_qkv,
    w_qkv, w_out, w_ff, x_v, q_v, ka_v, kb_v, kt_v, vu_v, o_v, lse_v, h_v, b_v, g_v, u_v, m_v,
    dmo, do_v, first, s1, r1, r2, len_v, dk_a, dv_a, st_ff, st_out, st_qkv, g_z, g_x,
    loc, a2a_s, a2a_r, hop, hsib, e1, e2, vsem, x_s, x_r, z_s, z_r, zo_r, f_s, f_r, f_l, stage, gz_s, gz_r, gx_s, gx_r,
    free,
):
    mb, block_rows, dim = o_y.shape
    x, c, z, n_t, nx, jz = me.x, me.c, me.z, me.n_t, me.nx, me.jz
    part = dim // nx
    quarter = part // 2
    cols, ow, half = w_qkv.shape[3], w_out.shape[0] // mb, w_ff.shape[2] // 2
    seq = x_v.shape[0]
    rows = seq // CHUNKS
    pairs = q_v.shape[0]
    slot_pairs = cols // PAIR
    first_plane, second_plane = me.section == 0, me.section == 1
    other_plane = {"section": 1 - me.section}

    def block(n):
        return pl.ds(pl.multiple_of(n * block_rows, 128), block_rows)

    def give_back(t, src, dst):
        @pl.when(me.here)
        def _():
            for d in range(1, n_t):
                to = lax.rem(z + d, n_t)
                remote(src.at[block(to), :], dst.at[jz], a2a_s.at[t, d], a2a_r.at[t, jz], {"tensor": to}).start()
            pltpu.make_async_copy(src.at[block(z), :], dst.at[jz], loc.at[t]).start()

    give_back(0, r2, o_y)

    def chunk(r):
        return pl.ds(pl.multiple_of(r * rows, 128), rows)

    def half_rows(r, core):
        return dmo.at[pl.ds(pl.multiple_of(r * rows + core * (rows // 2), 16), rows // 2), :]

    def swap(buffer, r, sems):
        return remote(s1.at[chunk(r), :], buffer.at[chunk(r), :], sems.at[0, r], sems.at[1, r], me.sibling)

    gain_one, gain_two = gains[0:1, :], gains[1:2, :]
    o_gain[...] = jnp.zeros_like(o_gain)

    def buffers_free(n):
        pl.semaphore_signal(free.at[n], inc=1, device_id=me.sibling, device_id_type=MESH)

    def y_sent():
        @pl.when(me.here)
        def _():
            for d in range(1, n_t):
                there = r2.at[block(0), :]
                remote(there, o_y.at[0], a2a_s.at[0, d], a2a_r.at[0, jz], me.right).wait_send()
            pltpu.make_async_copy(r2.at[block(z), :], o_y.at[jz], loc.at[0]).wait()

    buffers_free(0)
    pl.semaphore_wait(free.at[0], 1)

    def finish_mixed(r):
        at = chunk(r)
        swap(r1, r, e1).wait_recv()
        db = s1[at, :].astype(F32) + r1[at, :].astype(F32)
        back, gain = norm_back(h_v[at, :], gain_two, db)
        o_gain[1:2, :] += gain
        dh = dmo[at, :].astype(F32) + back
        h_v[at, :] = dh
        back_out = dot_nt(dh.astype(BF), w_out[...]).astype(BF)
        for p in range(pairs):
            do_v[p, at, :] = back_out[:, p * PAIR:(p + 1) * PAIR]

    def expand(r):
        at = chunk(r)

        @pl.when(first_plane)
        def _():
            mine, theirs = half_rows(r, c), half_rows(r, 1 - c)
            remote(mine, mine, hop.at[0, r], hop.at[1, r], me.sibling).wait_recv()
            remote(mine, mine, hsib.at[0, r], hsib.at[1, r], me.sibling).start()
            remote(theirs, theirs, hsib.at[0, r], hsib.at[1, r], me.sibling).wait_recv()

        @pl.when(second_plane)
        def _():
            position = (r * rows + lax.broadcasted_iota(jnp.int32, (rows, dim), 0)).astype(F32)
            dmo[at, :] = jnp.where(position < len_v[0:1, 0:1], dmo[at, :].astype(F32), 0.0).astype(BF)

        dy = dmo[at, :]
        total = None
        for j in range(mb):
            dm = dot_nt(dy, w_ff[j, 0])
            gate, up = g_v[j, at, :].astype(F32), u_v[j, at, :].astype(F32)
            sig = 1.0 / (1.0 + jnp.exp(-gate))
            d_gate = (dm * up * (sig * (1.0 + gate * (1.0 - sig)))).astype(BF)
            d_up = (dm * (gate * sig)).astype(BF)
            g_v[j, at, :] = d_gate
            u_v[j, at, :] = d_up
            term = dot(d_gate, w_ff[j, 1]) + dot(d_up, w_ff[j, 2])
            total = term if total is None else total + term
        s1[at, :] = total.astype(BF)
        swap(r1, r, e1).start()

    def ff_grads(t):
        left = (m_v, g_v, u_v)[t]
        right = (dmo, b_v, b_v)[t]

        @pl.loop(0, mb)
        def _(j):
            @pl.loop(0, 2)
            def _(n):
                lanes = pl.ds(pl.multiple_of(n * (dim // 2), 128), dim // 2)
                w_ff[j, t, :, lanes] = dot_tn(left[j], right[:, lanes]).astype(BF)

    def column(p):
        return pl.ds(pl.multiple_of(p * part, 128), part)

    def order(i):
        return jnp.where(c == 0, i, mb - 1 - i)

    def key(kind, n):
        return KEY[kind] + n

    def half_of(n):
        return pl.ds(pl.multiple_of(lax.rem(n, 2) * half, 16), half)

    def grad_part(kind, n, j, p):
        if kind == FF:
            return w_ff.at[j, n // 2, half_of(n), column(p)]
        if kind == OUTS:
            return w_out.at[pl.ds(pl.multiple_of(j * ow, 16), ow), column(p)]
        return w_qkv.at[j, :, pl.ds(pl.multiple_of(p * part + n * quarter, 16), quarter), :]

    def landing(bufs, kind, n, slot):
        if kind == FF:
            return bufs[FF].at[slot, n // 2, half_of(n), :]
        if kind == OUTS:
            return bufs[OUTS].at[slot]
        return bufs[HEADS].at[slot, :, pl.ds(n * quarter, quarter), :]

    def land_x(kind, n, j, d):
        return landing([b.at[d - 1] for b in (lx_ff, lx_out, lx_qkv)], kind, n, j)

    def land_z(kind, n, slot):
        return landing((lz_ff, lz_out, lz_qkv), kind, n, slot)

    def staged(kind, slot):
        return (st_ff, st_out, st_qkv)[kind].at[slot]

    def x_copies(kind, n, j):
        k = key(kind, n)
        for d in range(1, nx):
            to = lax.rem(x + d, nx)
            yield d, remote(
                grad_part(kind, n, j, to), land_x(kind, n, j, d), x_s.at[k, j, d], x_r.at[k, j, d], me.at_x(d)
            )

    def x_start(kind, n, i):
        for _, copy in x_copies(kind, n, order(i)):
            copy.start()

    def reduce_step(kind, n, i):
        k, j = key(kind, n), order(i)
        s = c * mb + j
        mine = grad_part(kind, n, j, x)
        outer = ((s > z) & (z > 0)) | ((s < z) & (z < n_t - 1))
        fetch = [pltpu.make_async_copy(land_x(kind, n, j, d), staged(kind, d - 1), stage.at[d - 1]) for d in range(1, nx)]
        from_z = land_z(kind, n, j)
        fetch_z = pltpu.make_async_copy(from_z, staged(kind, nx - 1), stage.at[nx - 1])
        for d, copy in x_copies(kind, n, j):
            copy.wait_recv()
            fetch[d - 1].start()

        @pl.when(outer)
        def _():
            remote(from_z, from_z, z_s.at[k, j], z_r.at[k, j], me.right).wait_recv()
            fetch_z.start()

        for copy in fetch:
            copy.wait()
        total = mine[...].astype(F32)
        for d in range(1, nx):
            total = total + staged(kind, d - 1)[...].astype(F32)
        mine[...] = total.astype(BF)

        @pl.when(outer)
        def _():
            fetch_z.wait()
            mine[...] = (mine[...].astype(F32) + staged(kind, nx - 1)[...].astype(F32)).astype(BF)

        pl.when(s > z)(remote(mine, land_z(kind, n, j), z_s.at[k, j], z_r.at[k, j], me.right).start)
        pl.when(s < z - 1)(remote(mine, land_z(kind, n, j), z_s.at[k, j], z_r.at[k, j], me.left).start)
        pl.when(s == z - 1)(remote(mine, land_z(kind, n, mb), z_s.at[k, j], zo_r.at[k], me.left).start)

    def final_part(kind, n):
        if kind == FF:
            return o_down.at[half_of(n), :] if n < 2 else o_gu.at[n // 2 - 1, half_of(n), :]
        return o_out if kind == OUTS else o_qkv

    def final_copies(kind, n):
        k, target, mine = key(kind, n), final_part(kind, n), grad_part(kind, n, jz, x)
        cases = []
        for core in range(2):
            if kind == HEADS:
                stays = theirs = mine
            else:
                stays = mine.at[:, core * quarter:(core + 1) * quarter]
                theirs = mine.at[:, (1 - core) * quarter:(2 - core) * quarter]
            if kind != HEADS or core == n:
                cases.append((c == core, pltpu.make_async_copy(stays, target, f_l.at[k]), True))
            if kind != HEADS or core != n:
                cases.append((c == core, remote(theirs, target, f_s.at[k], f_r.at[k], me.sibling), False))
        return cases

    def own_piece(kind, n):
        k = key(kind, n)
        mine = grad_part(kind, n, jz, x)

        @pl.when(me.here)
        def _():
            sides = ((z > 0, land_z(kind, n, jz), z_r.at[k, jz], 0), (z < n_t - 1, land_z(kind, n, mb), zo_r.at[k], nx - 1))
            for there, src, sem, slot in sides:
                @pl.when(there)
                def _(src=src, sem=sem, slot=slot):
                    remote(src, src, f_s.at[k], sem, me.right).wait_recv()
                    pltpu.make_async_copy(src, staged(kind, slot), stage.at[slot]).start()
            for there, src, sem, slot in sides:
                @pl.when(there)
                def _(src=src, slot=slot):
                    pltpu.make_async_copy(src, staged(kind, slot), stage.at[slot]).wait()
                    mine[...] = (mine[...].astype(F32) + staged(kind, slot)[...].astype(F32)).astype(BF)
            for case, copy, _ in final_copies(kind, n):
                pl.when(case)(copy.start)

    n_k = len(PIECES)

    def ahead(index):
        if index + AHEAD < n_k * mb:
            piece, i = divmod(index + AHEAD, mb)
            x_start(*PIECES[piece], i)

    def begin_reduce():
        for index in range(AHEAD):
            x_start(FF, index // mb, index % mb)

    def ff_round(n):
        for i in range(mb):
            n_next, i_next = n + (i + AHEAD) // mb, (i + AHEAD) % mb

            @pl.when(n_next < FF_PIECES)
            def _(n_next=n_next, i_next=i_next):
                x_start(FF, n_next, i_next)
            reduce_step(FF, n, i)

    def send_dv(r):
        return remote(vu_v.at[:, chunk(r), :], first.at[:, chunk(r), :], vsem.at[0, r], vsem.at[1, r], other_plane)

    def attention(r):
        at = chunk(r)
        for i in range(CHUNKS):
            @pl.when(r == i)
            def _(i=i):
                block_rows_i = slice(i * rows, (i + 1) * rows)

                @pl.loop(0, pairs, unroll=2)
                def _(p):
                    lanes = pl.ds(pl.multiple_of(p * PAIR, PAIR), PAIR)

                    def add_to(acc):
                        def add(a, b, value, fresh):
                            if fresh:
                                acc[p, a:b, :] = value
                            else:
                                acc[p, a:b, :] += value
                        return add

                    dq = attend_back_block(
                        i, rows, q_v[p, block_rows_i, :],
                        lambda h, a, b: (ka_v, kb_v)[h][p, a:b, :],
                        lambda rows_h, a, b: kt_v[p, rows_h, a:b],
                        lambda a, b: vu_v[p, a:b, :],
                        o_v[block_rows_i, lanes], do_v[p, block_rows_i, :],
                        lambda h, lo, hi: lse_v[p, h:h + 1, lo:hi],
                        add_to(dv_a), add_to(dk_a),
                    )
                    q_v[p, block_rows_i, :] = rotate_pair(
                        dq, cos[block_rows_i, :], -sin[block_rows_i, :]
                    ).astype(BF)

        pl.when(first_plane)(lambda: send_dv(r).wait_recv())
        for p in range(pairs):
            ka_v[p, at, :] = rotate_pair(dk_a[p, at, :], cos[at, :], -sin[at, :]).astype(BF)

            @pl.when(first_plane)
            def _(p=p):
                vu_v[p, at, :] = (dv_a[p, at, :] + first[p, at, :].astype(F32)).astype(BF)

            @pl.when(second_plane)
            def _(p=p):
                vu_v[p, at, :] = (0.5 * dv_a[p, at, :]).astype(BF)

    def slot_rows(t, j, at):
        source = (q_v, ka_v, vu_v)[t]
        return jnp.concatenate([source[j * slot_pairs + n, at, :] for n in range(slot_pairs)], axis=1)

    def finish_input(r):
        at = chunk(r)
        swap(r2, r, e2).wait_recv()
        da = s1[at, :].astype(F32) + r2[at, :].astype(F32)
        back, gain = norm_back(x_v[at, :].astype(F32), gain_one, da)
        o_gain[0:1, :] += gain
        r2[at, :] = (h_v[at, :] + back).astype(BF)

        @pl.when(second_plane)
        def _():
            mine = pl.ds(pl.multiple_of(r * rows + c * (rows // 2), 16), rows // 2)
            remote(r2.at[mine, :], dmo.at[mine, :], hop.at[0, r], hop.at[1, r], other_plane).start()

    def input_part(r):
        total = None
        for j in range(mb):
            for t in range(3):
                term = dot_nt(slot_rows(t, j, chunk(r)), w_qkv[j, t])
                total = term if total is None else total + term
        swap(r1, r, e1).wait_send()
        s1[chunk(r), :] = total.astype(BF)
        swap(r2, r, e2).start()

    def back(t):
        return CHUNKS - 1 - t

    @pl.when(first_plane)
    def _():
        @pl.loop(0, CHUNKS)
        def _(t):
            expand(back(t))

            @pl.when(t > 0)
            def _():
                finish_mixed(back(t - 1))

        ff_grads(0)
        finish_mixed(0)
        begin_reduce()
        ff_grads(1)
        ff_grads(2)

    @pl.when(second_plane)
    def _():
        expand(CHUNKS - 1)

    @pl.loop(0, pairs)
    def _(p):
        inside, _ = head_views(0, (seq, PAIR))
        kt_v[p] = jnp.where(inside, ka_v[p].astype(F32), kb_v[p].astype(F32)).T.astype(BF)

    y_sent()
    buffers_free(1)
    pl.semaphore_wait(free.at[1], 1)

    @pl.loop(0, CHUNKS)
    def _(t):
        r = back(t)
        pl.when(first_plane)(lambda: ff_round(t))

        @pl.when(second_plane)
        def _():
            pl.when(t < CHUNKS - 1)(lambda: expand(back(t + 1)))
            finish_mixed(r)

        attention(r)
        input_part(r)

        @pl.when(t > 0)
        def _():
            finish_input(back(t - 1))

    finish_input(0)

    @pl.when(second_plane)
    def _():
        for t in range(CHUNKS):
            send_dv(back(t)).start()

    give_back(1, r2, o_dx)
    for d in range(1, n_t):
        remote(o_gain, g_z.at[d], gz_s.at[d], gz_r.at[d], {"tensor": lax.rem(z + d, n_t)}).start()

    @pl.when(second_plane)
    def _():
        for t in range(3):
            ff_grads(t)
        begin_reduce()

    @pl.loop(0, 4)
    def _(n):
        lanes = pl.ds(pl.multiple_of(n * (dim // 4), 128), dim // 4)
        w_out[:, lanes] = dot_tn(o_v[...], h_v[:, lanes].astype(BF)).astype(BF)

    everything = pl.ds(0, seq)

    @pl.loop(0, CHUNKS)
    def _(r):
        b_v[chunk(r), :] = (normalise(x_v[chunk(r), :].astype(F32)) * gain_one).astype(BF)

    @pl.loop(0, mb)
    def _(j):
        for t in range(3):
            w_qkv[j, t] = dot_tn(b_v[...], slot_rows(t, j, everything)).astype(BF)

    @pl.when(second_plane)
    def _():
        @pl.loop(0, pairs)
        def _(p):
            ff_round(p)

    for index in range(FF_PIECES * mb, min(pairs * mb + AHEAD, n_k * mb)):
        x_start(*PIECES[index // mb], index % mb)
    for piece in range(pairs, n_k):
        for i in range(mb):
            ahead(piece * mb + i)
            reduce_step(*PIECES[piece], i)
        for done in range(piece - LAG) if piece == pairs else (piece - LAG,):
            own_piece(*PIECES[done])
        if piece == pairs:
            own_piece(*PIECES[piece - LAG])
    for piece in range(n_k - LAG, n_k):
        own_piece(*PIECES[piece])

    for d in range(1, n_t):
        remote(o_gain, g_z.at[d], gz_s.at[d], gz_r.at[d], me.right).wait()
    g_z[0] = o_gain[...]
    for d in range(1, n_t):
        g_z[0] += g_z[d]
    for d in range(1, nx):
        remote(g_z.at[0], g_x.at[d], gx_s.at[d], gx_r.at[d], me.at_x(d)).start()
    for d in range(1, nx):
        remote(g_z.at[0], g_x.at[d], gx_s.at[d], gx_r.at[d], me.at_x(d)).wait()
    o_gain[...] = g_z[0]
    for d in range(1, nx):
        o_gain[...] += g_x[d]

    @pl.when(jnp.logical_not(me.here))
    def _():
        for kind, n in PIECES:
            k, target = key(kind, n), final_part(kind, n)
            taken = remote(target, target, f_s.at[k], f_r.at[k], me.sibling)
            if kind == HEADS:
                pl.when(c == n)(taken.wait_recv)
            else:
                taken.wait_recv()

    for kind, n in PIECES:
        k = key(kind, n)
        for j in range(mb):
            for _, copy in x_copies(kind, n, j):
                copy.wait_send()
            mine = grad_part(kind, n, j, x)
            pl.when(c * mb + j != z)(remote(mine, mine, z_s.at[k, j], z_r.at[k, j], me.right).wait_send)

    @pl.when(me.here)
    def _():
        for kind, n in PIECES:
            for case, copy, local in final_copies(kind, n):
                pl.when(case)(copy.wait if local else copy.wait_send)
        for d in range(1, n_t):
            there = r2.at[block(0), :]
            remote(there, o_dx.at[0], a2a_s.at[1, d], a2a_r.at[1, jz], me.right).wait_send()
        pltpu.make_async_copy(r2.at[block(z), :], o_dx.at[jz], loc.at[1]).wait()

    for t, dst in enumerate((o_y, o_dx)):
        for i in range(mb):
            @pl.when(c * mb + i != z)
            def _(t=t, i=i, dst=dst):
                remote(dst.at[i], dst.at[i], a2a_s.at[t, 0], a2a_r.at[t, i], me.right).wait_recv()

    for r in range(CHUNKS):
        swap(r2, r, e2).wait_send()
        mine = half_rows(r, c)
        pl.when(second_plane)(remote(mine, mine, hop.at[0, r], hop.at[1, r], me.sibling).wait_send)
        pl.when(first_plane)(remote(mine, mine, hsib.at[0, r], hsib.at[1, r], me.sibling).wait_send)
        pl.when(second_plane)(send_dv(r).wait_send)


def layer_kernel(
    tok, cot, lens, qkv, out, gu, down, gains, cos, sin,
    o_y, o_dx, o_qkv, o_out, o_gu, o_down, o_gain, tok_o, lx_ff, lx_out, lx_qkv, lz_ff, lz_out, lz_qkv,
    w_qkv, w_out, w_ff, x_v, first, q_v, ka_v, kb_v, vt_v, v_v, vu_v, o_v, lse_v, h_v, b_v, g_v, u_v, m_v,
    s1, r1, r2, dmo, len_v, dk_a, dv_a, st_ff, st_out, st_qkv, g_z, g_x,
    *sems,
):
    me = Place(tok.shape[0])
    me.meet()
    forward_part(
        me, tok, cot, lens, qkv, out, gu, down, gains, cos, sin, tok_o,
        w_qkv, w_out, w_ff, x_v, first, q_v, ka_v, kb_v, vt_v, v_v, vu_v, o_v, lse_v, h_v, b_v, g_v, u_v, m_v,
        s1, r1, r2, dmo, len_v, *sems[:20],
    )
    backward_part(
        me, gains, cos, sin, o_y, o_dx, o_qkv, o_out, o_gu, o_down, o_gain,
        lx_ff, lx_out, lx_qkv, lz_ff, lz_out, lz_qkv,
        w_qkv, w_out, w_ff, x_v, q_v, ka_v, kb_v, vt_v, vu_v, o_v, lse_v, h_v, b_v, g_v, u_v, m_v,
        dmo, v_v, first, s1, r1, r2, len_v, dk_a, dv_a, st_ff, st_out, st_qkv, g_z, g_x, *sems[20:],
    )


def layer(tokens, cotangent, lens, qkv, out, gu, down, gains, tables):
    mb, block_rows, dim = tokens.shape
    n_t, n_dp = lax.axis_size("tensor"), lax.axis_size("dp")
    nx = n_dp // 2
    seq = block_rows * n_t
    part, quarter = dim // nx, dim // n_dp
    cols, ow, ff = qkv.shape[3], out.shape[1], down.shape[1]
    pairs = mb * cols // PAIR
    assert pairs == COUNT[GU] == CHUNKS
    dma = pltpu.SemaphoreType.DMA
    wide, heads, turned = (seq, dim), (pairs, seq, PAIR), (pairs, PAIR, seq)
    hidden, block = (mb, seq, ff), (mb, block_rows, dim)
    n_k = len(PIECES)
    shape = lambda s, t=BF: jax.ShapeDtypeStruct(s, t)
    vmem = lambda s, t=BF: pltpu.VMEM(s, t)

    def parts(lead, split):
        return (*lead, 3, ff, split), (*lead, ow, split), (*lead, 3, split, cols)

    return pl.pallas_call(
        layer_kernel,
        out_shape=(
            shape(block), shape(block),
            shape((3, quarter, cols)), shape((ow, quarter)), shape((2, ff, quarter)), shape((ff, quarter)),
            shape((2, dim), F32), shape(wide),
            *(shape(s) for s in parts((nx - 1, mb), part)),
            *(shape(s) for s in parts((mb + 1,), part)),
        ),
        in_specs=[ANY, ANY, VMEM, ANY, ANY, ANY, ANY, VMEM, VMEM, VMEM],
        out_specs=(*(ANY,) * 6, VMEM, *(ANY,) * 7),
        scratch_shapes=[
            vmem((mb, 3, dim, cols)), vmem((mb * ow, dim)), vmem((mb, 3, ff, dim)),
            vmem(wide), *[vmem(heads)] * 4, vmem(turned), *[vmem(heads)] * 2,
            vmem((seq, pairs * PAIR)), vmem((pairs, 2, seq), F32), vmem(wide, F32), vmem(wide), *[vmem(hidden)] * 3,
            *[vmem(wide)] * 4, vmem((8, 128), F32), *[vmem(heads, F32)] * 2,
            vmem((nx, ff // 2, part)), vmem((nx, ow, part)), vmem((nx, 3, quarter, cols)),
            vmem((n_t, 2, dim), F32), vmem((nx, 2, dim), F32),
            dma((5,)), dma((mb,)), dma((n_t,)), dma((mb,)), dma((n_t,)), dma((n_t,)), dma((n_t,)), dma((2,)),
            dma((N_PIECES,)), dma((N_PIECES,)), dma((N_PIECES, mb)), dma((N_PIECES, mb)),
            dma((N_PIECES, mb, nx)), dma((N_PIECES, mb, nx)),
            *[dma((2, CHUNKS))] * 5, dma((2,)),
            dma((2,)), dma((2, n_t)), dma((2, mb)), *[dma((2, CHUNKS))] * 5,
            dma((n_k, mb, nx)), dma((n_k, mb, nx)), dma((n_k, mb)), dma((n_k, mb)), *[dma((n_k,))] * 4,
            dma((nx,)), dma((n_t,)), dma((n_t,)), dma((nx,)), dma((nx,)), pltpu.SemaphoreType.REGULAR((2,)),
        ],
        compiler_params=pltpu.CompilerParams(
            collective_id=0, has_side_effects=True, vmem_limit_bytes=63 << 20
        ),
        name="layer",
    )(tokens, cotangent, lens, qkv, out, gu, down, gains, *tables)


def publish_kernel(*refs):
    count = len(refs) // 3
    sources, targets, held, sems = refs[:count], refs[count:2 * count], refs[2 * count:3 * count], refs[-1]
    copies = [pltpu.make_async_copy(src, dst, sems.at[n]) for n, (src, dst) in enumerate(zip(sources, held))]
    for copy in copies:
        copy.start()
    for copy, dst, src in zip(copies, targets, held):
        copy.wait()
        dst[...] = src[...].astype(dst.dtype)


def publish(*arrays):
    types = (BF,) + (F32,) * (len(arrays) - 1)
    return pl.pallas_call(
        publish_kernel,
        out_shape=tuple(jax.ShapeDtypeStruct(a.shape, t) for a, t in zip(arrays, types)),
        in_specs=[ANY] * len(arrays),
        out_specs=(VMEM,) * len(arrays),
        scratch_shapes=[*(pltpu.VMEM(a.shape, a.dtype) for a in arrays), pltpu.SemaphoreType.DMA((len(arrays),))],
        compiler_params=pltpu.CompilerParams(vmem_limit_bytes=60 << 20),
        name="publish",
    )(*arrays)


def shards(tokens, lengths, qkv_weight, out_weight, gate_up_weight, down_weight, norm_gains, cotangent):
    dp, z = lax.axis_index("dp"), lax.axis_index("tensor")
    mb, rows, dim = tokens.shape
    n_t = lax.axis_size("tensor")
    tables = tuple(jnp.asarray(t) for t in rope_tables(rows * n_t))
    lens = jnp.broadcast_to(lengths.astype(F32)[:, None, None], (mb, 8, 128))
    o_y, o_dx, o_qkv, o_out, o_gu, o_down, gain = layer(
        tokens, cotangent, lens, qkv_weight, out_weight, jnp.swapaxes(gate_up_weight, 2, 3), down_weight,
        norm_gains[0], tables,
    )[:7]
    share = dim // (lax.axis_size("dp") * n_t)
    gain = lax.dynamic_slice_in_dim(gain, (dp * n_t + z) * share, share, 1)
    o_y, o_dx, o_qkv, o_out, o_gu, o_down = publish(o_y, o_dx, o_qkv, o_out, o_gu, o_down)
    return (
        o_y[None], o_dx[None], o_qkv[None], o_out[None], jnp.swapaxes(o_gu, 1, 2)[None], o_down[None],
        gain[None],
    )


def solution(mesh):
    in_specs = (
        P("dp", "tensor", None),
        P("dp"),
        P("section", None, None, "tensor"),
        P("section", "tensor", None),
        P("section", None, None, "tensor"),
        P("section", "tensor", None),
        P("section", None, None),
        P("dp", "tensor", None),
    )
    out_specs = (
        P("section", "dp", "tensor", None),
        P("section", "dp", "tensor", None),
        P("section", None, "dp", "tensor"),
        P("section", "tensor", "dp"),
        P("section", None, "dp", "tensor"),
        P("section", "tensor", "dp"),
        P("section", None, ("dp", "tensor")),
    )
    return jax.shard_map(shards, mesh=mesh, in_specs=in_specs, out_specs=out_specs, check_vma=False)
```

```python
import jax
import jax.numpy as jnp
import numpy as np
from jax import lax
from jax.experimental import pallas as pl
from jax.experimental.pallas import tpu as pltpu
from jax.sharding import PartitionSpec as P

MESH = pl.DeviceIdType.MESH
ANY = pl.BlockSpec(memory_space=pl.ANY)
VMEM = pl.BlockSpec(memory_space=pltpu.VMEM)
NORM_EPS = 1e-6
ROPE_BASE = 10000.0
SCORE_SCALE = 0.125
MASK_VALUE = -1e30
HD = 64
PAIR = 2 * HD
CHUNKS = 4
NT = (((1,), (1,)), ((), ()))
BF, F32 = jnp.bfloat16, jnp.float32

QKV, OUT, GU, DOWN = range(4)
COUNT = (2, 1, 4, 2)
BASE = (0, 2, 3, 7)
N_PIECES = 9


def dot(a, b):
    return jnp.dot(a, b, preferred_element_type=F32)


def dot_nt(a, b):
    return lax.dot_general(a, b, NT, preferred_element_type=F32)


def dot_tn(a, b):
    return lax.dot_general(a, b, (((0,), (0,)), ((), ())), preferred_element_type=F32)


def remote(src, dst, send, recv, to):
    return pltpu.make_async_remote_copy(
        src_ref=src, dst_ref=dst, send_sem=send, recv_sem=recv, device_id=to, device_id_type=MESH
    )


class Place:
    def __init__(self, mb):
        self.n_t = lax.axis_size("tensor")
        self.nx = lax.axis_size("dp") // 2
        self.section = lax.axis_index("section")
        dp = lax.axis_index("dp")
        self.z = lax.axis_index("tensor")
        self.x, self.c = dp // 2, lax.rem(dp, 2)
        self.here = self.z // mb == self.c
        self.jz = self.z - self.c * mb
        self.sibling = {"dp": 2 * self.x + 1 - self.c}
        self.right, self.left = {"tensor": self.z + 1}, {"tensor": self.z - 1}

    def at_x(self, d):
        return {"dp": 2 * lax.rem(self.x + d, self.nx) + self.c}

    def meet(self):
        barrier = pltpu.get_barrier_semaphore()
        partners = [{"tensor": lax.rem(self.z + k, self.n_t)} for k in range(1, self.n_t)]
        partners += [self.at_x(k) for k in range(1, self.nx)]
        partners += [self.sibling, {"section": 1 - self.section}]
        for partner in partners:
            pl.semaphore_signal(barrier, inc=1, device_id=partner, device_id_type=MESH)
        pl.semaphore_wait(barrier, len(partners))


def rope_tables(positions):
    lane = np.arange(PAIR)
    frequency = ROPE_BASE ** (-(lane % (HD // 2)) * 2.0 / HD)
    angles = np.arange(positions)[:, None] * frequency[None, :]
    sign = np.where(lane % HD < HD // 2, -1.0, 1.0)
    return np.cos(angles).astype(np.float32), (np.sin(angles) * sign).astype(np.float32)


def rotate_pair(values, cos, sin):
    lane = lax.broadcasted_iota(jnp.int32, values.shape, 1)
    partner = jnp.where(
        lax.rem(lane, HD) < HD // 2,
        pltpu.roll(values, PAIR - HD // 2, 1),
        pltpu.roll(values, HD // 2, 1),
    )
    return values * cos + partner * sin


def normalise(values):
    return values * lax.rsqrt(jnp.mean(values * values, axis=-1, keepdims=True) + NORM_EPS)


def head_views(h, shape):
    lane = lax.broadcasted_iota(jnp.int32, shape, 1)
    return lane // HD == h, lane == (1 - h) * HD


def causal_block(blk):
    key = lax.broadcasted_iota(jnp.int32, (blk, blk), 0)
    query = lax.broadcasted_iota(jnp.int32, (blk, blk), 1)
    return key <= query


def head_keys(keys, length, first_row):
    position = (first_row + lax.broadcasted_iota(jnp.int32, keys.shape, 0)).astype(F32)
    bias = jnp.where(position < length, 0.0, MASK_VALUE)
    views = []
    for h in range(2):
        inside, extra = head_views(h, keys.shape)
        views.append(jnp.where(inside, keys, jnp.where(extra, bias, 0.0)).astype(BF))
    return views


def head_queries(h, queries, mark):
    inside, extra = head_views(h, queries.shape)
    return jnp.where(inside, queries, jnp.where(extra, mark, 0.0)).astype(BF)


def attend_block(i, blk, queries, keys, vals_t, put_out, put_lse):
    lo, hi = i * blk, (i + 1) * blk
    visible = causal_block(blk)
    queries = queries.astype(F32)
    parts = []
    for h in range(2):
        qi = head_queries(h, queries, 1.0)
        vh = slice(h * HD, (h + 1) * HD)
        s_diag = jnp.where(visible, dot_nt(keys(h, lo, hi), qi), MASK_VALUE)
        top = jnp.max(s_diag, axis=0, keepdims=True)
        if i:
            s_full = dot_nt(keys(h, 0, lo), qi)
            top = jnp.maximum(top, jnp.max(s_full, axis=0, keepdims=True))
        p_diag = jnp.exp(s_diag - top)
        total = jnp.sum(p_diag, axis=0, keepdims=True)
        acc = dot(vals_t(vh, lo, hi), p_diag.astype(BF))
        if i:
            p_full = jnp.exp(s_full - top)
            total = total + jnp.sum(p_full, axis=0, keepdims=True)
            acc = acc + dot(vals_t(vh, 0, lo), p_full.astype(BF))
        parts.append(acc / total)
        put_lse(h, lo, hi, top + jnp.log(total))
    put_out(lo, hi, jnp.concatenate(parts, axis=0).T.astype(BF))


def forward_part(
    me, tok, cot, lens, qkv, out, gu, down, gains, cos, sin, tok_o,
    w_qkv, w_out, w_ff, x_v, first, q_v, ka_v, kb_v, vt_v, v_v, vu_v, o_v, lse_v, h_v, b_v, g_v, u_v, m_v,
    s1, r1, r2, dmo, len_v,
    loc, a2a_s, a2a_r, c2a_s, c2a_r, y_s, y_r, sib, own_r, own_l, z_r, z_f, x_s, x_r, hop, hsib, e1, e2, vsem, lsem,
):
    mb, block_rows, dim = tok.shape
    x, c, z, n_t, nx, jz = me.x, me.c, me.z, me.n_t, me.nx, me.jz
    part = dim // nx
    cols, ow, half = qkv.shape[3], out.shape[1], down.shape[1] // 2
    seq = x_v.shape[0]
    rows = seq // CHUNKS
    pairs = q_v.shape[0]
    first_plane, second_plane = me.section == 0, me.section == 1

    def column(p):
        return pl.ds(pl.multiple_of(p * part, 128), part)

    def shard_part(w, n, p):
        if w == QKV:
            return qkv.at[0, :, pl.ds(pl.multiple_of(p * part + n * (part // 2), 16), part // 2), :]
        if w == OUT:
            return out.at[0, :, column(p)]
        if w == GU:
            return gu.at[0, n // 2, pl.ds(pl.multiple_of(lax.rem(n, 2) * half, 16), half), column(p)]
        return down.at[0, pl.ds(n * half, half), column(p)]

    def slot_part(w, n, j, p):
        if w == QKV:
            return w_qkv.at[j, :, pl.ds(pl.multiple_of(p * part + n * (part // 2), 16), part // 2), :]
        if w == OUT:
            return w_out.at[pl.ds(pl.multiple_of(j * ow, 16), ow), column(p)]
        if w == GU:
            return w_ff.at[j, 1 + n // 2, pl.ds(pl.multiple_of(lax.rem(n, 2) * half, 16), half), column(p)]
        return w_ff.at[j, 0, pl.ds(n * half, half), column(p)]

    own_slots = (
        (qkv.at[0], w_qkv.at[jz]),
        (out.at[0], w_out.at[pl.ds(pl.multiple_of(jz * ow, 16), ow), :]),
        (gu.at[0], w_ff.at[jz, 1:3]),
        (down.at[0], w_ff.at[jz, 0]),
    )

    def own_copies(w, n):
        k = BASE[w] + n
        src, dst = shard_part(w, n, x), slot_part(w, n, jz, x)
        return (
            (z < n_t - 1, remote(src, dst, own_r.at[k], z_r.at[k, jz], me.right)),
            (z > 0, remote(src, dst, own_l.at[k], z_r.at[k, jz], me.left)),
        )

    def own_start(w, n):
        @pl.when(me.here)
        def _():
            for there, copy in own_copies(w, n):
                pl.when(there)(copy.start)

    def own_wait(w, n):
        @pl.when(me.here)
        def _():
            for there, copy in own_copies(w, n):
                pl.when(there)(copy.wait_send)

    def order(i):
        return jnp.where(c == 0, mb - 1 - i, i)

    def foreign(w, n, i):
        j = order(i)
        s = c * mb + j
        k = BASE[w] + n

        @pl.when(s != z)
        def _():
            piece = slot_part(w, n, j, x)
            to_right = remote(piece, piece, z_f.at[k, j], z_r.at[k, j], me.right)
            to_left = remote(piece, piece, z_f.at[k, j], z_r.at[k, j], me.left)
            to_right.wait_recv()
            pl.when((s < z) & (z < n_t - 1))(to_right.start)
            pl.when((s > z) & (z > 0))(to_left.start)
            for d in range(1, nx):
                remote(piece, piece, x_s.at[k, j, d], x_r.at[k, j, x], me.at_x(d)).start()

    def wait_slot(w, j):
        s = c * mb + j

        @pl.when(s != z)
        def _():
            for n in range(COUNT[w]):
                k = BASE[w] + n
                for d in range(1, nx):
                    p = lax.rem(x + d, nx)
                    piece = slot_part(w, n, j, p)
                    remote(piece, piece, x_s.at[k, j, d], x_r.at[k, j, p], me.right).wait_recv()

    def gu_step(n, i):
        if i == 0:
            @pl.when(n >= 2)
            def _():
                own_wait(GU, n - 2)
            own_start(GU, n)
        foreign(GU, n, i)

    def down_steps(i):
        for n in range(COUNT[DOWN]):
            if i == 0:
                own_wait(GU, n + 2)
                own_start(DOWN, n)
            foreign(DOWN, n, i)

    def block_at(n):
        return pl.ds(pl.multiple_of(n * block_rows, 128), block_rows)

    block = block_at(z)
    other_plane = {"section": 1 - me.section}

    def spread(source, target, send, recv):
        for i in range(mb):
            zt = c * mb + i

            @pl.when(zt != z)
            def _(i=i, zt=zt):
                remote(source.at[i], target.at[block, :], send.at[i], recv.at[z], {"tensor": zt}).start()

    def arrived(target, zs, recv):
        there = target.at[block_at(zs), :]
        return remote(there, there, recv.at[zs], recv.at[zs], me.right)

    def to_first(zs):
        return remote(tok_o.at[block_at(zs), :], x_v.at[block_at(zs), :], y_s.at[zs], y_r.at[zs], other_plane)

    pl.when(second_plane)(lambda: spread(tok, tok_o, a2a_s, a2a_r))
    for i in range(mb):
        @pl.when(first_plane & (c * mb + i == z))
        def _(i=i):
            pltpu.make_async_copy(tok.at[i], x_v.at[block, :], loc.at[4]).start()

    @pl.when(me.here)
    def _():
        remote(lens.at[jz], len_v, lsem.at[0], lsem.at[1], me.sibling).start()
        len_v[...] = lens[jz]
        for w, (src, dst) in enumerate(own_slots):
            pltpu.make_async_copy(src, dst, loc.at[w]).start()

    own_start(QKV, 0)
    own_start(QKV, 1)
    for w, n in ((QKV, 0), (QKV, 1), (OUT, 0)):
        if w == OUT:
            own_wait(QKV, 0)
            own_start(OUT, 0)
        for i in range(mb):
            foreign(w, n, i)
        if (w, n) == (QKV, 1):
            @pl.when(second_plane & me.here)
            def _():
                for zs in range(n_t):
                    @pl.when(zs != z)
                    def _(zs=zs):
                        arrived(tok_o, zs, a2a_r).wait_recv()
                        to_first(zs).start()

    def ff_steps(i):
        @pl.loop(0, COUNT[GU])
        def _(n):
            gu_step(n, i)
        down_steps(i)

    @pl.when(second_plane)
    def _():
        for i in range(mb):
            ff_steps(i)
        spread(cot, dmo, c2a_s, c2a_r)
        for i in range(mb):
            @pl.when(c * mb + i == z)
            def _(i=i):
                pltpu.make_async_copy(cot.at[i], dmo.at[block, :], loc.at[4]).start()

    @pl.when(first_plane & me.here)
    def _():
        for zs in range(n_t):
            @pl.when(zs != z)
            def _(zs=zs):
                to_first(zs).wait_recv()
        pltpu.make_async_copy(tok.at[0], x_v.at[block, :], loc.at[4]).wait()
        remote(x_v, x_v, sib.at[0], sib.at[1], me.sibling).start()

    @pl.when(jnp.logical_not(me.here))
    def _():
        remote(len_v, len_v, lsem.at[0], lsem.at[1], me.sibling).wait_recv()
        pl.when(first_plane)(remote(x_v, x_v, sib.at[0], sib.at[1], me.sibling).wait_recv)

    length = len_v[0:1, :]

    @pl.when(me.here)
    def _():
        for w, (src, dst) in enumerate(own_slots):
            pltpu.make_async_copy(src, dst, loc.at[w]).wait()

    for j in range(mb):
        wait_slot(QKV, j)
        wait_slot(OUT, j)

    gain_one, gain_two = gains[0:1, :], gains[1:2, :]

    def chunk(r):
        return pl.ds(pl.multiple_of(r * rows, 128), rows)

    def halves(r, core):
        return x_v.at[pl.ds(pl.multiple_of(r * rows + core * (rows // 2), 16), rows // 2), :]

    def send_v(r):
        return remote(v_v.at[:, chunk(r), :], first.at[:, chunk(r), :], vsem.at[0, r], vsem.at[1, r], other_plane)

    def swap(buffer, r, sems):
        return remote(s1.at[chunk(r), :], buffer.at[chunk(r), :], sems.at[0, r], sems.at[1, r], me.sibling)

    def project(r):
        at = chunk(r)
        a = (normalise(x_v[at, :].astype(F32)) * gain_one).astype(BF)
        cos_r, sin_r = cos[at, :], sin[at, :]
        for j in range(mb):
            q = dot(a, w_qkv[j, 0])
            k = dot(a, w_qkv[j, 1])
            v = dot(a, w_qkv[j, 2])
            for n in range(cols // PAIR):
                p = j * (cols // PAIR) + n
                lanes = slice(n * PAIR, (n + 1) * PAIR)
                q_v[p, at, :] = (rotate_pair(q[:, lanes], cos_r, sin_r) * SCORE_SCALE).astype(BF)
                keys = rotate_pair(k[:, lanes], cos_r, sin_r).astype(BF).astype(F32)
                ka_v[p, at, :], kb_v[p, at, :] = head_keys(keys, length, r * rows)
                v_v[p, at, :] = v[:, lanes].astype(BF)

        @pl.when(first_plane)
        def _():
            send_v(r).start()
            for p in range(pairs):
                vals = v_v[p, at, :]
                vu_v[p, at, :] = vals
                vt_v[p, :, at] = vals.astype(F32).T.astype(BF)

        @pl.when(second_plane)
        def _():
            send_v(r).wait_recv()
            for p in range(pairs):
                vals = (0.5 * v_v[p, at, :].astype(F32) + 0.5 * first[p, at, :].astype(F32)).astype(BF)
                vu_v[p, at, :] = vals
                vt_v[p, :, at] = vals.astype(F32).T.astype(BF)

    def attention(r):
        for i in range(CHUNKS):
            @pl.when(r == i)
            def _(i=i):
                @pl.loop(0, pairs, unroll=2)
                def _(p):
                    lanes = pl.ds(pl.multiple_of(p * PAIR, PAIR), PAIR)

                    def put_out(lo, hi, value):
                        o_v[lo:hi, lanes] = value

                    def put_lse(h, lo, hi, value):
                        lse_v[p, h:h + 1, lo:hi] = value

                    attend_block(
                        i, rows, q_v[p, i * rows:(i + 1) * rows, :],
                        lambda h, lo, hi: (ka_v, kb_v)[h][p, lo:hi, :],
                        lambda vh, lo, hi: vt_v[p, vh, lo:hi],
                        put_out, put_lse,
                    )

    def enter(r):
        at = chunk(r)
        swap(r1, r, e1).wait_recv()
        h = x_v[at, :].astype(F32) + s1[at, :].astype(F32) + r1[at, :].astype(F32)
        h_v[at, :] = h
        b_v[at, :] = (normalise(h) * gain_two).astype(BF)
        swap(r1, r, e1).wait_send()

    def through_slot(r, j):
        at = chunk(r)
        b = b_v[at, :]
        gate = dot_nt(b, w_ff[j, 1])
        up = dot_nt(b, w_ff[j, 2])
        m = (gate / (1.0 + jnp.exp(-gate)) * up).astype(BF)
        g_v[j, at, :] = gate.astype(BF)
        u_v[j, at, :] = up.astype(BF)
        m_v[j, at, :] = m
        return dot(m, w_ff[j, 0])

    def leave(r, grown):
        s1[chunk(r), :] = grown.astype(BF)
        swap(r2, r, e2).start()

    def finish(r):
        at = chunk(r)
        swap(r2, r, e2).wait_recv()
        r2[at, :] = (h_v[at, :] + s1[at, :].astype(F32) + r2[at, :].astype(F32)).astype(BF)

        @pl.when(first_plane)
        def _():
            mine = pl.ds(pl.multiple_of(r * rows + c * (rows // 2), 16), rows // 2)
            remote(
                r2.at[mine, :], x_v.at[mine, :], hop.at[0, r], hop.at[1, r], other_plane
            ).start()

    def finish_before(r):
        @pl.when(r > 0)
        def _():
            finish(r - 1)

    def mix_all(r):
        enter(r)
        leave(r, sum(through_slot(r, j) for j in range(mb)))
        finish_before(r)

    @pl.when(second_plane)
    def _():
        for j in range(mb):
            wait_slot(GU, j)
            wait_slot(DOWN, j)

    @pl.loop(0, CHUNKS)
    def _(r):
        @pl.when(first_plane)
        def _():
            gu_step(r, 0)

        @pl.when(second_plane)
        def _():
            mine, theirs = halves(r, c), halves(r, 1 - c)
            remote(mine, mine, hop.at[0, r], hop.at[1, r], me.sibling).wait_recv()
            remote(mine, mine, hsib.at[0, r], hsib.at[1, r], me.sibling).start()
            remote(theirs, theirs, hsib.at[0, r], hsib.at[1, r], me.sibling).wait_recv()

        @pl.when(second_plane & me.here & (r == CHUNKS - 1))
        def _():
            for zs in range(n_t):
                @pl.when(zs != z)
                def _(zs=zs):
                    arrived(dmo, zs, c2a_r).wait_recv()
            pltpu.make_async_copy(cot.at[0], dmo.at[block, :], loc.at[4]).wait()
            remote(dmo, dmo, sib.at[0], sib.at[1], me.sibling).start()

        project(r)
        attention(r)
        s1[chunk(r), :] = dot(o_v[chunk(r), :], w_out[...]).astype(BF)
        swap(r1, r, e1).start()

        @pl.when(second_plane & (r > 0))
        def _():
            mix_all(r - 1)

    pl.when(second_plane)(lambda: mix_all(CHUNKS - 1))

    @pl.when(first_plane)
    def _():
        down_steps(0)
        for i in range(1, mb - 1):
            ff_steps(i)
        for i in range(mb - 1):
            wait_slot(GU, order(i))
            wait_slot(DOWN, order(i))

        @pl.loop(0, CHUNKS)
        def _(r):
            gu_step(r, mb - 1)
            enter(r)
            s1[chunk(r), :] = sum(through_slot(r, order(i)) for i in range(mb - 1)).astype(BF)

        down_steps(mb - 1)
        wait_slot(GU, order(mb - 1))
        wait_slot(DOWN, order(mb - 1))

        @pl.loop(0, CHUNKS)
        def _(r):
            leave(r, s1[chunk(r), :].astype(F32) + through_slot(r, order(mb - 1)))
            finish_before(r)

    finish(CHUNKS - 1)
    for w, n in ((QKV, 1), (OUT, 0), (DOWN, 0), (DOWN, 1)):
        own_wait(w, n)
    for w in range(4):
        for n in range(COUNT[w]):
            k = BASE[w] + n
            for j in range(mb):
                s = c * mb + j

                @pl.when(s != z)
                def _(w=w, n=n, k=k, j=j, s=s):
                    piece = slot_part(w, n, j, x)
                    for d in range(1, nx):
                        remote(piece, piece, x_s.at[k, j, d], x_r.at[k, j, x], me.right).wait_send()
                    forwarded = ((s < z) & (z < n_t - 1)) | ((s > z) & (z > 0))
                    pl.when(forwarded)(remote(piece, piece, z_f.at[k, j], z_r.at[k, j], me.right).wait_send)

    @pl.when(second_plane)
    def _():
        for i in range(mb):
            @pl.when(c * mb + i != z)
            def _(i=i):
                remote(tok.at[i], tok.at[i], a2a_s.at[i], a2a_r.at[z], me.right).wait_send()
                remote(tok.at[i], tok.at[i], c2a_s.at[i], c2a_r.at[z], me.right).wait_send()

        @pl.when(me.here)
        def _():
            for zs in range(n_t):
                @pl.when(zs != z)
                def _(zs=zs):
                    to_first(zs).wait_send()

    @pl.when(me.here)
    def _():
        remote(lens.at[jz], len_v, lsem.at[0], lsem.at[1], me.sibling).wait_send()
        pl.when(first_plane)(remote(x_v, x_v, sib.at[0], sib.at[1], me.sibling).wait_send)
        pl.when(second_plane)(remote(dmo, dmo, sib.at[0], sib.at[1], me.sibling).wait_send)

    @pl.when(second_plane & jnp.logical_not(me.here))
    def _():
        remote(dmo, dmo, sib.at[0], sib.at[1], me.sibling).wait_recv()

    for r in range(CHUNKS):
        swap(r2, r, e2).wait_send()
        pl.when(first_plane)(send_v(r).wait_send)
        mine = halves(r, c)
        pl.when(first_plane)(remote(mine, mine, hop.at[0, r], hop.at[1, r], me.sibling).wait_send)
        pl.when(second_plane)(remote(mine, mine, hsib.at[0, r], hsib.at[1, r], me.sibling).wait_send)


LAG = 2
AHEAD = 3
FF, OUTS, HEADS = range(3)
FF_PIECES = 6
PIECES = [(FF, n) for n in range(FF_PIECES)] + [(OUTS, 0)] + [(HEADS, n) for n in range(4)]
KEY = (0, FF_PIECES, FF_PIECES + 1)


def attend_back_block(i, blk, queries, keys, keys_t, vals, outs, grads, stats, add_dv, add_dk):
    lo, hi = i * blk, (i + 1) * blk
    visible = causal_block(blk)
    queries, grads = queries.astype(F32), grads.astype(F32)
    product = (grads * outs.astype(F32)).T
    parts = []
    for h in range(2):
        qh, qz, gh = head_queries(h, queries, 1.0), head_queries(h, queries, 0.0), head_queries(h, grads, 0.0)
        rows_h = slice(h * HD, (h + 1) * HD)
        delta = jnp.sum(product[rows_h], axis=0, keepdims=True)
        stat = stats(h, lo, hi)

        def side(a, b, diagonal):
            p = jnp.exp(dot_nt(keys(h, a, b), qh) - stat)
            if diagonal:
                p = jnp.where(visible, p, 0.0)
            ds = (p * (dot_nt(vals(a, b), gh) - delta)).astype(BF)
            fresh = i == CHUNKS - 1 and h == 0
            add_dv(a, b, dot(p.astype(BF), gh), fresh)
            add_dk(a, b, dot(ds, qz), fresh)
            return dot(keys_t(rows_h, a, b), ds)

        dq_t = side(lo, hi, True)
        if i:
            dq_t = dq_t + side(0, lo, False)
        parts.append(dq_t)
    return jnp.concatenate(parts, axis=0).T * SCORE_SCALE


def norm_back(values, gain, grad):
    scale = lax.rsqrt(jnp.mean(values * values, axis=-1, keepdims=True) + NORM_EPS)
    unit = values * scale
    inner = grad * gain
    back = scale * (inner - unit * jnp.mean(inner * unit, axis=-1, keepdims=True))
    return back, jnp.sum(grad * unit, axis=0, keepdims=True)


def backward_part(
    me, gains, cos, sin, o_y, o_dx, o_qkv, o_out, o_gu, o_down, o_gain, lx_ff, lx_out, lx_qkv, lz_ff, lz_out, lz_qkv,
    w_qkv, w_out, w_ff, x_v, q_v, ka_v, kb_v, kt_v, vu_v, o_v, lse_v, h_v, b_v, g_v, u_v, m_v,
    dmo, do_v, first, s1, r1, r2, len_v, dk_a, dv_a, st_ff, st_out, st_qkv, g_z, g_x,
    loc, a2a_s, a2a_r, hop, hsib, e1, e2, vsem, x_s, x_r, z_s, z_r, zo_r, f_s, f_r, f_l, stage, gz_s, gz_r, gx_s, gx_r,
    free,
):
    mb, block_rows, dim = o_y.shape
    x, c, z, n_t, nx, jz = me.x, me.c, me.z, me.n_t, me.nx, me.jz
    part = dim // nx
    quarter, eighth = part // 2, part // 4
    cols, ow, half = w_qkv.shape[3], w_out.shape[0] // mb, w_ff.shape[2] // 2
    seq = x_v.shape[0]
    rows = seq // CHUNKS
    pairs = q_v.shape[0]
    slot_pairs = cols // PAIR
    first_plane, second_plane = me.section == 0, me.section == 1
    other_plane = {"section": 1 - me.section}

    def block(n):
        return pl.ds(pl.multiple_of(n * block_rows, 128), block_rows)

    def give_back(t, src, dst):
        @pl.when(me.here)
        def _():
            for d in range(1, n_t):
                to = lax.rem(z + d, n_t)
                remote(src.at[block(to), :], dst.at[jz], a2a_s.at[t, d], a2a_r.at[t, jz], {"tensor": to}).start()
            pltpu.make_async_copy(src.at[block(z), :], dst.at[jz], loc.at[t]).start()

    give_back(0, r2, o_y)

    def chunk(r):
        return pl.ds(pl.multiple_of(r * rows, 128), rows)

    def half_rows(r, core):
        return dmo.at[pl.ds(pl.multiple_of(r * rows + core * (rows // 2), 16), rows // 2), :]

    def swap(buffer, r, sems):
        return remote(s1.at[chunk(r), :], buffer.at[chunk(r), :], sems.at[0, r], sems.at[1, r], me.sibling)

    gain_one, gain_two = gains[0:1, :], gains[1:2, :]
    o_gain[...] = jnp.zeros_like(o_gain)

    def buffers_free(n):
        pl.semaphore_signal(free.at[n], inc=1, device_id=me.sibling, device_id_type=MESH)

    def y_sent():
        @pl.when(me.here)
        def _():
            for d in range(1, n_t):
                there = r2.at[block(0), :]
                remote(there, o_y.at[0], a2a_s.at[0, d], a2a_r.at[0, jz], me.right).wait_send()
            pltpu.make_async_copy(r2.at[block(z), :], o_y.at[jz], loc.at[0]).wait()

    buffers_free(0)
    pl.semaphore_wait(free.at[0], 1)

    def finish_mixed(r):
        at = chunk(r)
        swap(r1, r, e1).wait_recv()
        db = s1[at, :].astype(F32) + r1[at, :].astype(F32)
        back, gain = norm_back(h_v[at, :], gain_two, db)
        o_gain[1:2, :] += gain
        dh = dmo[at, :].astype(F32) + back
        h_v[at, :] = dh
        back_out = dot_nt(dh.astype(BF), w_out[...]).astype(BF)
        for p in range(pairs):
            do_v[p, at, :] = back_out[:, p * PAIR:(p + 1) * PAIR]

    def expand(r):
        at = chunk(r)

        @pl.when(first_plane)
        def _():
            mine, theirs = half_rows(r, c), half_rows(r, 1 - c)
            remote(mine, mine, hop.at[0, r], hop.at[1, r], me.sibling).wait_recv()
            remote(mine, mine, hsib.at[0, r], hsib.at[1, r], me.sibling).start()
            remote(theirs, theirs, hsib.at[0, r], hsib.at[1, r], me.sibling).wait_recv()

        @pl.when(second_plane)
        def _():
            position = (r * rows + lax.broadcasted_iota(jnp.int32, (rows, dim), 0)).astype(F32)
            dmo[at, :] = jnp.where(position < len_v[0:1, 0:1], dmo[at, :].astype(F32), 0.0).astype(BF)

        dy = dmo[at, :]
        total = None
        for j in range(mb):
            dm = dot_nt(dy, w_ff[j, 0])
            gate, up = g_v[j, at, :].astype(F32), u_v[j, at, :].astype(F32)
            sig = 1.0 / (1.0 + jnp.exp(-gate))
            d_gate = (dm * up * (sig * (1.0 + gate * (1.0 - sig)))).astype(BF)
            d_up = (dm * (gate * sig)).astype(BF)
            g_v[j, at, :] = d_gate
            u_v[j, at, :] = d_up
            term = dot(d_gate, w_ff[j, 1]) + dot(d_up, w_ff[j, 2])
            total = term if total is None else total + term
        s1[at, :] = total.astype(BF)
        swap(r1, r, e1).start()

    def ff_grads(t):
        left = (m_v, g_v, u_v)[t]
        right = (dmo, b_v, b_v)[t]

        @pl.loop(0, mb)
        def _(j):
            @pl.loop(0, 2)
            def _(n):
                lanes = pl.ds(pl.multiple_of(n * (dim // 2), 128), dim // 2)
                w_ff[j, t, :, lanes] = dot_tn(left[j], right[:, lanes]).astype(BF)

    def column(p):
        return pl.ds(pl.multiple_of(p * part, 128), part)

    def order(i):
        return jnp.where(c == 0, i, mb - 1 - i)

    def key(kind, n):
        return KEY[kind] + n

    def half_of(n):
        return pl.ds(pl.multiple_of(lax.rem(n, 2) * half, 16), half)

    def grad_part(kind, n, j, p):
        if kind == FF:
            return w_ff.at[j, n // 2, half_of(n), column(p)]
        if kind == OUTS:
            return w_out.at[pl.ds(pl.multiple_of(j * ow, 16), ow), column(p)]
        return w_qkv.at[j, :, pl.ds(pl.multiple_of(p * part + n * eighth, 16), eighth), :]

    def landing(bufs, kind, n, slot):
        if kind == FF:
            return bufs[FF].at[slot, n // 2, half_of(n), :]
        if kind == OUTS:
            return bufs[OUTS].at[slot]
        return bufs[HEADS].at[slot, :, pl.ds(n * eighth, eighth), :]

    def land_x(kind, n, j, d):
        return landing([b.at[d - 1] for b in (lx_ff, lx_out, lx_qkv)], kind, n, j)

    def land_z(kind, n, slot):
        return landing((lz_ff, lz_out, lz_qkv), kind, n, slot)

    def staged(kind, slot):
        return (st_ff, st_out, st_qkv)[kind].at[slot]

    def x_copies(kind, n, j):
        k = key(kind, n)
        for d in range(1, nx):
            to = lax.rem(x + d, nx)
            yield d, remote(
                grad_part(kind, n, j, to), land_x(kind, n, j, d), x_s.at[k, j, d], x_r.at[k, j, d], me.at_x(d)
            )

    def x_start(kind, n, i):
        for _, copy in x_copies(kind, n, order(i)):
            copy.start()

    def reduce_step(kind, n, i):
        k, j = key(kind, n), order(i)
        s = c * mb + j
        mine = grad_part(kind, n, j, x)
        outer = ((s > z) & (z > 0)) | ((s < z) & (z < n_t - 1))
        fetch = [pltpu.make_async_copy(land_x(kind, n, j, d), staged(kind, d - 1), stage.at[d - 1]) for d in range(1, nx)]
        from_z = land_z(kind, n, j)
        fetch_z = pltpu.make_async_copy(from_z, staged(kind, nx - 1), stage.at[nx - 1])
        for d, copy in x_copies(kind, n, j):
            copy.wait_recv()
            fetch[d - 1].start()

        @pl.when(outer)
        def _():
            remote(from_z, from_z, z_s.at[k, j], z_r.at[k, j], me.right).wait_recv()
            fetch_z.start()

        for copy in fetch:
            copy.wait()
        total = mine[...].astype(F32)
        for d in range(1, nx):
            total = total + staged(kind, d - 1)[...].astype(F32)
        mine[...] = total.astype(BF)

        @pl.when(outer)
        def _():
            fetch_z.wait()
            mine[...] = (mine[...].astype(F32) + staged(kind, nx - 1)[...].astype(F32)).astype(BF)

        pl.when(s > z)(remote(mine, land_z(kind, n, j), z_s.at[k, j], z_r.at[k, j], me.right).start)
        pl.when(s < z - 1)(remote(mine, land_z(kind, n, j), z_s.at[k, j], z_r.at[k, j], me.left).start)
        pl.when(s == z - 1)(remote(mine, land_z(kind, n, mb), z_s.at[k, j], zo_r.at[k], me.left).start)

    def final_part(kind, n):
        if kind == FF:
            return o_down.at[half_of(n), :] if n < 2 else o_gu.at[n // 2 - 1, half_of(n), :]
        return o_out if kind == OUTS else o_qkv.at[:, pl.ds(n % 2 * eighth, eighth), :]

    def final_copies(kind, n):
        k, target, mine = key(kind, n), final_part(kind, n), grad_part(kind, n, jz, x)
        cases = []
        for core in range(2):
            if kind == HEADS:
                stays = theirs = mine
            else:
                stays = mine.at[:, core * quarter:(core + 1) * quarter]
                theirs = mine.at[:, (1 - core) * quarter:(2 - core) * quarter]
            if kind != HEADS or core == n // 2:
                cases.append((c == core, pltpu.make_async_copy(stays, target, f_l.at[k]), True))
            if kind != HEADS or core != n // 2:
                cases.append((c == core, remote(theirs, target, f_s.at[k], f_r.at[k], me.sibling), False))
        return cases

    def own_piece(kind, n):
        k = key(kind, n)
        mine = grad_part(kind, n, jz, x)

        @pl.when(me.here)
        def _():
            sides = ((z > 0, land_z(kind, n, jz), z_r.at[k, jz], 0), (z < n_t - 1, land_z(kind, n, mb), zo_r.at[k], nx - 1))
            for there, src, sem, slot in sides:
                @pl.when(there)
                def _(src=src, sem=sem, slot=slot):
                    remote(src, src, f_s.at[k], sem, me.right).wait_recv()
                    pltpu.make_async_copy(src, staged(kind, slot), stage.at[slot]).start()
            for there, src, sem, slot in sides:
                @pl.when(there)
                def _(src=src, slot=slot):
                    pltpu.make_async_copy(src, staged(kind, slot), stage.at[slot]).wait()
                    mine[...] = (mine[...].astype(F32) + staged(kind, slot)[...].astype(F32)).astype(BF)
            for case, copy, _ in final_copies(kind, n):
                pl.when(case)(copy.start)

    n_k = len(PIECES)

    def ahead(index):
        if index + AHEAD < n_k * mb:
            piece, i = divmod(index + AHEAD, mb)
            x_start(*PIECES[piece], i)

    def begin_reduce():
        for index in range(AHEAD):
            x_start(FF, index // mb, index % mb)

    def ff_round(n):
        for i in range(mb):
            n_next, i_next = n + (i + AHEAD) // mb, (i + AHEAD) % mb

            @pl.when(n_next < FF_PIECES)
            def _(n_next=n_next, i_next=i_next):
                x_start(FF, n_next, i_next)
            reduce_step(FF, n, i)

    def send_dv(r):
        return remote(vu_v.at[:, chunk(r), :], first.at[:, chunk(r), :], vsem.at[0, r], vsem.at[1, r], other_plane)

    def attention(r):
        at = chunk(r)
        for i in range(CHUNKS):
            @pl.when(r == i)
            def _(i=i):
                block_rows_i = slice(i * rows, (i + 1) * rows)

                @pl.loop(0, pairs, unroll=2)
                def _(p):
                    lanes = pl.ds(pl.multiple_of(p * PAIR, PAIR), PAIR)

                    def add_to(acc):
                        def add(a, b, value, fresh):
                            if fresh:
                                acc[p, a:b, :] = value
                            else:
                                acc[p, a:b, :] += value
                        return add

                    dq = attend_back_block(
                        i, rows, q_v[p, block_rows_i, :],
                        lambda h, a, b: (ka_v, kb_v)[h][p, a:b, :],
                        lambda rows_h, a, b: kt_v[p, rows_h, a:b],
                        lambda a, b: vu_v[p, a:b, :],
                        o_v[block_rows_i, lanes], do_v[p, block_rows_i, :],
                        lambda h, lo, hi: lse_v[p, h:h + 1, lo:hi],
                        add_to(dv_a), add_to(dk_a),
                    )
                    q_v[p, block_rows_i, :] = rotate_pair(
                        dq, cos[block_rows_i, :], -sin[block_rows_i, :]
                    ).astype(BF)

        pl.when(first_plane)(lambda: send_dv(r).wait_recv())
        for p in range(pairs):
            ka_v[p, at, :] = rotate_pair(dk_a[p, at, :], cos[at, :], -sin[at, :]).astype(BF)

            @pl.when(first_plane)
            def _(p=p):
                vu_v[p, at, :] = (dv_a[p, at, :] + first[p, at, :].astype(F32)).astype(BF)

            @pl.when(second_plane)
            def _(p=p):
                vu_v[p, at, :] = (0.5 * dv_a[p, at, :]).astype(BF)

    def slot_rows(t, j, at):
        source = (q_v, ka_v, vu_v)[t]
        return jnp.concatenate([source[j * slot_pairs + n, at, :] for n in range(slot_pairs)], axis=1)

    def finish_input(r):
        at = chunk(r)
        swap(r2, r, e2).wait_recv()
        da = s1[at, :].astype(F32) + r2[at, :].astype(F32)
        back, gain = norm_back(x_v[at, :].astype(F32), gain_one, da)
        o_gain[0:1, :] += gain
        r2[at, :] = (h_v[at, :] + back).astype(BF)

        @pl.when(second_plane)
        def _():
            mine = pl.ds(pl.multiple_of(r * rows + c * (rows // 2), 16), rows // 2)
            remote(r2.at[mine, :], dmo.at[mine, :], hop.at[0, r], hop.at[1, r], other_plane).start()

    def input_part(r):
        total = None
        for j in range(mb):
            for t in range(3):
                term = dot_nt(slot_rows(t, j, chunk(r)), w_qkv[j, t])
                total = term if total is None else total + term
        swap(r1, r, e1).wait_send()
        s1[chunk(r), :] = total.astype(BF)
        swap(r2, r, e2).start()

    def back(t):
        return CHUNKS - 1 - t

    @pl.when(first_plane)
    def _():
        @pl.loop(0, CHUNKS)
        def _(t):
            expand(back(t))

            @pl.when(t > 0)
            def _():
                finish_mixed(back(t - 1))

        ff_grads(0)
        finish_mixed(0)
        begin_reduce()
        ff_grads(1)
        ff_grads(2)

    @pl.when(second_plane)
    def _():
        expand(CHUNKS - 1)

    @pl.loop(0, pairs)
    def _(p):
        inside, _ = head_views(0, (seq, PAIR))
        kt_v[p] = jnp.where(inside, ka_v[p].astype(F32), kb_v[p].astype(F32)).T.astype(BF)

    y_sent()
    buffers_free(1)
    pl.semaphore_wait(free.at[1], 1)

    @pl.loop(0, CHUNKS)
    def _(t):
        r = back(t)
        pl.when(first_plane)(lambda: ff_round(t))

        @pl.when(second_plane)
        def _():
            pl.when(t < CHUNKS - 1)(lambda: expand(back(t + 1)))
            finish_mixed(r)

        attention(r)
        input_part(r)

        @pl.when(t > 0)
        def _():
            finish_input(back(t - 1))

    finish_input(0)

    @pl.when(second_plane)
    def _():
        for t in range(CHUNKS):
            send_dv(back(t)).start()

    give_back(1, r2, o_dx)
    for d in range(1, n_t):
        remote(o_gain, g_z.at[d], gz_s.at[d], gz_r.at[d], {"tensor": lax.rem(z + d, n_t)}).start()

    @pl.when(second_plane)
    def _():
        for t in range(3):
            ff_grads(t)
        begin_reduce()

    @pl.loop(0, 4)
    def _(n):
        lanes = pl.ds(pl.multiple_of(n * (dim // 4), 128), dim // 4)
        w_out[:, lanes] = dot_tn(o_v[...], h_v[:, lanes].astype(BF)).astype(BF)

    everything = pl.ds(0, seq)

    @pl.loop(0, CHUNKS)
    def _(r):
        b_v[chunk(r), :] = (normalise(x_v[chunk(r), :].astype(F32)) * gain_one).astype(BF)

    @pl.loop(0, mb)
    def _(j):
        for t in range(3):
            w_qkv[j, t] = dot_tn(b_v[...], slot_rows(t, j, everything)).astype(BF)

    @pl.when(second_plane)
    def _():
        @pl.loop(0, pairs)
        def _(p):
            ff_round(p)

    for index in range(FF_PIECES * mb, min(pairs * mb + AHEAD, n_k * mb)):
        x_start(*PIECES[index // mb], index % mb)
    for piece in range(pairs, n_k):
        for i in range(mb):
            ahead(piece * mb + i)
            reduce_step(*PIECES[piece], i)
        for done in range(piece - LAG) if piece == pairs else (piece - LAG,):
            own_piece(*PIECES[done])
        if piece == pairs:
            own_piece(*PIECES[piece - LAG])
    for piece in range(n_k - LAG, n_k):
        own_piece(*PIECES[piece])

    for d in range(1, n_t):
        remote(o_gain, g_z.at[d], gz_s.at[d], gz_r.at[d], me.right).wait()
    g_z[0] = o_gain[...]
    for d in range(1, n_t):
        g_z[0] += g_z[d]
    for d in range(1, nx):
        remote(g_z.at[0], g_x.at[d], gx_s.at[d], gx_r.at[d], me.at_x(d)).start()
    for d in range(1, nx):
        remote(g_z.at[0], g_x.at[d], gx_s.at[d], gx_r.at[d], me.at_x(d)).wait()
    o_gain[...] = g_z[0]
    for d in range(1, nx):
        o_gain[...] += g_x[d]

    @pl.when(jnp.logical_not(me.here))
    def _():
        for kind, n in PIECES:
            k, target = key(kind, n), final_part(kind, n)
            taken = remote(target, target, f_s.at[k], f_r.at[k], me.sibling)
            if kind == HEADS:
                pl.when(c == n // 2)(taken.wait_recv)
            else:
                taken.wait_recv()

    for kind, n in PIECES:
        k = key(kind, n)
        for j in range(mb):
            for _, copy in x_copies(kind, n, j):
                copy.wait_send()
            mine = grad_part(kind, n, j, x)
            pl.when(c * mb + j != z)(remote(mine, mine, z_s.at[k, j], z_r.at[k, j], me.right).wait_send)

    @pl.when(me.here)
    def _():
        for kind, n in PIECES:
            for case, copy, local in final_copies(kind, n):
                pl.when(case)(copy.wait if local else copy.wait_send)
        for d in range(1, n_t):
            there = r2.at[block(0), :]
            remote(there, o_dx.at[0], a2a_s.at[1, d], a2a_r.at[1, jz], me.right).wait_send()
        pltpu.make_async_copy(r2.at[block(z), :], o_dx.at[jz], loc.at[1]).wait()

    for t, dst in enumerate((o_y, o_dx)):
        for i in range(mb):
            @pl.when(c * mb + i != z)
            def _(t=t, i=i, dst=dst):
                remote(dst.at[i], dst.at[i], a2a_s.at[t, 0], a2a_r.at[t, i], me.right).wait_recv()

    for r in range(CHUNKS):
        swap(r2, r, e2).wait_send()
        mine = half_rows(r, c)
        pl.when(second_plane)(remote(mine, mine, hop.at[0, r], hop.at[1, r], me.sibling).wait_send)
        pl.when(first_plane)(remote(mine, mine, hsib.at[0, r], hsib.at[1, r], me.sibling).wait_send)
        pl.when(second_plane)(send_dv(r).wait_send)


def layer_kernel(
    tok, cot, lens, qkv, out, gu, down, gains, cos, sin,
    o_y, o_dx, o_qkv, o_out, o_gu, o_down, o_gain, tok_o, lx_ff, lx_out, lx_qkv, lz_ff, lz_out, lz_qkv,
    w_qkv, w_out, w_ff, x_v, first, q_v, ka_v, kb_v, vt_v, v_v, vu_v, o_v, lse_v, h_v, b_v, g_v, u_v, m_v,
    s1, r1, r2, dmo, len_v, dk_a, dv_a, st_ff, st_out, st_qkv, g_z, g_x,
    *sems,
):
    me = Place(tok.shape[0])
    me.meet()
    forward_part(
        me, tok, cot, lens, qkv, out, gu, down, gains, cos, sin, tok_o,
        w_qkv, w_out, w_ff, x_v, first, q_v, ka_v, kb_v, vt_v, v_v, vu_v, o_v, lse_v, h_v, b_v, g_v, u_v, m_v,
        s1, r1, r2, dmo, len_v, *sems[:20],
    )
    backward_part(
        me, gains, cos, sin, o_y, o_dx, o_qkv, o_out, o_gu, o_down, o_gain,
        lx_ff, lx_out, lx_qkv, lz_ff, lz_out, lz_qkv,
        w_qkv, w_out, w_ff, x_v, q_v, ka_v, kb_v, vt_v, vu_v, o_v, lse_v, h_v, b_v, g_v, u_v, m_v,
        dmo, v_v, first, s1, r1, r2, len_v, dk_a, dv_a, st_ff, st_out, st_qkv, g_z, g_x, *sems[20:],
    )


def layer(tokens, cotangent, lens, qkv, out, gu, down, gains, tables):
    mb, block_rows, dim = tokens.shape
    n_t, n_dp = lax.axis_size("tensor"), lax.axis_size("dp")
    nx = n_dp // 2
    seq = block_rows * n_t
    part, quarter = dim // nx, dim // n_dp
    cols, ow, ff = qkv.shape[3], out.shape[1], down.shape[1]
    pairs = mb * cols // PAIR
    assert pairs == COUNT[GU] == CHUNKS
    dma = pltpu.SemaphoreType.DMA
    wide, heads, turned = (seq, dim), (pairs, seq, PAIR), (pairs, PAIR, seq)
    hidden, block = (mb, seq, ff), (mb, block_rows, dim)
    n_k = len(PIECES)
    shape = lambda s, t=BF: jax.ShapeDtypeStruct(s, t)
    vmem = lambda s, t=BF: pltpu.VMEM(s, t)

    def parts(lead, split):
        return (*lead, 3, ff, split), (*lead, ow, split), (*lead, 3, split, cols)

    return pl.pallas_call(
        layer_kernel,
        out_shape=(
            shape(block), shape(block),
            shape((3, quarter, cols)), shape((ow, quarter)), shape((2, ff, quarter)), shape((ff, quarter)),
            shape((2, dim), F32), shape(wide),
            *(shape(s) for s in parts((nx - 1, mb), part)),
            *(shape(s) for s in parts((mb + 1,), part)),
        ),
        in_specs=[ANY, ANY, VMEM, ANY, ANY, ANY, ANY, VMEM, VMEM, VMEM],
        out_specs=(*(ANY,) * 6, VMEM, *(ANY,) * 7),
        scratch_shapes=[
            vmem((mb, 3, dim, cols)), vmem((mb * ow, dim)), vmem((mb, 3, ff, dim)),
            vmem(wide), *[vmem(heads)] * 4, vmem(turned), *[vmem(heads)] * 2,
            vmem((seq, pairs * PAIR)), vmem((pairs, 2, seq), F32), vmem(wide, F32), vmem(wide), *[vmem(hidden)] * 3,
            *[vmem(wide)] * 4, vmem((8, 128), F32), *[vmem(heads, F32)] * 2,
            vmem((nx, ff // 2, part)), vmem((nx, ow, part)), vmem((nx, 3, quarter // 2, cols)),
            vmem((n_t, 2, dim), F32), vmem((nx, 2, dim), F32),
            dma((5,)), dma((mb,)), dma((n_t,)), dma((mb,)), dma((n_t,)), dma((n_t,)), dma((n_t,)), dma((2,)),
            dma((N_PIECES,)), dma((N_PIECES,)), dma((N_PIECES, mb)), dma((N_PIECES, mb)),
            dma((N_PIECES, mb, nx)), dma((N_PIECES, mb, nx)),
            *[dma((2, CHUNKS))] * 5, dma((2,)),
            dma((2,)), dma((2, n_t)), dma((2, mb)), *[dma((2, CHUNKS))] * 5,
            dma((n_k, mb, nx)), dma((n_k, mb, nx)), dma((n_k, mb)), dma((n_k, mb)), *[dma((n_k,))] * 4,
            dma((nx,)), dma((n_t,)), dma((n_t,)), dma((nx,)), dma((nx,)), pltpu.SemaphoreType.REGULAR((2,)),
        ],
        compiler_params=pltpu.CompilerParams(
            collective_id=0, has_side_effects=True, vmem_limit_bytes=63 << 20
        ),
        name="layer",
    )(tokens, cotangent, lens, qkv, out, gu, down, gains, *tables)


def publish_kernel(*refs):
    count = len(refs) // 3
    sources, targets, held, sems = refs[:count], refs[count:2 * count], refs[2 * count:3 * count], refs[-1]
    copies = [pltpu.make_async_copy(src, dst, sems.at[n]) for n, (src, dst) in enumerate(zip(sources, held))]
    for copy in copies:
        copy.start()
    for copy, dst, src in zip(copies[:-1], targets, held):
        copy.wait()
        dst[...] = src[...].astype(dst.dtype)
    copies[-1].wait()
    dim, share = held[-1].shape[1], targets[-1].shape[1]
    place = lax.axis_index("dp") * lax.axis_size("tensor") + lax.axis_index("tensor")
    targets[-1][...] = pltpu.roll(held[-1][...], lax.rem(dim - place * share, dim), 1)[:, :share]


def publish(*arrays):
    types = (BF,) + (F32,) * (len(arrays) - 1)
    gain = arrays[-1]
    shapes = [a.shape for a in arrays[:-1]]
    shapes.append((2, gain.shape[1] // (lax.axis_size("dp") * lax.axis_size("tensor"))))
    return pl.pallas_call(
        publish_kernel,
        out_shape=tuple(jax.ShapeDtypeStruct(a, t) for a, t in zip(shapes, types)),
        in_specs=[ANY] * len(arrays),
        out_specs=(VMEM,) * len(arrays),
        scratch_shapes=[*(pltpu.VMEM(a.shape, a.dtype) for a in arrays), pltpu.SemaphoreType.DMA((len(arrays),))],
        compiler_params=pltpu.CompilerParams(vmem_limit_bytes=60 << 20),
        name="publish",
    )(*arrays)


def shards(tokens, lengths, qkv_weight, out_weight, gate_up_weight, down_weight, norm_gains, cotangent):
    mb, rows, _ = tokens.shape
    n_t = lax.axis_size("tensor")
    tables = tuple(jnp.asarray(t) for t in rope_tables(rows * n_t))
    lens = jnp.broadcast_to(lengths.astype(F32)[:, None, None], (mb, 8, 128))
    o_y, o_dx, o_qkv, o_out, o_gu, o_down, gain = layer(
        tokens, cotangent, lens, qkv_weight, out_weight, jnp.swapaxes(gate_up_weight, 2, 3), down_weight,
        norm_gains[0], tables,
    )[:7]
    o_y, o_dx, o_qkv, o_out, o_gu, o_down, gain = publish(o_y, o_dx, o_qkv, o_out, o_gu, o_down, gain)
    return (
        o_y[None], o_dx[None], o_qkv[None], o_out[None], jnp.swapaxes(o_gu, 1, 2)[None], o_down[None],
        gain[None],
    )


def solution(mesh):
    in_specs = (
        P("dp", "tensor", None),
        P("dp"),
        P("section", None, None, "tensor"),
        P("section", "tensor", None),
        P("section", None, None, "tensor"),
        P("section", "tensor", None),
        P("section", None, None),
        P("dp", "tensor", None),
    )
    out_specs = (
        P("section", "dp", "tensor", None),
        P("section", "dp", "tensor", None),
        P("section", None, "dp", "tensor"),
        P("section", "tensor", "dp"),
        P("section", None, "dp", "tensor"),
        P("section", "tensor", "dp"),
        P("section", None, ("dp", "tensor")),
    )
    return jax.shard_map(shards, mesh=mesh, in_specs=in_specs, out_specs=out_specs, check_vma=False)
```

```python
import jax
import jax.numpy as jnp
import numpy as np
from jax import lax
from jax.experimental import pallas as pl
from jax.experimental.pallas import tpu as pltpu
from jax.sharding import PartitionSpec as P

MESH = pl.DeviceIdType.MESH
ANY = pl.BlockSpec(memory_space=pl.ANY)
VMEM = pl.BlockSpec(memory_space=pltpu.VMEM)
NORM_EPS = 1e-6
ROPE_BASE = 10000.0
SCORE_SCALE = 0.125
MASK_VALUE = -1e30
HD = 64
PAIR = 2 * HD
CHUNKS = 4
NT = (((1,), (1,)), ((), ()))
BF, F32 = jnp.bfloat16, jnp.float32

QKV, OUT, GU, DOWN = range(4)
COUNT = (2, 1, 4, 2)
BASE = (0, 2, 3, 7)
N_PIECES = 9


def dot(a, b):
    return jnp.dot(a, b, preferred_element_type=F32)


def dot_nt(a, b):
    return lax.dot_general(a, b, NT, preferred_element_type=F32)


def dot_tn(a, b):
    return lax.dot_general(a, b, (((0,), (0,)), ((), ())), preferred_element_type=F32)


def remote(src, dst, send, recv, to):
    return pltpu.make_async_remote_copy(
        src_ref=src, dst_ref=dst, send_sem=send, recv_sem=recv, device_id=to, device_id_type=MESH
    )


class Place:
    def __init__(self, mb):
        self.n_t = lax.axis_size("tensor")
        self.nx = lax.axis_size("dp") // 2
        self.section = lax.axis_index("section")
        dp = lax.axis_index("dp")
        self.z = lax.axis_index("tensor")
        self.x, self.c = dp // 2, lax.rem(dp, 2)
        self.here = self.z // mb == self.c
        self.jz = self.z - self.c * mb
        self.sibling = {"dp": 2 * self.x + 1 - self.c}
        self.right, self.left = {"tensor": self.z + 1}, {"tensor": self.z - 1}

    def at_x(self, d):
        return {"dp": 2 * lax.rem(self.x + d, self.nx) + self.c}

    def meet(self):
        barrier = pltpu.get_barrier_semaphore()
        partners = [{"tensor": lax.rem(self.z + k, self.n_t)} for k in range(1, self.n_t)]
        partners += [self.at_x(k) for k in range(1, self.nx)]
        partners += [self.sibling, {"section": 1 - self.section}]
        for partner in partners:
            pl.semaphore_signal(barrier, inc=1, device_id=partner, device_id_type=MESH)
        pl.semaphore_wait(barrier, len(partners))


def rope_tables(positions):
    lane = np.arange(PAIR)
    frequency = ROPE_BASE ** (-(lane % (HD // 2)) * 2.0 / HD)
    angles = np.arange(positions)[:, None] * frequency[None, :]
    sign = np.where(lane % HD < HD // 2, -1.0, 1.0)
    return np.cos(angles).astype(np.float32), (np.sin(angles) * sign).astype(np.float32)


def rotate_pair(values, cos, sin):
    lane = lax.broadcasted_iota(jnp.int32, values.shape, 1)
    partner = jnp.where(
        lax.rem(lane, HD) < HD // 2,
        pltpu.roll(values, PAIR - HD // 2, 1),
        pltpu.roll(values, HD // 2, 1),
    )
    return values * cos + partner * sin


def normalise(values):
    return values * lax.rsqrt(jnp.mean(values * values, axis=-1, keepdims=True) + NORM_EPS)


def head_views(h, shape):
    lane = lax.broadcasted_iota(jnp.int32, shape, 1)
    return lane // HD == h, lane == (1 - h) * HD


def causal_block(blk):
    key = lax.broadcasted_iota(jnp.int32, (blk, blk), 0)
    query = lax.broadcasted_iota(jnp.int32, (blk, blk), 1)
    return key <= query


def head_keys(keys, length, first_row):
    position = (first_row + lax.broadcasted_iota(jnp.int32, keys.shape, 0)).astype(F32)
    bias = jnp.where(position < length, 0.0, MASK_VALUE)
    views = []
    for h in range(2):
        inside, extra = head_views(h, keys.shape)
        views.append(jnp.where(inside, keys, jnp.where(extra, bias, 0.0)).astype(BF))
    return views


def head_queries(h, queries, mark):
    inside, extra = head_views(h, queries.shape)
    return jnp.where(inside, queries, jnp.where(extra, mark, 0.0)).astype(BF)


def attend_block(i, blk, queries, keys, vals_t, put_out, put_lse):
    lo, hi = i * blk, (i + 1) * blk
    visible = causal_block(blk)
    queries = queries.astype(F32)
    parts = []
    for h in range(2):
        qi = head_queries(h, queries, 1.0)
        vh = slice(h * HD, (h + 1) * HD)
        s_diag = jnp.where(visible, dot_nt(keys(h, lo, hi), qi), MASK_VALUE)
        top = jnp.max(s_diag, axis=0, keepdims=True)
        if i:
            s_full = dot_nt(keys(h, 0, lo), qi)
            top = jnp.maximum(top, jnp.max(s_full, axis=0, keepdims=True))
        p_diag = jnp.exp(s_diag - top)
        total = jnp.sum(p_diag, axis=0, keepdims=True)
        acc = dot(vals_t(vh, lo, hi), p_diag.astype(BF))
        if i:
            p_full = jnp.exp(s_full - top)
            total = total + jnp.sum(p_full, axis=0, keepdims=True)
            acc = acc + dot(vals_t(vh, 0, lo), p_full.astype(BF))
        parts.append(acc / total)
        put_lse(h, lo, hi, top + jnp.log(total))
    put_out(lo, hi, jnp.concatenate(parts, axis=0).T.astype(BF))


def forward_part(
    me, tok, cot, lens, qkv, out, gu, down, gains, cos, sin, tok_o,
    w_qkv, w_out, w_ff, x_v, first, q_v, ka_v, kb_v, vt_v, v_v, vu_v, o_v, lse_v, h_v, b_v, g_v, u_v, m_v,
    s1, r1, r2, dmo, len_v,
    loc, a2a_s, a2a_r, c2a_s, c2a_r, y_s, y_r, sib, own_r, own_l, z_r, z_f, x_s, x_r, hop, hsib, e1, e2, vsem, lsem,
):
    mb, block_rows, dim = tok.shape
    x, c, z, n_t, nx, jz = me.x, me.c, me.z, me.n_t, me.nx, me.jz
    part = dim // nx
    cols, ow, half = qkv.shape[3], out.shape[1], down.shape[1] // 2
    seq = x_v.shape[0]
    rows = seq // CHUNKS
    pairs = q_v.shape[0]
    first_plane, second_plane = me.section == 0, me.section == 1

    def column(p):
        return pl.ds(pl.multiple_of(p * part, 128), part)

    def shard_part(w, n, p):
        if w == QKV:
            return qkv.at[0, :, pl.ds(pl.multiple_of(p * part + n * (part // 2), 16), part // 2), :]
        if w == OUT:
            return out.at[0, :, column(p)]
        if w == GU:
            return gu.at[0, n // 2, pl.ds(pl.multiple_of(lax.rem(n, 2) * half, 16), half), column(p)]
        return down.at[0, pl.ds(n * half, half), column(p)]

    def slot_part(w, n, j, p):
        if w == QKV:
            return w_qkv.at[j, :, pl.ds(pl.multiple_of(p * part + n * (part // 2), 16), part // 2), :]
        if w == OUT:
            return w_out.at[pl.ds(pl.multiple_of(j * ow, 16), ow), column(p)]
        if w == GU:
            return w_ff.at[j, 1 + n // 2, pl.ds(pl.multiple_of(lax.rem(n, 2) * half, 16), half), column(p)]
        return w_ff.at[j, 0, pl.ds(n * half, half), column(p)]

    own_slots = (
        (qkv.at[0], w_qkv.at[jz]),
        (out.at[0], w_out.at[pl.ds(pl.multiple_of(jz * ow, 16), ow), :]),
        (gu.at[0], w_ff.at[jz, 1:3]),
        (down.at[0], w_ff.at[jz, 0]),
    )

    def own_copies(w, n):
        k = BASE[w] + n
        src, dst = shard_part(w, n, x), slot_part(w, n, jz, x)
        return (
            (z < n_t - 1, remote(src, dst, own_r.at[k], z_r.at[k, jz], me.right)),
            (z > 0, remote(src, dst, own_l.at[k], z_r.at[k, jz], me.left)),
        )

    def own_start(w, n):
        @pl.when(me.here)
        def _():
            for there, copy in own_copies(w, n):
                pl.when(there)(copy.start)

    def own_wait(w, n):
        @pl.when(me.here)
        def _():
            for there, copy in own_copies(w, n):
                pl.when(there)(copy.wait_send)

    def order(i):
        return jnp.where(c == 0, mb - 1 - i, i)

    def foreign(w, n, i):
        j = order(i)
        s = c * mb + j
        k = BASE[w] + n

        @pl.when(s != z)
        def _():
            piece = slot_part(w, n, j, x)
            to_right = remote(piece, piece, z_f.at[k, j], z_r.at[k, j], me.right)
            to_left = remote(piece, piece, z_f.at[k, j], z_r.at[k, j], me.left)
            to_right.wait_recv()
            pl.when((s < z) & (z < n_t - 1))(to_right.start)
            pl.when((s > z) & (z > 0))(to_left.start)
            for d in range(1, nx):
                remote(piece, piece, x_s.at[k, j, d], x_r.at[k, j, x], me.at_x(d)).start()

    def wait_slot(w, j):
        s = c * mb + j

        @pl.when(s != z)
        def _():
            for n in range(COUNT[w]):
                k = BASE[w] + n
                for d in range(1, nx):
                    p = lax.rem(x + d, nx)
                    piece = slot_part(w, n, j, p)
                    remote(piece, piece, x_s.at[k, j, d], x_r.at[k, j, p], me.right).wait_recv()

    def gu_step(n, i):
        if i == 0:
            @pl.when(n >= 2)
            def _():
                own_wait(GU, n - 2)
            own_start(GU, n)
        foreign(GU, n, i)

    def down_steps(i):
        for n in range(COUNT[DOWN]):
            if i == 0:
                own_wait(GU, n + 2)
                own_start(DOWN, n)
            foreign(DOWN, n, i)

    def block_at(n):
        return pl.ds(pl.multiple_of(n * block_rows, 128), block_rows)

    block = block_at(z)
    other_plane = {"section": 1 - me.section}

    def spread(source, target, send, recv):
        for i in range(mb):
            zt = c * mb + i

            @pl.when(zt != z)
            def _(i=i, zt=zt):
                remote(source.at[i], target.at[block, :], send.at[i], recv.at[z], {"tensor": zt}).start()

    def arrived(target, zs, recv):
        there = target.at[block_at(zs), :]
        return remote(there, there, recv.at[zs], recv.at[zs], me.right)

    def to_first(zs):
        return remote(tok_o.at[block_at(zs), :], x_v.at[block_at(zs), :], y_s.at[zs], y_r.at[zs], other_plane)

    pl.when(second_plane)(lambda: spread(tok, tok_o, a2a_s, a2a_r))
    for i in range(mb):
        @pl.when(first_plane & (c * mb + i == z))
        def _(i=i):
            pltpu.make_async_copy(tok.at[i], x_v.at[block, :], loc.at[4]).start()

    @pl.when(me.here)
    def _():
        remote(lens.at[jz], len_v, lsem.at[0], lsem.at[1], me.sibling).start()
        len_v[...] = lens[jz]
        for w, (src, dst) in enumerate(own_slots):
            pltpu.make_async_copy(src, dst, loc.at[w]).start()

    own_start(QKV, 0)
    own_start(QKV, 1)
    for w, n in ((QKV, 0), (QKV, 1), (OUT, 0)):
        if w == OUT:
            own_wait(QKV, 0)
            own_start(OUT, 0)
        for i in range(mb):
            foreign(w, n, i)
        if (w, n) == (QKV, 1):
            @pl.when(second_plane & me.here)
            def _():
                for zs in range(n_t):
                    @pl.when(zs != z)
                    def _(zs=zs):
                        arrived(tok_o, zs, a2a_r).wait_recv()
                        to_first(zs).start()

    def ff_steps(i):
        @pl.loop(0, COUNT[GU])
        def _(n):
            gu_step(n, i)
        down_steps(i)

    @pl.when(second_plane)
    def _():
        for i in range(mb):
            ff_steps(i)
        spread(cot, dmo, c2a_s, c2a_r)
        for i in range(mb):
            @pl.when(c * mb + i == z)
            def _(i=i):
                pltpu.make_async_copy(cot.at[i], dmo.at[block, :], loc.at[4]).start()

    @pl.when(first_plane & me.here)
    def _():
        for zs in range(n_t):
            @pl.when(zs != z)
            def _(zs=zs):
                to_first(zs).wait_recv()
        pltpu.make_async_copy(tok.at[0], x_v.at[block, :], loc.at[4]).wait()
        remote(x_v, x_v, sib.at[0], sib.at[1], me.sibling).start()

    @pl.when(jnp.logical_not(me.here))
    def _():
        remote(len_v, len_v, lsem.at[0], lsem.at[1], me.sibling).wait_recv()
        pl.when(first_plane)(remote(x_v, x_v, sib.at[0], sib.at[1], me.sibling).wait_recv)

    length = len_v[0:1, :]

    @pl.when(me.here)
    def _():
        for w, (src, dst) in enumerate(own_slots):
            pltpu.make_async_copy(src, dst, loc.at[w]).wait()

    for j in range(mb):
        wait_slot(QKV, j)
        wait_slot(OUT, j)

    gain_one, gain_two = gains[0:1, :], gains[1:2, :]

    def chunk(r):
        return pl.ds(pl.multiple_of(r * rows, 128), rows)

    def halves(r, core):
        return x_v.at[pl.ds(pl.multiple_of(r * rows + core * (rows // 2), 16), rows // 2), :]

    def send_v(r):
        return remote(v_v.at[:, chunk(r), :], first.at[:, chunk(r), :], vsem.at[0, r], vsem.at[1, r], other_plane)

    def swap(buffer, r, sems):
        return remote(s1.at[chunk(r), :], buffer.at[chunk(r), :], sems.at[0, r], sems.at[1, r], me.sibling)

    def project(r):
        at = chunk(r)
        a = (normalise(x_v[at, :].astype(F32)) * gain_one).astype(BF)
        cos_r, sin_r = cos[at, :], sin[at, :]
        for j in range(mb):
            q = dot(a, w_qkv[j, 0])
            k = dot(a, w_qkv[j, 1])
            v = dot(a, w_qkv[j, 2])
            for n in range(cols // PAIR):
                p = j * (cols // PAIR) + n
                lanes = slice(n * PAIR, (n + 1) * PAIR)
                q_v[p, at, :] = (rotate_pair(q[:, lanes], cos_r, sin_r) * SCORE_SCALE).astype(BF)
                keys = rotate_pair(k[:, lanes], cos_r, sin_r).astype(BF).astype(F32)
                ka_v[p, at, :], kb_v[p, at, :] = head_keys(keys, length, r * rows)
                v_v[p, at, :] = v[:, lanes].astype(BF)

        @pl.when(first_plane)
        def _():
            send_v(r).start()
            for p in range(pairs):
                vals = v_v[p, at, :]
                vu_v[p, at, :] = vals
                vt_v[p, :, at] = vals.astype(F32).T.astype(BF)

        @pl.when(second_plane)
        def _():
            send_v(r).wait_recv()
            for p in range(pairs):
                vals = (0.5 * v_v[p, at, :].astype(F32) + 0.5 * first[p, at, :].astype(F32)).astype(BF)
                vu_v[p, at, :] = vals
                vt_v[p, :, at] = vals.astype(F32).T.astype(BF)

    def attention(r):
        for i in range(CHUNKS):
            @pl.when(r == i)
            def _(i=i):
                @pl.loop(0, pairs, unroll=2)
                def _(p):
                    lanes = pl.ds(pl.multiple_of(p * PAIR, PAIR), PAIR)

                    def put_out(lo, hi, value):
                        o_v[lo:hi, lanes] = value

                    def put_lse(h, lo, hi, value):
                        lse_v[p, h:h + 1, lo:hi] = value

                    attend_block(
                        i, rows, q_v[p, i * rows:(i + 1) * rows, :],
                        lambda h, lo, hi: (ka_v, kb_v)[h][p, lo:hi, :],
                        lambda vh, lo, hi: vt_v[p, vh, lo:hi],
                        put_out, put_lse,
                    )

    def enter(r):
        at = chunk(r)
        swap(r1, r, e1).wait_recv()
        h = x_v[at, :].astype(F32) + s1[at, :].astype(F32) + r1[at, :].astype(F32)
        h_v[at, :] = h
        b_v[at, :] = (normalise(h) * gain_two).astype(BF)
        swap(r1, r, e1).wait_send()

    def through_slot(r, j):
        at = chunk(r)
        b = b_v[at, :]
        gate = dot_nt(b, w_ff[j, 1])
        up = dot_nt(b, w_ff[j, 2])
        m = (gate / (1.0 + jnp.exp(-gate)) * up).astype(BF)
        g_v[j, at, :] = gate.astype(BF)
        u_v[j, at, :] = up.astype(BF)
        m_v[j, at, :] = m
        return dot(m, w_ff[j, 0])

    def leave(r, grown):
        s1[chunk(r), :] = grown.astype(BF)
        swap(r2, r, e2).start()

    def finish(r):
        at = chunk(r)
        swap(r2, r, e2).wait_recv()
        r2[at, :] = (h_v[at, :] + s1[at, :].astype(F32) + r2[at, :].astype(F32)).astype(BF)

        @pl.when(first_plane)
        def _():
            mine = pl.ds(pl.multiple_of(r * rows + c * (rows // 2), 16), rows // 2)
            remote(
                r2.at[mine, :], x_v.at[mine, :], hop.at[0, r], hop.at[1, r], other_plane
            ).start()

    def finish_before(r):
        @pl.when(r > 0)
        def _():
            finish(r - 1)

    def mix_all(r):
        enter(r)
        leave(r, sum(through_slot(r, j) for j in range(mb)))
        finish_before(r)

    @pl.when(second_plane)
    def _():
        for j in range(mb):
            wait_slot(GU, j)
            wait_slot(DOWN, j)

    @pl.loop(0, CHUNKS)
    def _(r):
        @pl.when(first_plane)
        def _():
            gu_step(r, 0)

        @pl.when(second_plane)
        def _():
            mine, theirs = halves(r, c), halves(r, 1 - c)
            remote(mine, mine, hop.at[0, r], hop.at[1, r], me.sibling).wait_recv()
            remote(mine, mine, hsib.at[0, r], hsib.at[1, r], me.sibling).start()
            remote(theirs, theirs, hsib.at[0, r], hsib.at[1, r], me.sibling).wait_recv()

        @pl.when(second_plane & me.here & (r == CHUNKS - 1))
        def _():
            for zs in range(n_t):
                @pl.when(zs != z)
                def _(zs=zs):
                    arrived(dmo, zs, c2a_r).wait_recv()
            pltpu.make_async_copy(cot.at[0], dmo.at[block, :], loc.at[4]).wait()
            remote(dmo, dmo, sib.at[0], sib.at[1], me.sibling).start()

        project(r)
        attention(r)
        s1[chunk(r), :] = dot(o_v[chunk(r), :], w_out[...]).astype(BF)
        swap(r1, r, e1).start()

        @pl.when(second_plane & (r > 0))
        def _():
            mix_all(r - 1)

    pl.when(second_plane)(lambda: mix_all(CHUNKS - 1))

    @pl.when(first_plane)
    def _():
        down_steps(0)
        for i in range(1, mb - 1):
            ff_steps(i)
        for i in range(mb - 1):
            wait_slot(GU, order(i))
            wait_slot(DOWN, order(i))

        @pl.loop(0, CHUNKS)
        def _(r):
            gu_step(r, mb - 1)
            enter(r)
            s1[chunk(r), :] = sum(through_slot(r, order(i)) for i in range(mb - 1)).astype(BF)

        down_steps(mb - 1)
        wait_slot(GU, order(mb - 1))
        wait_slot(DOWN, order(mb - 1))

        @pl.loop(0, CHUNKS)
        def _(r):
            leave(r, s1[chunk(r), :].astype(F32) + through_slot(r, order(mb - 1)))
            finish_before(r)

    finish(CHUNKS - 1)
    for w, n in ((QKV, 1), (OUT, 0), (DOWN, 0), (DOWN, 1)):
        own_wait(w, n)
    for w in range(4):
        for n in range(COUNT[w]):
            k = BASE[w] + n
            for j in range(mb):
                s = c * mb + j

                @pl.when(s != z)
                def _(w=w, n=n, k=k, j=j, s=s):
                    piece = slot_part(w, n, j, x)
                    for d in range(1, nx):
                        remote(piece, piece, x_s.at[k, j, d], x_r.at[k, j, x], me.right).wait_send()
                    forwarded = ((s < z) & (z < n_t - 1)) | ((s > z) & (z > 0))
                    pl.when(forwarded)(remote(piece, piece, z_f.at[k, j], z_r.at[k, j], me.right).wait_send)

    @pl.when(second_plane)
    def _():
        for i in range(mb):
            @pl.when(c * mb + i != z)
            def _(i=i):
                remote(tok.at[i], tok.at[i], a2a_s.at[i], a2a_r.at[z], me.right).wait_send()
                remote(tok.at[i], tok.at[i], c2a_s.at[i], c2a_r.at[z], me.right).wait_send()

        @pl.when(me.here)
        def _():
            for zs in range(n_t):
                @pl.when(zs != z)
                def _(zs=zs):
                    to_first(zs).wait_send()

    @pl.when(me.here)
    def _():
        remote(lens.at[jz], len_v, lsem.at[0], lsem.at[1], me.sibling).wait_send()
        pl.when(first_plane)(remote(x_v, x_v, sib.at[0], sib.at[1], me.sibling).wait_send)
        pl.when(second_plane)(remote(dmo, dmo, sib.at[0], sib.at[1], me.sibling).wait_send)

    @pl.when(second_plane & jnp.logical_not(me.here))
    def _():
        remote(dmo, dmo, sib.at[0], sib.at[1], me.sibling).wait_recv()

    for r in range(CHUNKS):
        swap(r2, r, e2).wait_send()
        pl.when(first_plane)(send_v(r).wait_send)
        mine = halves(r, c)
        pl.when(first_plane)(remote(mine, mine, hop.at[0, r], hop.at[1, r], me.sibling).wait_send)
        pl.when(second_plane)(remote(mine, mine, hsib.at[0, r], hsib.at[1, r], me.sibling).wait_send)


LAG = 1
AHEAD = 3
FF, OUTS, HEADS = range(3)
FF_PIECES = 6
PIECES = [(FF, n) for n in range(FF_PIECES)] + [(OUTS, 0)] + [(HEADS, n) for n in range(4)]
KEY = (0, FF_PIECES, FF_PIECES + 1)


def attend_back_block(i, blk, queries, keys, keys_t, vals, outs, grads, stats, add_dv, add_dk):
    lo, hi = i * blk, (i + 1) * blk
    visible = causal_block(blk)
    queries, grads = queries.astype(F32), grads.astype(F32)
    product = (grads * outs.astype(F32)).T
    parts = []
    for h in range(2):
        qh, qz, gh = head_queries(h, queries, 1.0), head_queries(h, queries, 0.0), head_queries(h, grads, 0.0)
        rows_h = slice(h * HD, (h + 1) * HD)
        delta = jnp.sum(product[rows_h], axis=0, keepdims=True)
        stat = stats(h, lo, hi)

        def side(a, b, diagonal):
            p = jnp.exp(dot_nt(keys(h, a, b), qh) - stat)
            if diagonal:
                p = jnp.where(visible, p, 0.0)
            ds = (p * (dot_nt(vals(a, b), gh) - delta)).astype(BF)
            fresh = i == CHUNKS - 1 and h == 0
            add_dv(a, b, dot(p.astype(BF), gh), fresh)
            add_dk(a, b, dot(ds, qz), fresh)
            return dot(keys_t(rows_h, a, b), ds)

        dq_t = side(lo, hi, True)
        if i:
            dq_t = dq_t + side(0, lo, False)
        parts.append(dq_t)
    return jnp.concatenate(parts, axis=0).T * SCORE_SCALE


def norm_back(values, gain, grad):
    scale = lax.rsqrt(jnp.mean(values * values, axis=-1, keepdims=True) + NORM_EPS)
    unit = values * scale
    inner = grad * gain
    back = scale * (inner - unit * jnp.mean(inner * unit, axis=-1, keepdims=True))
    return back, jnp.sum(grad * unit, axis=0, keepdims=True)


def backward_part(
    me, gains, cos, sin, o_y, o_dx, o_qkv, o_out, o_gu, o_down, o_gain, lx_ff, lx_out, lx_qkv, lz_ff, lz_out, lz_qkv,
    w_qkv, w_out, w_ff, x_v, q_v, ka_v, kb_v, kt_v, vu_v, o_v, lse_v, h_v, b_v, g_v, u_v, m_v,
    dmo, do_v, first, s1, r1, r2, len_v, dk_a, dv_a, st_ff, st_out, st_qkv, g_z, g_x,
    loc, a2a_s, a2a_r, hop, hsib, e1, e2, vsem, x_s, x_r, z_s, z_r, zo_r, f_s, f_r, f_l, stage, gz_s, gz_r, gx_s, gx_r,
    free,
):
    mb, block_rows, dim = o_y.shape
    x, c, z, n_t, nx, jz = me.x, me.c, me.z, me.n_t, me.nx, me.jz
    part = dim // nx
    quarter, eighth = part // 2, part // 4
    cols, ow, half = w_qkv.shape[3], w_out.shape[0] // mb, w_ff.shape[2] // 2
    seq = x_v.shape[0]
    rows = seq // CHUNKS
    pairs = q_v.shape[0]
    slot_pairs = cols // PAIR
    first_plane, second_plane = me.section == 0, me.section == 1
    other_plane = {"section": 1 - me.section}

    def block(n):
        return pl.ds(pl.multiple_of(n * block_rows, 128), block_rows)

    def give_back(t, src, dst):
        @pl.when(me.here)
        def _():
            for d in range(1, n_t):
                to = lax.rem(z + d, n_t)
                remote(src.at[block(to), :], dst.at[jz], a2a_s.at[t, d], a2a_r.at[t, jz], {"tensor": to}).start()
            pltpu.make_async_copy(src.at[block(z), :], dst.at[jz], loc.at[t]).start()

    give_back(0, r2, o_y)

    def chunk(r):
        return pl.ds(pl.multiple_of(r * rows, 128), rows)

    def half_rows(r, core):
        return dmo.at[pl.ds(pl.multiple_of(r * rows + core * (rows // 2), 16), rows // 2), :]

    def swap(buffer, r, sems):
        return remote(s1.at[chunk(r), :], buffer.at[chunk(r), :], sems.at[0, r], sems.at[1, r], me.sibling)

    gain_one, gain_two = gains[0:1, :], gains[1:2, :]
    o_gain[...] = jnp.zeros_like(o_gain)

    def buffers_free(n):
        pl.semaphore_signal(free.at[n], inc=1, device_id=me.sibling, device_id_type=MESH)

    def y_sent():
        @pl.when(me.here)
        def _():
            for d in range(1, n_t):
                there = r2.at[block(0), :]
                remote(there, o_y.at[0], a2a_s.at[0, d], a2a_r.at[0, jz], me.right).wait_send()
            pltpu.make_async_copy(r2.at[block(z), :], o_y.at[jz], loc.at[0]).wait()

    buffers_free(0)
    pl.semaphore_wait(free.at[0], 1)

    def finish_mixed(r):
        at = chunk(r)
        swap(r1, r, e1).wait_recv()
        db = s1[at, :].astype(F32) + r1[at, :].astype(F32)
        back, gain = norm_back(h_v[at, :], gain_two, db)
        o_gain[1:2, :] += gain
        dh = dmo[at, :].astype(F32) + back
        h_v[at, :] = dh
        back_out = dot_nt(dh.astype(BF), w_out[...]).astype(BF)
        for p in range(pairs):
            do_v[p, at, :] = back_out[:, p * PAIR:(p + 1) * PAIR]

    def expand(r):
        at = chunk(r)

        @pl.when(first_plane)
        def _():
            mine, theirs = half_rows(r, c), half_rows(r, 1 - c)
            remote(mine, mine, hop.at[0, r], hop.at[1, r], me.sibling).wait_recv()
            remote(mine, mine, hsib.at[0, r], hsib.at[1, r], me.sibling).start()
            remote(theirs, theirs, hsib.at[0, r], hsib.at[1, r], me.sibling).wait_recv()

        @pl.when(second_plane)
        def _():
            position = (r * rows + lax.broadcasted_iota(jnp.int32, (rows, dim), 0)).astype(F32)
            dmo[at, :] = jnp.where(position < len_v[0:1, 0:1], dmo[at, :].astype(F32), 0.0).astype(BF)

        dy = dmo[at, :]
        total = None
        for j in range(mb):
            dm = dot_nt(dy, w_ff[j, 0])
            gate, up = g_v[j, at, :].astype(F32), u_v[j, at, :].astype(F32)
            sig = 1.0 / (1.0 + jnp.exp(-gate))
            d_gate = (dm * up * (sig * (1.0 + gate * (1.0 - sig)))).astype(BF)
            d_up = (dm * (gate * sig)).astype(BF)
            g_v[j, at, :] = d_gate
            u_v[j, at, :] = d_up
            term = dot(d_gate, w_ff[j, 1]) + dot(d_up, w_ff[j, 2])
            total = term if total is None else total + term
        s1[at, :] = total.astype(BF)
        swap(r1, r, e1).start()

    def ff_grads(t):
        left = (m_v, g_v, u_v)[t]
        right = (dmo, b_v, b_v)[t]

        @pl.loop(0, mb)
        def _(j):
            @pl.loop(0, 2)
            def _(n):
                lanes = pl.ds(pl.multiple_of(n * (dim // 2), 128), dim // 2)
                w_ff[j, t, :, lanes] = dot_tn(left[j], right[:, lanes]).astype(BF)

    def column(p):
        return pl.ds(pl.multiple_of(p * part, 128), part)

    def order(i):
        return jnp.where(c == 0, i, mb - 1 - i)

    def key(kind, n):
        return KEY[kind] + n

    def half_of(n):
        return pl.ds(pl.multiple_of(lax.rem(n, 2) * half, 16), half)

    def grad_part(kind, n, j, p):
        if kind == FF:
            return w_ff.at[j, n // 2, half_of(n), column(p)]
        if kind == OUTS:
            return w_out.at[pl.ds(pl.multiple_of(j * ow, 16), ow), column(p)]
        return w_qkv.at[j, :, pl.ds(pl.multiple_of(p * part + n * eighth, 16), eighth), :]

    def landing(bufs, kind, n, slot):
        if kind == FF:
            return bufs[FF].at[slot, n // 2, half_of(n), :]
        if kind == OUTS:
            return bufs[OUTS].at[slot]
        return bufs[HEADS].at[slot, :, pl.ds(n * eighth, eighth), :]

    def land_x(kind, n, j, d):
        return landing([b.at[d - 1] for b in (lx_ff, lx_out, lx_qkv)], kind, n, j)

    def land_z(kind, n, slot):
        return landing((lz_ff, lz_out, lz_qkv), kind, n, slot)

    def staged(kind, slot):
        return (st_ff, st_out, st_qkv)[kind].at[slot]

    def x_copies(kind, n, j):
        k = key(kind, n)
        for d in range(1, nx):
            to = lax.rem(x + d, nx)
            yield d, remote(
                grad_part(kind, n, j, to), land_x(kind, n, j, d), x_s.at[k, j, d], x_r.at[k, j, d], me.at_x(d)
            )

    def x_start(kind, n, i):
        for _, copy in x_copies(kind, n, order(i)):
            copy.start()

    def reduce_step(kind, n, i):
        k, j = key(kind, n), order(i)
        s = c * mb + j
        mine = grad_part(kind, n, j, x)
        outer = ((s > z) & (z > 0)) | ((s < z) & (z < n_t - 1))
        fetch = [pltpu.make_async_copy(land_x(kind, n, j, d), staged(kind, d - 1), stage.at[d - 1]) for d in range(1, nx)]
        from_z = land_z(kind, n, j)
        fetch_z = pltpu.make_async_copy(from_z, staged(kind, nx - 1), stage.at[nx - 1])
        for d, copy in x_copies(kind, n, j):
            copy.wait_recv()
            fetch[d - 1].start()

        @pl.when(outer)
        def _():
            remote(from_z, from_z, z_s.at[k, j], z_r.at[k, j], me.right).wait_recv()
            fetch_z.start()

        for copy in fetch:
            copy.wait()
        total = mine[...].astype(F32)
        for d in range(1, nx):
            total = total + staged(kind, d - 1)[...].astype(F32)
        mine[...] = total.astype(BF)

        @pl.when(outer)
        def _():
            fetch_z.wait()
            mine[...] = (mine[...].astype(F32) + staged(kind, nx - 1)[...].astype(F32)).astype(BF)

        pl.when(s > z)(remote(mine, land_z(kind, n, j), z_s.at[k, j], z_r.at[k, j], me.right).start)
        pl.when(s < z - 1)(remote(mine, land_z(kind, n, j), z_s.at[k, j], z_r.at[k, j], me.left).start)
        pl.when(s == z - 1)(remote(mine, land_z(kind, n, mb), z_s.at[k, j], zo_r.at[k], me.left).start)

    def final_part(kind, n):
        if kind == FF:
            return o_down.at[half_of(n), :] if n < 2 else o_gu.at[n // 2 - 1, half_of(n), :]
        return o_out if kind == OUTS else o_qkv.at[:, pl.ds(n % 2 * eighth, eighth), :]

    def final_copies(kind, n):
        k, target, mine = key(kind, n), final_part(kind, n), grad_part(kind, n, jz, x)
        cases = []
        for core in range(2):
            if kind == HEADS:
                stays = theirs = mine
            else:
                stays = mine.at[:, core * quarter:(core + 1) * quarter]
                theirs = mine.at[:, (1 - core) * quarter:(2 - core) * quarter]
            if kind != HEADS or core == n // 2:
                cases.append((c == core, pltpu.make_async_copy(stays, target, f_l.at[k]), True))
            if kind != HEADS or core != n // 2:
                cases.append((c == core, remote(theirs, target, f_s.at[k], f_r.at[k], me.sibling), False))
        return cases

    def own_piece(kind, n):
        k = key(kind, n)
        mine = grad_part(kind, n, jz, x)

        @pl.when(me.here)
        def _():
            sides = ((z > 0, land_z(kind, n, jz), z_r.at[k, jz], 0), (z < n_t - 1, land_z(kind, n, mb), zo_r.at[k], nx - 1))
            for there, src, sem, slot in sides:
                @pl.when(there)
                def _(src=src, sem=sem, slot=slot):
                    remote(src, src, f_s.at[k], sem, me.right).wait_recv()
                    pltpu.make_async_copy(src, staged(kind, slot), stage.at[slot]).start()
            for there, src, sem, slot in sides:
                @pl.when(there)
                def _(src=src, slot=slot):
                    pltpu.make_async_copy(src, staged(kind, slot), stage.at[slot]).wait()
                    mine[...] = (mine[...].astype(F32) + staged(kind, slot)[...].astype(F32)).astype(BF)
            for case, copy, _ in final_copies(kind, n):
                pl.when(case)(copy.start)

    n_k = len(PIECES)

    def ahead(index):
        if index + AHEAD < n_k * mb:
            piece, i = divmod(index + AHEAD, mb)
            x_start(*PIECES[piece], i)

    def begin_reduce():
        for index in range(AHEAD):
            x_start(FF, index // mb, index % mb)

    def ff_round(n):
        for i in range(mb):
            n_next, i_next = n + (i + AHEAD) // mb, (i + AHEAD) % mb

            @pl.when(n_next < FF_PIECES)
            def _(n_next=n_next, i_next=i_next):
                x_start(FF, n_next, i_next)
            reduce_step(FF, n, i)

    def send_dv(r):
        return remote(vu_v.at[:, chunk(r), :], first.at[:, chunk(r), :], vsem.at[0, r], vsem.at[1, r], other_plane)

    def attention(r):
        at = chunk(r)
        for i in range(CHUNKS):
            @pl.when(r == i)
            def _(i=i):
                block_rows_i = slice(i * rows, (i + 1) * rows)

                @pl.loop(0, pairs, unroll=2)
                def _(p):
                    lanes = pl.ds(pl.multiple_of(p * PAIR, PAIR), PAIR)

                    def add_to(acc):
                        def add(a, b, value, fresh):
                            if fresh:
                                acc[p, a:b, :] = value
                            else:
                                acc[p, a:b, :] += value
                        return add

                    dq = attend_back_block(
                        i, rows, q_v[p, block_rows_i, :],
                        lambda h, a, b: (ka_v, kb_v)[h][p, a:b, :],
                        lambda rows_h, a, b: kt_v[p, rows_h, a:b],
                        lambda a, b: vu_v[p, a:b, :],
                        o_v[block_rows_i, lanes], do_v[p, block_rows_i, :],
                        lambda h, lo, hi: lse_v[p, h:h + 1, lo:hi],
                        add_to(dv_a), add_to(dk_a),
                    )
                    q_v[p, block_rows_i, :] = rotate_pair(
                        dq, cos[block_rows_i, :], -sin[block_rows_i, :]
                    ).astype(BF)

        pl.when(first_plane)(lambda: send_dv(r).wait_recv())
        for p in range(pairs):
            ka_v[p, at, :] = rotate_pair(dk_a[p, at, :], cos[at, :], -sin[at, :]).astype(BF)

            @pl.when(first_plane)
            def _(p=p):
                vu_v[p, at, :] = (dv_a[p, at, :] + first[p, at, :].astype(F32)).astype(BF)

            @pl.when(second_plane)
            def _(p=p):
                vu_v[p, at, :] = (0.5 * dv_a[p, at, :]).astype(BF)

    def slot_rows(t, j, at):
        source = (q_v, ka_v, vu_v)[t]
        return jnp.concatenate([source[j * slot_pairs + n, at, :] for n in range(slot_pairs)], axis=1)

    def finish_input(r):
        at = chunk(r)
        swap(r2, r, e2).wait_recv()
        da = s1[at, :].astype(F32) + r2[at, :].astype(F32)
        back, gain = norm_back(x_v[at, :].astype(F32), gain_one, da)
        o_gain[0:1, :] += gain
        r2[at, :] = (h_v[at, :] + back).astype(BF)

        @pl.when(second_plane)
        def _():
            mine = pl.ds(pl.multiple_of(r * rows + c * (rows // 2), 16), rows // 2)
            remote(r2.at[mine, :], dmo.at[mine, :], hop.at[0, r], hop.at[1, r], other_plane).start()

    def input_part(r):
        total = None
        for j in range(mb):
            for t in range(3):
                term = dot_nt(slot_rows(t, j, chunk(r)), w_qkv[j, t])
                total = term if total is None else total + term
        swap(r1, r, e1).wait_send()
        s1[chunk(r), :] = total.astype(BF)
        swap(r2, r, e2).start()

    def back(t):
        return CHUNKS - 1 - t

    @pl.when(first_plane)
    def _():
        @pl.loop(0, CHUNKS)
        def _(t):
            expand(back(t))

            @pl.when(t > 0)
            def _():
                finish_mixed(back(t - 1))

        ff_grads(0)
        begin_reduce()
        finish_mixed(0)
        ff_grads(1)
        ff_grads(2)

    @pl.when(second_plane)
    def _():
        expand(CHUNKS - 1)

    @pl.loop(0, pairs)
    def _(p):
        inside, _ = head_views(0, (seq, PAIR))
        kt_v[p] = jnp.where(inside, ka_v[p].astype(F32), kb_v[p].astype(F32)).T.astype(BF)

    y_sent()
    buffers_free(1)
    pl.semaphore_wait(free.at[1], 1)

    @pl.loop(0, CHUNKS)
    def _(t):
        r = back(t)
        pl.when(first_plane)(lambda: ff_round(t))

        @pl.when(second_plane)
        def _():
            pl.when(t < CHUNKS - 1)(lambda: expand(back(t + 1)))
            finish_mixed(r)

        attention(r)
        input_part(r)

        @pl.when(t > 0)
        def _():
            finish_input(back(t - 1))

    finish_input(0)

    @pl.when(second_plane)
    def _():
        for t in range(CHUNKS):
            send_dv(back(t)).start()

    give_back(1, r2, o_dx)
    for d in range(1, n_t):
        remote(o_gain, g_z.at[d], gz_s.at[d], gz_r.at[d], {"tensor": lax.rem(z + d, n_t)}).start()

    @pl.when(second_plane)
    def _():
        for t in range(3):
            ff_grads(t)
        begin_reduce()

    @pl.loop(0, 4)
    def _(n):
        lanes = pl.ds(pl.multiple_of(n * (dim // 4), 128), dim // 4)
        w_out[:, lanes] = dot_tn(o_v[...], h_v[:, lanes].astype(BF)).astype(BF)

    everything = pl.ds(0, seq)

    @pl.loop(0, CHUNKS)
    def _(r):
        b_v[chunk(r), :] = (normalise(x_v[chunk(r), :].astype(F32)) * gain_one).astype(BF)

    @pl.loop(0, mb)
    def _(j):
        for t in range(3):
            w_qkv[j, t] = dot_tn(b_v[...], slot_rows(t, j, everything)).astype(BF)

    @pl.when(second_plane)
    def _():
        @pl.loop(0, pairs)
        def _(p):
            ff_round(p)

    for index in range(FF_PIECES * mb, min(pairs * mb + AHEAD, n_k * mb)):
        x_start(*PIECES[index // mb], index % mb)
    for piece in range(pairs, n_k):
        for i in range(mb):
            ahead(piece * mb + i)
            reduce_step(*PIECES[piece], i)
        for done in range(piece - LAG) if piece == pairs else (piece - LAG,):
            own_piece(*PIECES[done])
        if piece == pairs:
            own_piece(*PIECES[piece - LAG])
    for piece in range(n_k - LAG, n_k):
        own_piece(*PIECES[piece])

    for d in range(1, n_t):
        remote(o_gain, g_z.at[d], gz_s.at[d], gz_r.at[d], me.right).wait()
    g_z[0] = o_gain[...]
    for d in range(1, n_t):
        g_z[0] += g_z[d]
    for d in range(1, nx):
        remote(g_z.at[0], g_x.at[d], gx_s.at[d], gx_r.at[d], me.at_x(d)).start()
    for d in range(1, nx):
        remote(g_z.at[0], g_x.at[d], gx_s.at[d], gx_r.at[d], me.at_x(d)).wait()
    o_gain[...] = g_z[0]
    for d in range(1, nx):
        o_gain[...] += g_x[d]

    @pl.when(jnp.logical_not(me.here))
    def _():
        for kind, n in PIECES:
            k, target = key(kind, n), final_part(kind, n)
            taken = remote(target, target, f_s.at[k], f_r.at[k], me.sibling)
            if kind == HEADS:
                pl.when(c == n // 2)(taken.wait_recv)
            else:
                taken.wait_recv()

    for kind, n in PIECES:
        k = key(kind, n)
        for j in range(mb):
            for _, copy in x_copies(kind, n, j):
                copy.wait_send()
            mine = grad_part(kind, n, j, x)
            pl.when(c * mb + j != z)(remote(mine, mine, z_s.at[k, j], z_r.at[k, j], me.right).wait_send)

    @pl.when(me.here)
    def _():
        for kind, n in PIECES:
            for case, copy, local in final_copies(kind, n):
                pl.when(case)(copy.wait if local else copy.wait_send)
        for d in range(1, n_t):
            there = r2.at[block(0), :]
            remote(there, o_dx.at[0], a2a_s.at[1, d], a2a_r.at[1, jz], me.right).wait_send()
        pltpu.make_async_copy(r2.at[block(z), :], o_dx.at[jz], loc.at[1]).wait()

    for t, dst in enumerate((o_y, o_dx)):
        for i in range(mb):
            @pl.when(c * mb + i != z)
            def _(t=t, i=i, dst=dst):
                remote(dst.at[i], dst.at[i], a2a_s.at[t, 0], a2a_r.at[t, i], me.right).wait_recv()

    for r in range(CHUNKS):
        swap(r2, r, e2).wait_send()
        mine = half_rows(r, c)
        pl.when(second_plane)(remote(mine, mine, hop.at[0, r], hop.at[1, r], me.sibling).wait_send)
        pl.when(first_plane)(remote(mine, mine, hsib.at[0, r], hsib.at[1, r], me.sibling).wait_send)
        pl.when(second_plane)(send_dv(r).wait_send)


def layer_kernel(
    tok, cot, lens, qkv, out, gu, down, gains, cos, sin,
    o_y, o_dx, o_qkv, o_out, o_gu, o_down, o_gain, tok_o, lx_ff, lx_out, lx_qkv, lz_ff, lz_out, lz_qkv,
    w_qkv, w_out, w_ff, x_v, first, q_v, ka_v, kb_v, vt_v, v_v, vu_v, o_v, lse_v, h_v, b_v, g_v, u_v, m_v,
    s1, r1, r2, dmo, len_v, dk_a, dv_a, st_ff, st_out, st_qkv, g_z, g_x,
    *sems,
):
    me = Place(tok.shape[0])
    me.meet()
    forward_part(
        me, tok, cot, lens, qkv, out, gu, down, gains, cos, sin, tok_o,
        w_qkv, w_out, w_ff, x_v, first, q_v, ka_v, kb_v, vt_v, v_v, vu_v, o_v, lse_v, h_v, b_v, g_v, u_v, m_v,
        s1, r1, r2, dmo, len_v, *sems[:20],
    )
    backward_part(
        me, gains, cos, sin, o_y, o_dx, o_qkv, o_out, o_gu, o_down, o_gain,
        lx_ff, lx_out, lx_qkv, lz_ff, lz_out, lz_qkv,
        w_qkv, w_out, w_ff, x_v, q_v, ka_v, kb_v, vt_v, vu_v, o_v, lse_v, h_v, b_v, g_v, u_v, m_v,
        dmo, v_v, first, s1, r1, r2, len_v, dk_a, dv_a, st_ff, st_out, st_qkv, g_z, g_x, *sems[20:],
    )


def layer(tokens, cotangent, lens, qkv, out, gu, down, gains, tables):
    mb, block_rows, dim = tokens.shape
    n_t, n_dp = lax.axis_size("tensor"), lax.axis_size("dp")
    nx = n_dp // 2
    seq = block_rows * n_t
    part, quarter = dim // nx, dim // n_dp
    cols, ow, ff = qkv.shape[3], out.shape[1], down.shape[1]
    pairs = mb * cols // PAIR
    assert pairs == COUNT[GU] == CHUNKS
    dma = pltpu.SemaphoreType.DMA
    wide, heads, turned = (seq, dim), (pairs, seq, PAIR), (pairs, PAIR, seq)
    hidden, block = (mb, seq, ff), (mb, block_rows, dim)
    n_k = len(PIECES)
    shape = lambda s, t=BF: jax.ShapeDtypeStruct(s, t)
    vmem = lambda s, t=BF: pltpu.VMEM(s, t)

    def parts(lead, split):
        return (*lead, 3, ff, split), (*lead, ow, split), (*lead, 3, split, cols)

    return pl.pallas_call(
        layer_kernel,
        out_shape=(
            shape(block), shape(block),
            shape((3, quarter, cols)), shape((ow, quarter)), shape((2, ff, quarter)), shape((ff, quarter)),
            shape((2, dim), F32), shape(wide),
            *(shape(s) for s in parts((nx - 1, mb), part)),
            *(shape(s) for s in parts((mb + 1,), part)),
        ),
        in_specs=[ANY, ANY, VMEM, ANY, ANY, ANY, ANY, VMEM, VMEM, VMEM],
        out_specs=(*(ANY,) * 6, VMEM, *(ANY,) * 7),
        scratch_shapes=[
            vmem((mb, 3, dim, cols)), vmem((mb * ow, dim)), vmem((mb, 3, ff, dim)),
            vmem(wide), *[vmem(heads)] * 4, vmem(turned), *[vmem(heads)] * 2,
            vmem((seq, pairs * PAIR)), vmem((pairs, 2, seq), F32), vmem(wide, F32), vmem(wide), *[vmem(hidden)] * 3,
            *[vmem(wide)] * 4, vmem((8, 128), F32), *[vmem(heads, F32)] * 2,
            vmem((nx, ff // 2, part)), vmem((nx, ow, part)), vmem((nx, 3, quarter // 2, cols)),
            vmem((n_t, 2, dim), F32), vmem((nx, 2, dim), F32),
            dma((5,)), dma((mb,)), dma((n_t,)), dma((mb,)), dma((n_t,)), dma((n_t,)), dma((n_t,)), dma((2,)),
            dma((N_PIECES,)), dma((N_PIECES,)), dma((N_PIECES, mb)), dma((N_PIECES, mb)),
            dma((N_PIECES, mb, nx)), dma((N_PIECES, mb, nx)),
            *[dma((2, CHUNKS))] * 5, dma((2,)),
            dma((2,)), dma((2, n_t)), dma((2, mb)), *[dma((2, CHUNKS))] * 5,
            dma((n_k, mb, nx)), dma((n_k, mb, nx)), dma((n_k, mb)), dma((n_k, mb)), *[dma((n_k,))] * 4,
            dma((nx,)), dma((n_t,)), dma((n_t,)), dma((nx,)), dma((nx,)), pltpu.SemaphoreType.REGULAR((2,)),
        ],
        compiler_params=pltpu.CompilerParams(
            collective_id=0, has_side_effects=True, vmem_limit_bytes=63 << 20
        ),
        name="layer",
    )(tokens, cotangent, lens, qkv, out, gu, down, gains, *tables)


def publish_kernel(*refs):
    count = len(refs) // 3
    sources, targets, held, sems = refs[:count], refs[count:2 * count], refs[2 * count:3 * count], refs[-1]
    copies = [pltpu.make_async_copy(src, dst, sems.at[n]) for n, (src, dst) in enumerate(zip(sources, held))]
    for copy in copies:
        copy.start()
    for copy, dst, src in zip(copies[:-1], targets, held):
        copy.wait()
        dst[...] = src[...].astype(dst.dtype)
    copies[-1].wait()
    dim, share = held[-1].shape[1], targets[-1].shape[1]
    place = lax.axis_index("dp") * lax.axis_size("tensor") + lax.axis_index("tensor")
    targets[-1][...] = pltpu.roll(held[-1][...], lax.rem(dim - place * share, dim), 1)[:, :share]


def publish(*arrays):
    types = (BF,) + (F32,) * (len(arrays) - 1)
    gain = arrays[-1]
    shapes = [a.shape for a in arrays[:-1]]
    shapes.append((2, gain.shape[1] // (lax.axis_size("dp") * lax.axis_size("tensor"))))
    return pl.pallas_call(
        publish_kernel,
        out_shape=tuple(jax.ShapeDtypeStruct(a, t) for a, t in zip(shapes, types)),
        in_specs=[ANY] * len(arrays),
        out_specs=(VMEM,) * len(arrays),
        scratch_shapes=[*(pltpu.VMEM(a.shape, a.dtype) for a in arrays), pltpu.SemaphoreType.DMA((len(arrays),))],
        compiler_params=pltpu.CompilerParams(vmem_limit_bytes=60 << 20),
        name="publish",
    )(*arrays)


def shards(tokens, lengths, qkv_weight, out_weight, gate_up_weight, down_weight, norm_gains, cotangent):
    mb, rows, _ = tokens.shape
    n_t = lax.axis_size("tensor")
    tables = tuple(jnp.asarray(t) for t in rope_tables(rows * n_t))
    lens = jnp.broadcast_to(lengths.astype(F32)[:, None, None], (mb, 8, 128))
    o_y, o_dx, o_qkv, o_out, o_gu, o_down, gain = layer(
        tokens, cotangent, lens, qkv_weight, out_weight, jnp.swapaxes(gate_up_weight, 2, 3), down_weight,
        norm_gains[0], tables,
    )[:7]
    o_y, o_dx, o_qkv, o_out, o_gu, o_down, gain = publish(o_y, o_dx, o_qkv, o_out, o_gu, o_down, gain)
    return (
        o_y[None], o_dx[None], o_qkv[None], o_out[None], jnp.swapaxes(o_gu, 1, 2)[None], o_down[None],
        gain[None],
    )


def solution(mesh):
    in_specs = (
        P("dp", "tensor", None),
        P("dp"),
        P("section", None, None, "tensor"),
        P("section", "tensor", None),
        P("section", None, None, "tensor"),
        P("section", "tensor", None),
        P("section", None, None),
        P("dp", "tensor", None),
    )
    out_specs = (
        P("section", "dp", "tensor", None),
        P("section", "dp", "tensor", None),
        P("section", None, "dp", "tensor"),
        P("section", "tensor", "dp"),
        P("section", None, "dp", "tensor"),
        P("section", "tensor", "dp"),
        P("section", None, ("dp", "tensor")),
    )
    return jax.shard_map(shards, mesh=mesh, in_specs=in_specs, out_specs=out_specs, check_vma=False)
```
